256 devices in a mesh: lat: 16 (over x_hi, z), lon: 8 (over y, x_lo), lev: 2 (over core).
Axes of the slice: x: 4 (x_hi: 2, x_lo: 2; x = x_hi * 2 + x_lo), y: 4, z: 8, core: 2. Of those that a mesh axis runs over, the one named last changes fastest.
Arguments:
- tracer: float32 [8, 1024, 2048], P('lev', 'lat', 'lon'), may hold values from -6 to 6
- diffusivity: float32 [8, 1024, 2048], P('lev', 'lat', 'lon'), may hold values from 0.02 to 0.1
- amplitude: float32 [8, 1024, 2048], P('lev', 'lat', 'lon'), may hold values from 0.05 to 0.5
- noise_w: float32 [2, 8, 1024, 2048], P(None, 'lev', 'lat', 'lon'), may hold values from -6 to 6
- noise_z: float32 [2, 8, 1024, 2048], P(None, 'lev', 'lat', 'lon'), may hold values from -6 to 6
- land_sea: int32 [8, 1024, 2048], P('lev', 'lat', 'lon'), may hold values 0 or 1
- partner: int32 [2048], replicated, may hold values from 0 to 2047, as said below
Outputs:
- tracer_out: float32 [8, 1024, 2048], P('lev', 'lat', 'lon')
The draws below stay inside these ranges and needn't reach their ends.
Inputs may be any that keep to these rules, and one draw needn't show every extreme that they name: partner[i] + i takes the same value modulo 2048 for every column i: the fold is a mirror of the columns.
All inputs are finite; a program needn't handle non-finite values. No bound on the sum of `land_sea` on one device may be relied on, other than what follows from the above.
Results may differ from the reference program's by a relative error of at most 0.00002.
Values sent between devices are 32-bit elements; how exact they have to be, the bound alone decides.
A program may use at most 64 MiB of HBM per device.

```python
import math
import jax
import jax.numpy as jnp

STEPS = 2
NZ = 8
NY = 1024
NX = 2048


def draw_partner(key, part):
    key = jax.random.fold_in(key, 7)
    offset = jax.random.randint(key, (), 0, NX, dtype=jnp.int32)
    return (offset - jnp.arange(NX, dtype=jnp.int32)) % NX


def place_ends(array, stream_key, least, high):
    longest = array.shape.index(max(array.shape))
    spots = []
    for shift in (0, 1):
        where = [jax.random.randint(jax.random.fold_in(stream_key, axis), (), 0, length) for axis, length in enumerate(array.shape)]
        where[longest] = (where[longest] + shift) % array.shape[longest]
        spots.append(tuple(where))
    return array.at[spots[0]].set(least).at[spots[1]].set(high)


def level_of(rng, shape, shards, low, top_value):
    level = 1.0
    for axis_at, shards_of in shards:
        heights = jax.random.uniform(jax.random.fold_in(jax.random.fold_in(rng, 6), axis_at), (shards_of,), jnp.float32, low / len(shards), top_value / len(shards))
        level = level * jnp.repeat(jnp.exp(heights), shape[axis_at] // shards_of).reshape((-1,) + (1,) * (len(shape) - 1 - axis_at))
    return level


def centred(own_key, extent, spread, reach, split=(), kind=jnp.bfloat16):
    result = jax.random.normal(own_key, extent, jnp.float32) * spread
    if len(split) > 0:
        result = level_of(own_key, extent, split, -0.22, 0.18) * result
    return jnp.clip(result, min=-reach, max=reach).astype(kind)


def setup_inputs(seed: int = 0) -> dict:
    arg_keys = jax.random.split(jax.random.key(seed), 8)
    tracer = centred(arg_keys[0], (NZ, NY, NX), 1.0, 6.0, ((0, 2), (1, 16), (2, 8)), jnp.float32)
    diffusivity = jnp.clip(jnp.exp(math.log(0.1) - 1.609438 * jax.random.uniform(arg_keys[1], (NZ, NY, NX), jnp.float32) ** level_of(arg_keys[1], (NZ, NY, NX), ((0, 2), (1, 16), (2, 8)), -0.2, 0.2)), 0.02, 0.1)
    amplitude = jnp.clip(jnp.exp(math.log(0.5) - 2.3025851 * jax.random.uniform(arg_keys[2], (NZ, NY, NX), jnp.float32) ** level_of(arg_keys[2], (NZ, NY, NX), ((0, 2), (1, 16), (2, 8)), -0.2, 0.2)), 0.05, 0.5)
    noise_w = centred(arg_keys[3], (STEPS, NZ, NY, NX), 1.0, 6.0, ((1, 2), (2, 16), (3, 8)), jnp.float32)
    noise_z = centred(arg_keys[4], (STEPS, NZ, NY, NX), 1.0, 6.0, ((1, 2), (2, 16), (3, 8)), jnp.float32)
    land_sea = place_ends((jax.random.randint(arg_keys[5], (NZ, NY, NX), 0, 10) < 7).astype(jnp.int32), jax.random.fold_in(arg_keys[5], 1), 0, 1)
    partner = draw_partner(jax.random.fold_in(arg_keys[7], 71), 0)
    return dict(tracer=tracer, diffusivity=diffusivity, amplitude=amplitude, noise_w=noise_w, noise_z=noise_z, land_sea=land_sea, partner=partner)


def extend(values, partner, margin):
    values = jnp.pad(values, ((margin, margin), (0, 0), (0, 0)))
    northern = values[:, values.shape[1] - margin:, :][:, ::-1, :]
    northern = jnp.take(northern, partner, axis=2)
    southern = jnp.zeros((values.shape[0], margin, values.shape[2]), jnp.float32)
    values = jnp.concatenate([southern, values, northern], axis=1)
    return jnp.concatenate([values[:, :, -margin:], values, values[:, :, :margin]], axis=2)


def tendency(values, diffusivity, ocean):
    inner = (slice(1, -1), slice(1, -1), slice(1, -1))
    centre = values[inner]
    centre_diff = diffusivity[inner]
    centre_ocean = ocean[inner]
    summed = jnp.zeros_like(centre)
    for axis_number in range(3):
        for offset in (-1, 1):
            picked = [slice(1, -1), slice(1, -1), slice(1, -1)]
            picked[axis_number] = slice(1 + offset, values.shape[axis_number] - 1 + offset)
            picked = tuple(picked)
            factor = 0.5 if axis_number == 0 else 1.0
            weight = factor * 0.5 * (centre_diff + diffusivity[picked]) * centre_ocean * ocean[picked]
            summed = summed + weight * (values[picked] - centre)
    return summed


def reference(tracer, diffusivity, amplitude, noise_w, noise_z, land_sea, partner):
    ocean = land_sea.astype(jnp.float32)
    diff_rim = extend(diffusivity, partner, 1)
    ocean_rim = extend(ocean, partner, 1)
    for step_index in range(STEPS):
        first = tendency(extend(tracer, partner, 1), diff_rim, ocean_rim)
        section = tracer + 0.75 * first + 1.5 * amplitude * noise_z[step_index]
        second = tendency(extend(section, partner, 1), diff_rim, ocean_rim)
        tracer = tracer + (first / 3.0 + 2.0 * second / 3.0) + amplitude * noise_w[step_index]
    return tracer
```

```python
import jax
import jax.numpy as jnp
from jax import lax
from jax.experimental import pallas as pl
from jax.experimental.pallas import tpu as pltpu
from jax.sharding import PartitionSpec as P


LAT, LON, LEV = 16, 8, 2
NL, ROWS, COLS = 4, 64, 256
RT = ROWS // 8
VMEM = 63 * 1024 * 1024
MESH = pl.DeviceIdType.MESH
f32 = jnp.float32


def kernel(
    tracer, diff, amp, noise_w, noise_z, land, partner, out,
    rx, rd, ra, rl, rw, rz, pc,
    xe, me, ge, he, ae, ke, x1, k2, wx, wy, wz, mp, mr,
    na, sa, nb, sb, em, wm, dne, dnw, dse, dsw, fa, fb,
    tn1, ts1, tn2, ts2, ep, wp, dn, ds,
    isem, ssem, rsem, fsem_s, fsem_r,
):
    lat, lon, lev = lax.axis_index("lat"), lax.axis_index("lon"), lax.axis_index("lev")
    east, west = lax.rem(lon + 1, LON), lax.rem(lon + LON - 1, LON)
    other = 1 - lev
    north_in, south_in = lat < LAT - 1, lat > 0
    at_fold = lat == LAT - 1

    bar = pltpu.get_barrier_semaphore()

    def greet(**where):
        pl.semaphore_signal(bar, inc=1, device_id=where, device_id_type=MESH)

    @pl.when(north_in)
    def _():
        greet(lat=lat + 1)
        greet(lat=lat + 1, lon=east)
        greet(lat=lat + 1, lon=west)

    @pl.when(south_in)
    def _():
        greet(lat=lat - 1)
        greet(lat=lat - 1, lon=east)
        greet(lat=lat - 1, lon=west)

    greet(lon=east)
    greet(lon=west)

    @pl.when(at_fold)
    def _():
        for k in range(2, LON - 1):
            greet(lon=lax.rem(lon + k, LON))

    greet(lev=other)

    loads = [
        pltpu.make_async_copy(s, d, isem.at[k])
        for k, (s, d) in enumerate(
            ((tracer, rx), (diff, rd), (land, rl), (amp, ra), (noise_z, rz), (noise_w, rw), (partner, pc))
        )
    ]
    for c in loads:
        c.start()

    lane = lax.broadcasted_iota(jnp.int32, (8, 128), 1)
    sub = lax.broadcasted_iota(jnp.int32, (8, 128), 0)
    lo_half, lo_sub = lane < 64, sub < 4
    east_part = (lane & 4) != 0

    def lroll(v, s):
        s = s % 128
        return v if s == 0 else pltpu.roll(v, s, 1)

    def sroll(v, s):
        return pltpu.roll(v, s, 0)

    def closed(v):
        return jnp.where(v > 0, v, -1.0)

    zero = jnp.zeros((8, 128), f32)
    own = NL * lev + 1

    def outside(r, _):
        sl = pl.ds(pl.multiple_of(8 * r, 8), 8)
        for p in (0, 9):
            for lt in range(3):
                me[p, lt, sl, :] = zero - 1.0
                for ref in (xe, ke, x1, k2):
                    ref[p, lt, sl, :] = zero
        return 0

    lax.fori_loop(0, RT + 1, outside, 0)

    @pl.when(lat == 0)
    def _():
        for i in range(NL):
            for lt in range(3):
                sa[NL * lev + i, lt] = zero
                sb[NL * lev + i, lt] = zero

    for c in loads:
        c.wait()

    def prep(n, _):
        i, r = n // RT, n % RT
        sl = pl.ds(pl.multiple_of(8 * r, 8), 8)
        p = own + i
        for lt in range(2):
            cs = pl.ds(128 * lt, 128)
            x = rx[i, sl, cs]
            amp_ = ra[i, sl, cs]
            m = 0.5 * rd[i, sl, cs] * rl[i, sl, cs].astype(f32)
            xe[p, lt, sl, :] = x
            mp[i, lt, sl, :] = m
            me[p, lt, sl, :] = closed(m)
            ge[p, lt, sl, :] = x + amp_ * rz[0, i, sl, cs]
            he[p, lt, sl, :] = x + amp_ * rw[0, i, sl, cs]
            ae[p, lt, sl, :] = amp_ * rz[1, i, sl, cs]
        return 0

    lax.fori_loop(0, NL * RT, prep, 0)

    def first_rows(x, m):
        return jnp.where(lo_sub, x, sroll(m, 4))

    def first_rows2(g, h, a):
        return jnp.where(lo_sub, g, jnp.where(sub == 7, sroll(a, 7), sroll(h, 4)))

    def last_rows(x, m):
        return jnp.where(lo_sub, sroll(m, 4), x)

    def last_rows2(g, h, a):
        return jnp.where(lo_sub, jnp.where(sub == 0, sroll(a, 1), sroll(h, 4)), g)

    top, bottom = pl.ds(ROWS - 8, 8), pl.ds(0, 8)

    def pack_rows(i, _):
        p = own + i
        for lt in range(2):
            tn1[i, lt] = first_rows(xe[p, lt, bottom, :], mp[i, lt, bottom, :])
            tn2[i, lt] = first_rows2(ge[p, lt, bottom, :], he[p, lt, bottom, :], ae[p, lt, bottom, :])
            ts1[i, lt] = last_rows(xe[p, lt, top, :], mp[i, lt, top, :])
            ts2[i, lt] = last_rows2(ge[p, lt, top, :], he[p, lt, top, :], ae[p, lt, top, :])
        return 0

    lax.fori_loop(0, NL, pack_rows, 0)

    for one, two, dst in ((tn1, tn2, dn), (ts1, ts2, ds)):
        d = zero
        for i in range(NL):
            z1 = jnp.where(lo_half, one[i, 0], one[i, 1])
            z2 = jnp.where(lo_half, two[i, 0], two[i, 1])
            d = jnp.where((lane >> 3) == 2 * i, lroll(z1, 16 * i + 4), d)
            d = jnp.where((lane >> 3) == 2 * i + 1, lroll(z2, 16 * i + 12), d)
        dst[...] = d

    def pack_columns(i, _):
        p = own + i
        p1, p2 = zero, zero
        for r in range(RT):
            sl = pl.ds(8 * r, 8)

            def edge(ref, q):
                return jnp.where(lo_half, ref[q, 0, sl, :], ref[q, 1, sl, :])

            a = edge(ae, p)
            ha = jnp.where(
                lane == 3, lroll(a, 3), jnp.where(lane == 124, lroll(a, 125), edge(he, p))
            )
            p1 = jnp.where((lane >> 3) == 2 * r, lroll(edge(xe, p), 16 * r + 4), p1)
            p1 = jnp.where((lane >> 3) == 2 * r + 1, lroll(edge(mp, i), 16 * r + 12), p1)
            at = (lane + 128 - 4 - 16 * r) & 127
            p2 = jnp.where(at < 8, lroll(edge(ge, p), 16 * r + 8), p2)
            p2 = jnp.where((at >= 8) & (at < 16), lroll(ha, 16 * r + 16), p2)
        ep[i] = jnp.where(east_part, p1, p2)
        wp[i] = jnp.where(east_part, p2, p1)
        return 0

    lax.fori_loop(0, NL, pack_columns, 0)

    def mirror_rows(v):
        for b in (1, 2, 4):
            v = jnp.where((sub & b) != 0, sroll(v, b), sroll(v, 8 - b))
        return v

    def mirror_lanes(v):
        for b in (1, 2, 4, 8, 16, 32, 64):
            v = jnp.where((lane & b) != 0, lroll(v, b), lroll(v, 128 - b))
        return v

    @pl.when(at_fold)
    def _():
        def pack_fold(i, _):
            p = own + i
            for lt in range(2):
                x, m, g, h, a = (
                    mirror_rows(v)
                    for v in (
                        xe[p, lt, top, :], mp[i, lt, top, :], ge[p, lt, top, :],
                        he[p, lt, top, :], ae[p, lt, top, :],
                    )
                )
                fa[2 * lon + lt, i] = mirror_lanes(first_rows(x, m))
                fb[2 * lon + lt, i] = mirror_lanes(first_rows2(g, h, a))
            return 0

        lax.fori_loop(0, NL, pack_fold, 0)

    @pl.when(lat == 0)
    def _():
        pl.semaphore_wait(bar, 6)

    @pl.when(at_fold)
    def _():
        pl.semaphore_wait(bar, 6 + LON - 3)

    @pl.when(north_in & south_in)
    def _():
        pl.semaphore_wait(bar, 9)

    def send(k, src, dst, **where):
        return pltpu.make_async_remote_copy(
            src_ref=src, dst_ref=dst, send_sem=ssem.at[k], recv_sem=rsem.at[k],
            device_id=where, device_id_type=MESH,
        )

    mine = pl.ds(NL * lev, NL)
    up, down = jnp.minimum(lat + 1, LAT - 1), jnp.maximum(lat - 1, 0)
    to_south = [
        send(0, tn1, na.at[mine, pl.ds(0, 2)], lat=down),
        send(1, dn, dne, lat=down, lon=west),
        send(2, dn, dnw, lat=down, lon=east),
        send(3, tn2, nb.at[mine, pl.ds(0, 2)], lat=down),
    ]
    to_north = [
        send(4, ts1, sa.at[mine, pl.ds(0, 2)], lat=up),
        send(5, ds, dse, lat=up, lon=west),
        send(6, ds, dsw, lat=up, lon=east),
        send(7, ts2, sb.at[mine, pl.ds(0, 2)], lat=up),
    ]
    to_side = [
        send(8, ep, em.at[mine], lon=west),
        send(9, wp, wm.at[mine], lon=east),
    ]
    block = pl.ds(2 * lon, 2)

    def fold_send(ref, half, k):
        return pltpu.make_async_remote_copy(
            src_ref=ref.at[block], dst_ref=ref.at[block],
            send_sem=fsem_s.at[half, k - 1], recv_sem=fsem_r.at[half, k - 1],
            device_id={"lon": lax.rem(lon + k, LON)}, device_id_type=MESH,
        )

    to_fold = [[fold_send(ref, half, k) for k in range(1, LON)] for half, ref in enumerate((fa, fb))]

    @pl.when(south_in)
    def _():
        for c in to_south[:3]:
            c.start()

    @pl.when(north_in)
    def _():
        for c in to_north[:3]:
            c.start()

    @pl.when(at_fold)
    def _():
        for c in to_fold[0]:
            c.start()

    for c in to_side:
        c.start()

    @pl.when(south_in)
    def _():
        to_south[3].start()

    @pl.when(north_in)
    def _():
        to_north[3].start()

    @pl.when(at_fold)
    def _():
        for c in to_fold[1]:
            c.start()

    inner = (pl.ds(0, 2), pl.ds(0, ROWS))

    def planes(ref, start, count):
        return ref.at[(pl.ds(start, count),) + inner]

    to_core = [
        send(10, planes(xe, own, NL), planes(xe, own, NL), lev=other),
        send(11, mp, mr, lev=other),
        send(12, planes(ge, 2 + 3 * lev, 3), planes(ge, 2 + 3 * lev, 3), lev=other),
        send(13, planes(he, 3 + 2 * lev, 2), planes(he, 3 + 2 * lev, 2), lev=other),
        send(14, planes(ae, 4 + lev, 1), planes(ae, 4 + lev, 1), lev=other),
    ]
    for c in to_core:
        c.start()

    def arrived(ref, start, count, k):
        part = planes(ref, start, count)
        pltpu.make_async_remote_copy(
            src_ref=part, dst_ref=part, send_sem=ssem.at[k], recv_sem=rsem.at[k],
            device_id={"lev": other}, device_id_type=MESH,
        ).wait_recv()

    theirs = NL * other + 1
    arrived(xe, theirs, NL, 10)
    to_core[1].wait_recv()
    arrived(ge, 2 + 3 * other, 3, 12)
    arrived(he, 3 + 2 * other, 2, 13)
    arrived(ae, 4 + other, 1, 14)

    def close(n, _):
        i, r = n // RT, n % RT
        sl = pl.ds(pl.multiple_of(8 * r, 8), 8)
        for lt in range(2):
            me[theirs + i, lt, sl, :] = closed(mr[i, lt, sl, :])
        return 0

    lax.fori_loop(0, NL * RT, close, 0)

    def relay(k, ref, start, count):
        part = ref.at[pl.ds(start, count)]
        return send(k, part, part, lev=other)

    relays = [
        relay(15, em, NL * lev, NL),
        relay(16, wm, NL * lev, NL),
        relay(17, na, NL * lev, NL),
        relay(18, sa, NL * lev, NL),
        relay(19, nb, 1 + 3 * lev, 3),
        relay(20, sb, 1 + 3 * lev, 3),
    ]
    to_side[0].wait_recv()
    relays[0].start()
    to_side[1].wait_recv()
    relays[1].start()

    def corners(e_ref, w_ref, one, two):
        d = jnp.where(east_part, e_ref[...], w_ref[...])
        for i in range(NL):
            one[NL * lev + i, 2] = lroll(d, 128 - (16 * i + 4))
            two[NL * lev + i, 2] = lroll(d, 128 - (16 * i + 12))

    @pl.when(south_in)
    def _():
        for c in to_north[:3]:
            c.wait_recv()
        corners(dse, dsw, sa, sb)

    relays[3].start()

    c0 = (pc[0] - COLS * lon) & (LON * COLS - 1)
    t0, shift = c0 >> 7, c0 & 127

    def unfold(src, dst):
        def level(i, _):
            t = [src[(t0 + k) & (2 * LON - 1), i] for k in (-3, -2, -1, 0, 1)]
            v = [
                pltpu.roll(jnp.where(lane >= 127 - shift, t[k + 1], t[k]), (shift + 1) & 127, 1)
                for k in range(4)
            ]
            dst[NL * lev + i, 0] = v[2]
            dst[NL * lev + i, 1] = v[1]
            dst[NL * lev + i, 2] = jnp.where(lo_half, v[0], v[3])
            return 0

        lax.fori_loop(0, NL, level, 0)

    def fold_arrived(ref, half):
        for k in range(1, LON):
            slot = pl.ds(2 * lax.rem(lon + LON - k, LON), 2)
            pltpu.make_async_remote_copy(
                src_ref=ref.at[slot], dst_ref=ref.at[slot],
                send_sem=fsem_s.at[half, k - 1], recv_sem=fsem_r.at[half, k - 1],
                device_id={"lon": lax.rem(lon + k, LON)}, device_id_type=MESH,
            ).wait_recv()

    @pl.when(north_in)
    def _():
        for c in to_south[:3]:
            c.wait_recv()
        corners(dne, dnw, na, nb)

    @pl.when(at_fold)
    def _():
        fold_arrived(fa, 0)
        unfold(fa, na)

    relays[2].start()

    @pl.when(south_in)
    def _():
        to_north[3].wait_recv()

    relays[5].start()

    @pl.when(north_in)
    def _():
        to_south[3].wait_recv()

    @pl.when(at_fold)
    def _():
        fold_arrived(fb, 1)
        unfold(fb, nb)

    relays[4].start()

    def relayed(k, ref, start, count):
        relay(k, ref, start, count).wait_recv()

    relayed(15, em, NL * other, NL)
    relayed(16, wm, NL * other, NL)
    relayed(17, na, NL * other, NL)
    relayed(18, sa, NL * other, NL)
    relayed(19, nb, 1 + 3 * other, 3)
    relayed(20, sb, 1 + 3 * other, 3)

    ring = pl.ds(ROWS, 8)

    def place_first(l, _):
        p = l + 1
        c1 = jnp.where(east_part, em[l], wm[l])
        for r in range(RT):
            sl = pl.ds(8 * r, 8)
            xe[p, 2, sl, :] = lroll(c1, 128 - (16 * r + 4))
            me[p, 2, sl, :] = closed(lroll(c1, 128 - (16 * r + 12)))
        for lt in range(3):
            n, s = na[l, lt], sa[l, lt]
            xe[p, lt, ring, :] = jnp.where(lo_sub, n, s)
            me[p, lt, ring, :] = closed(sroll(jnp.where(lo_sub, s, n), 4))
        return 0

    lax.fori_loop(0, 2 * NL, place_first, 0)

    def place_second(j, _):
        l = j + lev
        p = l + 1
        c2 = jnp.where(east_part, wm[l], em[l])
        for r in range(RT):
            sl = pl.ds(8 * r, 8)
            ge[p, 2, sl, :] = lroll(c2, 128 - (16 * r + 8))
            ha = lroll(c2, 128 - (16 * r + 16))
            he[p, 2, sl, :] = ha
            ae[p, 2, sl, :] = jnp.where(lo_half, lroll(ha, 125), lroll(ha, 3))
        for lt in range(3):
            n, s = nb[l, lt], sb[l, lt]
            ge[p, lt, ring, :] = jnp.where(lo_sub, n, s)
            ha = sroll(jnp.where(lo_sub, s, n), 4)
            he[p, lt, ring, :] = ha
            ae[p, lt, ring, :] = jnp.where(lo_sub, sroll(ha, 5), sroll(ha, 3))
        return 0

    lax.fori_loop(0, 2 * NL - 1, place_second, 0)

    def east_of(v):
        rolled = [lroll(t, 127) for t in v]
        return [jnp.where(lane == 127, rolled[(k + 1) % 3], rolled[k]) for k in range(3)]

    def west_of(v):
        rolled = [lroll(t, 1) for t in v]
        return [jnp.where(lane == 0, rolled[(k + 2) % 3], rolled[k]) for k in range(3)]

    def rows(ref, p, r):
        sl = pl.ds(8 * (r % (RT + 1)), 8)
        return [ref[p, lt, sl, :] for lt in range(3)]

    def weights(j, _):
        p = j + lev + 1
        nxt = [sroll(t, 7) for t in rows(me, p, 0)]
        first = nxt
        for r in range(RT + 1):
            sl = pl.ds(8 * r, 8)
            here, here_up = rows(me, p, r), nxt
            nxt = [sroll(t, 7) for t in rows(me, p, r + 1)] if r < RT else first
            e = east_of(here)
            below = rows(me, p - 1, r)
            for lt in range(3):
                n = jnp.where(sub == 7, nxt[lt], here_up[lt])
                wx[p, lt, sl, :] = jnp.maximum(here[lt] + e[lt], 0.0)
                wy[p, lt, sl, :] = jnp.maximum(here[lt] + n, 0.0)
                wz[p, lt, sl, :] = jnp.maximum(0.5 * (here[lt] + below[lt]), 0.0)
        return 0

    lax.fori_loop(0, 2 * NL, weights, 0)

    def operator(u, p, finish, last):
        def north_flux(r, up_here, up_next):
            here, w = rows(u, p, r), rows(wy, p, r)
            return [
                w[k] * (jnp.where(sub == 7, up_next[k], up_here[k]) - here[k]) for k in range(3)
            ]

        first = [sroll(t, 7) for t in rows(u, p, 0)]
        end = [sroll(t, 7) for t in rows(u, p, RT)]
        before = [sroll(t, 1) for t in north_flux(RT, end, first)]
        up_here = first
        for r in range(RT if last else RT + 1):
            if r + 1 < RT:
                up_next = [sroll(t, 7) for t in rows(u, p, r + 1)]
            else:
                up_next = end if r + 1 == RT else first
            here = rows(u, p, r)
            fy = north_flux(r, up_here, up_next)
            fy_up = [sroll(t, 1) for t in fy]
            e, w = east_of(here), rows(wx, p, r)
            fx = [w[k] * (e[k] - here[k]) for k in range(3)]
            fw = west_of(fx)
            above, below = rows(u, p + 1, r), rows(u, p - 1, r)
            wa, wb = rows(wz, p + 1, r), rows(wz, p, r)
            for k in range(2 if last else 3):
                fs = jnp.where(sub == 0, before[k], fy_up[k])
                total = (
                    (fx[k] - fw[k])
                    + (fy[k] - fs)
                    + (wa[k] * (above[k] - here[k]) - wb[k] * (here[k] - below[k]))
                )
                finish(r, k, total)
            before, up_here = fy_up, up_next

    def stage1(j, _):
        p = 1 + j + lev

        def finish(r, k, total):
            sl = pl.ds(8 * r, 8)
            ke[p, k, sl, :] = ge[p, k, sl, :] + 0.5 * total

        operator(xe, p, finish, False)
        return 0

    def stage2(j, _):
        p = 1 + j + 2 * lev

        def finish(r, k, total):
            sl = pl.ds(8 * r, 8)
            x1[p, k, sl, :] = he[p, k, sl, :] + total

        operator(ke, p, finish, False)
        return 0

    def stage3(j, _):
        p = 1 + j + 3 * lev

        def finish(r, k, total):
            sl = pl.ds(8 * r, 8)
            k2[p, k, sl, :] = (x1[p, k, sl, :] + ae[p, k, sl, :]) + 0.5 * total

        operator(x1, p, finish, False)
        return 0

    def stage4(j, _):
        p = 1 + j + 4 * lev

        def finish(r, k, total):
            sl, cs = pl.ds(8 * r, 8), pl.ds(128 * k, 128)
            out[j, sl, cs] = (x1[p, k, sl, :] + ra[j, sl, cs] * rw[1, j, sl, cs]) + total

        operator(k2, p, finish, True)
        return 0

    lax.fori_loop(0, 7, stage1, 0)
    lax.fori_loop(0, 6, stage2, 0)
    lax.fori_loop(0, 5, stage3, 0)
    lax.fori_loop(0, 4, stage4, 0)

    for c in to_side + to_core + relays:
        c.wait_send()

    @pl.when(south_in)
    def _():
        for c in to_south:
            c.wait_send()

    @pl.when(north_in)
    def _():
        for c in to_north:
            c.wait_send()

    @pl.when(at_fold)
    def _():
        for half in to_fold:
            for c in half:
                c.wait_send()


def local(tracer, diffusivity, amplitude, noise_w, noise_z, land_sea, partner):
    def vm(*shape, dtype=f32):
        return pltpu.VMEM(shape, dtype)

    cells = (NL, ROWS, COLS)
    plane = (3, ROWS + 8, 128)
    tile = (8, 128)
    rim = (2 * NL, 3) + tile
    sides = (2 * NL,) + tile
    rows = (NL, 2) + tile
    return pl.pallas_call(
        kernel,
        out_shape=jax.ShapeDtypeStruct(cells, f32),
        in_specs=[pl.BlockSpec(memory_space=pltpu.HBM)] * 7,
        out_specs=pl.BlockSpec(memory_space=pltpu.VMEM),
        scratch_shapes=[
            vm(*cells), vm(*cells), vm(*cells), vm(*cells, dtype=jnp.int32), vm(2, *cells), vm(2, *cells),
            pltpu.SMEM((LON * COLS,), jnp.int32),
        ]
        + [vm(10, *plane)] * 11
        + [vm(NL, 2, ROWS, 128)] * 2
        + [vm(*rim)] * 4
        + [vm(*sides)] * 2
        + [vm(*tile)] * 4
        + [vm(2 * LON, NL, *tile)] * 2
        + [vm(*rows)] * 4
        + [vm(NL, *tile)] * 2
        + [vm(*tile)] * 2
        + [
            pltpu.SemaphoreType.DMA((7,)),
            pltpu.SemaphoreType.DMA((21,)),
            pltpu.SemaphoreType.DMA((21,)),
            pltpu.SemaphoreType.DMA((2, LON - 1)),
            pltpu.SemaphoreType.DMA((2, LON - 1)),
        ],
        compiler_params=pltpu.CompilerParams(
            collective_id=0, has_side_effects=True, vmem_limit_bytes=VMEM
        ),
        name="ocean",
    )(tracer, diffusivity, amplitude, noise_w, noise_z, land_sea, partner)


def solution(mesh):
    block = P("lev", "lat", "lon")
    steps = P(None, "lev", "lat", "lon")
    return jax.shard_map(
        local,
        mesh=mesh,
        in_specs=(block, block, block, steps, steps, block, P()),
        out_specs=block,
        check_vma=False,
    )
```

```python
import jax
import jax.numpy as jnp
from jax import lax
from jax.experimental import pallas as pl
from jax.experimental.pallas import tpu as pltpu
from jax.sharding import PartitionSpec as P


LAT, LON, LEV = 16, 8, 2
NL, ROWS, COLS = 4, 64, 256
RT = ROWS // 8
VMEM = 60 * 1024 * 1024
MESH = pl.DeviceIdType.MESH
f32 = jnp.float32
X, M, G, H, A = range(5)


def kernel(
    tracer, diff, amp, noise_w, noise_z, land, partner, out,
    rx, rd, ra, rl, rw, rz, pc,
    xe, me, ge, he, ae, ke, x1, k2, wx, wy, wz, mp, mr, so,
    bx, bm, bg, bh, ba, vx, vy, vz, kr, x1r, k2r, x2r,
    na, sa, nb, sb, em, wm, dne, dnw, dse, dsw, fa, fb,
    tn1, ts1, tn2, ts2, ep, wp, dn, ds,
    isem, ssem, rsem, fsem_s, fsem_r,
):
    lat, lon, lev = lax.axis_index("lat"), lax.axis_index("lon"), lax.axis_index("lev")
    east, west = lax.rem(lon + 1, LON), lax.rem(lon + LON - 1, LON)
    other = 1 - lev
    north_in, south_in = lat < LAT - 1, lat > 0
    at_fold = lat == LAT - 1
    own, theirs = NL * lev + 1, NL * other + 1

    bar = pltpu.get_barrier_semaphore()

    def greet(**where):
        pl.semaphore_signal(bar, inc=1, device_id=where, device_id_type=MESH)

    @pl.when(north_in)
    def _():
        greet(lat=lat + 1)
        greet(lat=lat + 1, lon=east)
        greet(lat=lat + 1, lon=west)

    @pl.when(south_in)
    def _():
        greet(lat=lat - 1)
        greet(lat=lat - 1, lon=east)
        greet(lat=lat - 1, lon=west)

    greet(lon=east)
    greet(lon=west)

    @pl.when(at_fold)
    def _():
        for k in range(2, LON - 1):
            greet(lon=lax.rem(lon + k, LON))

    greet(lev=other)

    loads = [
        pltpu.make_async_copy(s, d, isem.at[k])
        for k, (s, d) in enumerate(
            ((tracer, rx), (diff, rd), (land, rl), (amp, ra), (noise_z, rz), (noise_w, rw), (partner, pc))
        )
    ]
    for c in loads:
        c.start()

    lane = lax.broadcasted_iota(jnp.int32, (8, 128), 1)
    sub = lax.broadcasted_iota(jnp.int32, (8, 128), 0)
    lo_half, lo_sub = lane < 64, sub < 4
    group_e = (lane * 171) >> 11
    group_w = (((lane + 8) * 171) >> 11) - 1
    k12 = lane - 12 * group_e
    halo_e, halo_w = k12 >= 8, (k12 >= 4) & (k12 < 8)
    ring_e = (group_e == 0) | (group_e == RT + 1)
    ring_w = (group_w == 0) | (group_w == RT + 1)
    zero = jnp.zeros((8, 128), f32)
    where = jnp.where

    def lroll(v, s):
        s = s % 128
        return v if s == 0 else pltpu.roll(v, s, 1)

    def sroll(v, s):
        return pltpu.roll(v, s, 0)

    def closed(v):
        return where(v > 0, v, -1.0)

    def both(v):
        return where(lo_half, v[0], v[1])

    top, bottom = pl.ds(ROWS - 8, 8), pl.ds(0, 8)

    def rows_at(r):
        return pl.ds(pl.multiple_of(8 * r, 8), 8)

    for c in loads[:3]:
        c.wait()

    def prep_first(i, _):
        p = own + i
        for r in range(RT):
            sl = pl.ds(8 * r, 8)
            for lt in range(2):
                cs = pl.ds(128 * lt, 128)
                m = 0.5 * rd[i, sl, cs] * rl[i, sl, cs].astype(f32)
                xe[p, lt, sl, :] = rx[i, sl, cs]
                mp[i, lt, sl, :] = m
                me[p, lt, sl, :] = closed(m)
        return 0

    lax.fori_loop(0, NL, prep_first, 0)

    def first_rows(x, m):
        return where(lo_sub, x, sroll(m, 4))

    def first_rows2(g, h, a):
        return where(lo_sub, g, where(sub == 7, sroll(a, 7), sroll(h, 4)))

    def last_rows(x, m):
        return where(lo_sub, sroll(m, 4), x)

    def last_rows2(g, h, a):
        return where(lo_sub, where(sub == 0, sroll(a, 1), sroll(h, 4)), g)

    def mirror_rows(v):
        for b in (1, 2, 4):
            v = where((sub & b) != 0, sroll(v, b), sroll(v, 8 - b))
        return v

    def mirror_lanes(v):
        return jnp.take_along_axis(v, 127 - lane, axis=1, mode="promise_in_bounds")

    for i in range(NL):
        for lt in range(2):
            tn1[i, lt] = first_rows(xe[own + i, lt, bottom, :], mp[i, lt, bottom, :])
            ts1[i, lt] = last_rows(xe[own + i, lt, top, :], mp[i, lt, top, :])

    @pl.when(at_fold)
    def _():
        for i in range(NL):
            for lt in range(2):
                x, m = mirror_rows(xe[own + i, lt, top, :]), mirror_rows(mp[i, lt, top, :])
                fa[2 * lon + lt, i] = mirror_lanes(first_rows(x, m))

    @pl.when(lat == 0)
    def _():
        pl.semaphore_wait(bar, 6)

    @pl.when(at_fold)
    def _():
        pl.semaphore_wait(bar, 6 + LON - 3)

    @pl.when(north_in & south_in)
    def _():
        pl.semaphore_wait(bar, 9)

    def send(k, src, dst, **where):
        return pltpu.make_async_remote_copy(
            src_ref=src, dst_ref=dst, send_sem=ssem.at[k], recv_sem=rsem.at[k],
            device_id=where, device_id_type=MESH,
        )

    mine = pl.ds(NL * lev, NL)
    two = pl.ds(0, 2)
    up, down = jnp.minimum(lat + 1, LAT - 1), jnp.maximum(lat - 1, 0)
    to_south = [
        send(0, tn1, na.at[mine, two], lat=down),
        send(1, tn2, nb.at[mine, two], lat=down),
        send(2, dn, dne, lat=down, lon=west),
        send(3, dn, dnw, lat=down, lon=east),
    ]
    to_north = [
        send(4, ts1, sa.at[mine, two], lat=up),
        send(5, ts2, sb.at[mine, two], lat=up),
        send(6, ds, dse, lat=up, lon=west),
        send(7, ds, dsw, lat=up, lon=east),
    ]
    to_side = [
        send(8, ep, em.at[mine], lon=west),
        send(9, wp, wm.at[mine], lon=east),
    ]
    block = pl.ds(2 * lon, 2)

    def fold_copy(ref, slot, half, k):
        return pltpu.make_async_remote_copy(
            src_ref=ref.at[slot], dst_ref=ref.at[slot],
            send_sem=fsem_s.at[half, k - 1], recv_sem=fsem_r.at[half, k - 1],
            device_id={"lon": lax.rem(lon + k, LON)}, device_id_type=MESH,
        )

    to_fold = [
        [fold_copy(ref, block, half, k) for k in range(1, LON)] for half, ref in enumerate((fa, fb))
    ]

    def planes(ref, start, count):
        return ref.at[pl.ds(start, count)]

    def share(k, ref, start, count):
        part = planes(ref, start, count)
        return send(k, part, part, lev=other)

    @pl.when(south_in)
    def _():
        to_south[0].start()

    @pl.when(north_in)
    def _():
        to_north[0].start()

    @pl.when(at_fold)
    def _():
        for c in to_fold[0]:
            c.start()

    to_core = [share(10, xe, own, NL), send(11, mp, mr, lev=other)]
    for c in to_core:
        c.start()

    for c in loads[3:]:
        c.wait()

    def prep_second(i, _):
        p = own + i
        for r in range(RT):
            sl = pl.ds(8 * r, 8)
            for lt in range(2):
                cs = pl.ds(128 * lt, 128)
                x = rx[i, sl, cs]
                amp_ = ra[i, sl, cs]
                ge[p, lt, sl, :] = x + amp_ * rz[0, i, sl, cs]
                he[p, lt, sl, :] = x + amp_ * rw[0, i, sl, cs]
                ae[p, lt, sl, :] = amp_ * rz[1, i, sl, cs]
        return 0

    lax.fori_loop(0, NL, prep_second, 0)

    for i in range(NL):
        p = own + i
        for lt in range(2):
            tn2[i, lt] = first_rows2(ge[p, lt, bottom, :], he[p, lt, bottom, :], ae[p, lt, bottom, :])
            ts2[i, lt] = last_rows2(ge[p, lt, top, :], he[p, lt, top, :], ae[p, lt, top, :])

    @pl.when(at_fold)
    def _():
        for i in range(NL):
            p = own + i
            for lt in range(2):
                g, h, a = (mirror_rows(ref[p, lt, top, :]) for ref in (ge, he, ae))
                fb[2 * lon + lt, i] = mirror_lanes(first_rows2(g, h, a))

    @pl.when(south_in)
    def _():
        to_south[1].start()

    @pl.when(north_in)
    def _():
        to_north[1].start()

    @pl.when(at_fold)
    def _():
        for c in to_fold[1]:
            c.start()

    for halves, dst in (((tn1, tn2), dn), ((ts1, ts2), ds)):
        d = zero
        for i in range(NL):
            for n, half in enumerate(halves):
                k = 2 * i + n
                d = where((lane >> 3) == k, lroll(both(half[i]), 8 * k + 4), d)
        dst[...] = d

    @pl.when(south_in)
    def _():
        to_south[2].start()
        to_south[3].start()

    @pl.when(north_in)
    def _():
        to_north[2].start()
        to_north[3].start()

    def pack_strips(i, _):
        p = own + i
        strips = []
        for f, ref, q in ((X, xe, p), (M, mp, i), (G, ge, p), (H, he, p), (A, ae, p)):
            s_e, s_w = zero, zero
            for r in range(RT):
                sl = pl.ds(8 * r, 8)
                v = lroll(where(lo_half, ref[q, 0, sl, :], ref[q, 1, sl, :]), 12 * (r + 1) + 8)
                s_e = where(group_e == r + 1, v, s_e)
                s_w = where(group_w == r + 1, v, s_w)
            so[p - 1, f, 0] = s_e
            so[p - 1, f, 1] = s_w
            strips.append(s_e)
        x, m, g, h, a = strips
        ep[i, 0] = where(halo_e, x, where(halo_w, lroll(m, 124), lroll(g, 120)))
        ep[i, 1] = where(halo_e, h, lroll(a, 124))
        wp[i, 0] = where(halo_w, x, where(halo_e, lroll(m, 4), lroll(g, 124)))
        wp[i, 1] = where(halo_w, h, lroll(a, 4))
        return 0

    lax.fori_loop(0, NL, pack_strips, 0)
    for c in to_side:
        c.start()

    late = [
        share(12, ge, 2 + 3 * lev, 3),
        share(13, he, 3 + 2 * lev, 2),
        share(14, ae, 4 + lev, 1),
        share(15, so, NL * lev, NL),
    ]
    for c in late:
        c.start()
    to_core += late

    for p in (0, 9):
        for lt in range(2):
            for r in range(RT):
                sl = pl.ds(8 * r, 8)
                me[p, lt, sl, :] = zero - 1.0
                for ref in (xe, ke, x1, k2):
                    ref[p, lt, sl, :] = zero
        for k in range(4):
            bx[p, k] = zero
            bm[p, k] = zero - 1.0
        for k in range(8):
            for ref in (kr, x1r, k2r):
                ref[p, k] = zero

    @pl.when(lat == 0)
    def _():
        for i in range(NL):
            for lt in range(3):
                sa[NL * lev + i, lt] = zero
                sb[NL * lev + i, lt] = zero

    share(10, xe, theirs, NL).wait_recv()
    to_core[1].wait_recv()

    def close(i, _):
        for r in range(RT):
            sl = pl.ds(8 * r, 8)
            for lt in range(2):
                me[theirs + i, lt, sl, :] = closed(mr[i, lt, sl, :])
        return 0

    lax.fori_loop(0, NL, close, 0)

    def pair(ref, p, r):
        sl = pl.ds(8 * r, 8)
        return [ref[p, lt, sl, :] for lt in range(2)]

    def east_of(v):
        r0, r1 = lroll(v[0], 127), lroll(v[1], 127)
        return [where(lane == 127, r1, r0), r1]

    def west_of(v):
        r0, r1 = lroll(v[0], 1), lroll(v[1], 1)
        return [r0, where(lane == 0, r0, r1)]

    def weights(j, _):
        p = j + lev + 1
        nxt = [sroll(t, 7) for t in pair(me, p, 0)]
        for r in range(RT):
            sl = pl.ds(8 * r, 8)
            here, here_up = pair(me, p, r), nxt
            if r + 1 < RT:
                nxt = [sroll(t, 7) for t in pair(me, p, r + 1)]
            e = east_of(here)
            below = pair(me, p - 1, r)
            for lt in range(2):
                n = where(sub == 7, nxt[lt], here_up[lt])
                wx[p, lt, sl, :] = jnp.maximum(here[lt] + e[lt], 0.0)
                wy[p, lt, sl, :] = jnp.maximum(here[lt] + n, 0.0)
                wz[p, lt, sl, :] = jnp.maximum(0.5 * (here[lt] + below[lt]), 0.0)
        return 0

    lax.fori_loop(0, 2 * NL, weights, 0)

    def inner(u, p, finish):
        up_here = [sroll(t, 7) for t in pair(u, p, 0)]
        before = [zero, zero]
        for r in range(RT):
            up_next = [sroll(t, 7) for t in pair(u, p, r + 1)] if r + 1 < RT else up_here
            here = pair(u, p, r)
            w = pair(wy, p, r)
            fy = [w[k] * (where(sub == 7, up_next[k], up_here[k]) - here[k]) for k in range(2)]
            fy_up = [sroll(t, 1) for t in fy]
            e, w = east_of(here), pair(wx, p, r)
            fx = [w[k] * (e[k] - here[k]) for k in range(2)]
            fw = west_of(fx)
            above, below = pair(u, p + 1, r), pair(u, p - 1, r)
            wa, wb = pair(wz, p + 1, r), pair(wz, p, r)
            for k in range(2):
                fs = where(sub == 0, before[k], fy_up[k])
                total = (
                    (fx[k] - fw[k])
                    + (fy[k] - fs)
                    + (wa[k] * (above[k] - here[k]) - wb[k] * (here[k] - below[k]))
                )
                finish(pl.ds(8 * r, 8), k, total)
            before, up_here = fy_up, up_next

    def inner1(j, _):
        p = 1 + j + lev

        def finish(sl, k, total):
            ke[p, k, sl, :] = ge[p, k, sl, :] + 0.5 * total

        inner(xe, p, finish)
        return 0

    def inner2(j, _):
        p = 1 + j + 2 * lev

        def finish(sl, k, total):
            x1[p, k, sl, :] = he[p, k, sl, :] + total

        inner(ke, p, finish)
        return 0

    def inner3(j, _):
        p = 1 + j + 3 * lev

        def finish(sl, k, total):
            k2[p, k, sl, :] = (x1[p, k, sl, :] + ae[p, k, sl, :]) + 0.5 * total

        inner(x1, p, finish)
        return 0

    def inner4(j, _):
        p = own + j

        def finish(sl, k, total):
            cs = pl.ds(128 * k, 128)
            out[j, sl, cs] = (x1[p, k, sl, :] + ra[j, sl, cs] * rw[1, j, sl, cs]) + total

        inner(k2, p, finish)
        return 0

    share(12, ge, 2 + 3 * other, 3).wait_recv()
    lax.fori_loop(0, 7, inner1, 0)
    share(13, he, 3 + 2 * other, 2).wait_recv()
    lax.fori_loop(0, 6, inner2, 0)
    share(14, ae, 4 + other, 1).wait_recv()
    lax.fori_loop(0, 5, inner3, 0)
    lax.fori_loop(0, 4, inner4, 0)
    share(15, so, NL * other, NL).wait_recv()

    relays = [
        share(16, em, NL * lev, NL),
        share(17, wm, NL * lev, NL),
        share(18, na, NL * lev, NL),
        share(19, sa, NL * lev, NL),
        share(20, nb, 1 + 3 * lev, 3),
        share(21, sb, 1 + 3 * lev, 3),
    ]
    to_side[0].wait_recv()
    relays[0].start()
    to_side[1].wait_recv()
    relays[1].start()

    def corners(w_ref, e_ref, at, one, half2):
        d = where((lane & 4) == 0, w_ref[...], e_ref[...])
        for i in range(NL):
            one[NL * lev + i, 2] = lroll(d, at - 16 * i)
            half2[NL * lev + i, 2] = lroll(d, at - 16 * i - 8)

    @pl.when(south_in)
    def _():
        for k in (0, 2, 3):
            to_north[k].wait_recv()
        corners(dsw, dse, 4, sa, sb)

    relays[3].start()

    c0 = (pc[0] - COLS * lon) & (LON * COLS - 1)
    t0, shift = c0 >> 7, c0 & 127

    def unfold(src, dst):
        for i in range(NL):
            t = [src[(t0 + k) & (2 * LON - 1), i] for k in (-3, -2, -1, 0, 1)]
            v = [
                pltpu.roll(where(lane >= 127 - shift, t[k + 1], t[k]), (shift + 1) & 127, 1)
                for k in range(4)
            ]
            dst[NL * lev + i, 0] = v[2]
            dst[NL * lev + i, 1] = v[1]
            dst[NL * lev + i, 2] = lroll(where(lo_half, v[0], v[3]), 116)

    def fold_arrived(ref, half):
        for k in range(1, LON):
            slot = pl.ds(2 * lax.rem(lon + LON - k, LON), 2)
            fold_copy(ref, slot, half, k).wait_recv()

    @pl.when(north_in)
    def _():
        for k in (0, 2, 3):
            to_south[k].wait_recv()
        corners(dnw, dne, 112, na, nb)

    @pl.when(at_fold)
    def _():
        fold_arrived(fa, 0)
        unfold(fa, na)

    relays[2].start()

    @pl.when(south_in)
    def _():
        to_north[1].wait_recv()

    relays[5].start()

    @pl.when(north_in)
    def _():
        to_south[1].wait_recv()

    @pl.when(at_fold)
    def _():
        fold_arrived(fb, 1)
        unfold(fb, nb)

    relays[4].start()

    def ends(n, s):
        r = where(lo_half, lroll(both(s), 8), lroll(both(n), 116))
        c = where(lo_half, s[2], n[2])
        return where(halo_e, c, r), where(halo_w, c, r)

    def strip(l, f, v_e, v_w, from_e, from_w):
        return (
            where(ring_e, v_e, where(halo_e, from_e, so[l, f, 0])),
            where(ring_w, v_w, where(halo_w, from_w, so[l, f, 1])),
        )

    def place_first(l):
        p = l + 1
        n, s = [na[l, k] for k in range(3)], [sa[l, k] for k in range(3)]
        e1, w1 = em[l, 0], wm[l, 0]
        for lt in range(2):
            bx[p, lt] = where(lo_sub, n[lt], s[lt])
            bm[p, lt] = closed(sroll(where(lo_sub, s[lt], n[lt]), 4))
        v = ends(n, s)
        bx[p, 2], bx[p, 3] = strip(l, X, v[0], v[1], e1, w1)
        m_e, m_w = strip(l, M, sroll(v[0], 4), sroll(v[1], 4), lroll(e1, 4), lroll(w1, 124))
        bm[p, 2], bm[p, 3] = closed(m_e), closed(m_w)

    def place_second(l):
        p = l + 1
        n, s = [nb[l, k] for k in range(3)], [sb[l, k] for k in range(3)]
        e1, w1, e2, w2 = em[l, 0], wm[l, 0], em[l, 1], wm[l, 1]
        for lt in range(2):
            bg[p, lt] = where(lo_sub, n[lt], s[lt])
            h = sroll(where(lo_sub, s[lt], n[lt]), 4)
            bh[p, lt] = h
            ba[p, lt] = where(lo_sub, sroll(h, 5), sroll(h, 3))
        v = ends(n, s)
        bg[p, 2], bg[p, 3] = strip(l, G, v[0], v[1], lroll(e1, 8), lroll(w1, 4))
        h = [sroll(t, 4) for t in v]
        bh[p, 2], bh[p, 3] = strip(l, H, h[0], h[1], e2, w2)
        a = [where(lo_half, sroll(t, 3), sroll(t, 5)) for t in h]
        ba[p, 2], ba[p, 3] = strip(l, A, a[0], a[1], lroll(e2, 4), lroll(w2, 124))

    for i in range(NL):
        place_first(NL * lev + i)
        place_second(NL * lev + i)

    for k, ref in ((16, em), (17, wm), (18, na), (19, sa)):
        share(k, ref, NL * other, NL).wait_recv()
    for i in range(NL):
        place_first(NL * other + i)
    share(20, nb, 1 + 3 * other, 3).wait_recv()
    share(21, sb, 1 + 3 * other, 3).wait_recv()
    for i in range(NL - 1):
        place_second(1 + 3 * other + i)

    def rim_of(full, part, p):
        return [
            full[p, 0, top, :], part[p, 0], full[p, 0, bottom, :],
            full[p, 1, top, :], part[p, 1], full[p, 1, bottom, :],
            part[p, 2], part[p, 3],
        ]

    def rim_east(v):
        r = [lroll(t, 127) for t in v]
        return [where(lane == 127, r[k + 3], r[k]) for k in range(3)] + r[3:]

    def rim_west(v):
        r = [lroll(t, 1) for t in v]
        return r[:3] + [where(lane == 0, r[k], r[k + 3]) for k in range(3)] + r[6:]

    def rim_north(v):
        r = [sroll(t, 7) for t in v]
        inside = [r[k] if k % 3 == 2 else where(sub == 7, r[k + 1], r[k]) for k in range(6)]
        return inside + [where(sub == 7, lroll(t, 116), t) for t in r[6:]]

    def rim_south(v):
        r = [sroll(t, 1) for t in v]
        inside = [r[k] if k % 3 == 0 else where(sub == 0, r[k - 1], r[k]) for k in range(6)]
        return inside + [where(sub == 0, lroll(t, 12), t) for t in r[6:]]

    fresh = (1, 4, 6, 7)
    below = rim_of(me, bm, lev)
    for j in range(2 * NL):
        p = 1 + j + lev
        m = rim_of(me, bm, p)
        e, n = rim_east(m), rim_north(m)
        for q, k in enumerate(fresh):
            vx[p, q] = jnp.maximum(m[k] + e[k], 0.0)
            vz[p, q] = jnp.maximum(0.5 * (m[k] + below[k]), 0.0)
            vy[p, q] = jnp.maximum(m[k] + n[k], 0.0)
        for q, k in enumerate((0, 3)):
            vy[p, 4 + q] = jnp.maximum(m[k] + n[k], 0.0)
        below = m

    def rim(u, base, count, finish, last=False):
        before, here = u(base - 1), u(base)

        def face(p, lo, hi):
            w = rim_of(wz, vz, p)
            return [w[k] * (hi[k] - lo[k]) for k in range(8)]

        fz = face(base, before, here)
        for j in range(count):
            p = base + j
            after = u(p + 1)
            fz_up = face(p + 1, here, after)
            w = rim_of(wx, vx, p)
            e = rim_east(here)
            fx = [w[k] * (e[k] - here[k]) for k in range(8)]
            fw = rim_west(fx)
            w = [
                vy[p, 4], vy[p, 0], wy[p, 0, bottom, :], vy[p, 5], vy[p, 1], wy[p, 1, bottom, :],
                vy[p, 2], vy[p, 3],
            ]
            n = rim_north(here)
            fy = [w[k] * (n[k] - here[k]) for k in range(8)]
            fs = rim_south(fy)
            finish(p, [(fx[k] - fw[k]) + (fy[k] - fs[k]) + (fz_up[k] - fz[k]) for k in range(8)])
            here, fz = after, fz_up

    def tiles(ref):
        return lambda p: [ref[p, k] for k in range(8)]

    def rim1(p, total):
        g = rim_of(ge, bg, p)
        for k in range(8):
            kr[p, k] = g[k] + 0.5 * total[k]

    def rim2(p, total):
        h = rim_of(he, bh, p)
        for k in range(8):
            x1r[p, k] = h[k] + total[k]

    def rim3(p, total):
        a = rim_of(ae, ba, p)
        for k in range(8):
            k2r[p, k] = (x1r[p, k] + a[k]) + 0.5 * total[k]

    def rim4(p, total):
        for k in range(8):
            x2r[p, k] = x1r[p, k] + total[k]

    rim(lambda p: rim_of(xe, bx, p), 1 + lev, 7, rim1)
    rim(tiles(kr), 1 + 2 * lev, 6, rim2)
    rim(tiles(x1r), 1 + 3 * lev, 5, rim3)
    rim(tiles(k2r), own, 4, rim4)

    def merge(i, _):
        p = own + i
        edge = where(halo_w, x2r[p, 6], x2r[p, 7])
        for r in range(RT):
            sl = pl.ds(8 * r, 8)
            cols = lroll(edge, 128 - (12 * (r + 1) + 8))
            for lt in range(2):
                cs = pl.ds(128 * lt, 128)
                noise = ra[i, sl, cs] * rw[1, i, sl, cs]
                at = (lane < 4) if lt == 0 else (lane >= 124)
                v = where(at, cols + noise, out[i, sl, cs])
                if r == 0:
                    v = where(lo_sub & ~at, x2r[p, 3 * lt + 2] + noise, v)
                if r == RT - 1:
                    v = where(~lo_sub & ~at, x2r[p, 3 * lt] + noise, v)
                out[i, sl, cs] = v
        return 0

    lax.fori_loop(0, NL, merge, 0)

    for c in to_side + to_core + relays:
        c.wait_send()

    @pl.when(south_in)
    def _():
        for c in to_south:
            c.wait_send()

    @pl.when(north_in)
    def _():
        for c in to_north:
            c.wait_send()

    @pl.when(at_fold)
    def _():
        for half in to_fold:
            for c in half:
                c.wait_send()


def local(*args):
    def vm(*shape, dtype=f32):
        return pltpu.VMEM(shape, dtype)

    cells = (NL, ROWS, COLS)
    tile = (8, 128)
    planes = (10, 2, ROWS, 128)
    rim = (2 * NL, 3) + tile
    sides = (2 * NL, 2) + tile
    rows = (NL, 2) + tile
    return pl.pallas_call(
        kernel,
        out_shape=pltpu.VMEM(cells, f32),
        in_specs=[pl.BlockSpec(memory_space=pltpu.HBM)] * 7,
        out_specs=pl.BlockSpec(memory_space=pltpu.VMEM),
        scratch_shapes=[
            vm(*cells), vm(*cells), vm(*cells), vm(*cells, dtype=jnp.int32), vm(2, *cells), vm(2, *cells),
            pltpu.SMEM((LON * COLS,), jnp.int32),
        ]
        + [vm(*planes)] * 11
        + [vm(NL, 2, ROWS, 128)] * 2
        + [vm(2 * NL, 5, 2, *tile)]
        + [vm(10, 4, *tile)] * 5
        + [vm(10, 4, *tile), vm(10, 6, *tile), vm(10, 4, *tile)]
        + [vm(10, 8, *tile)] * 4
        + [vm(*rim)] * 4
        + [vm(*sides)] * 2
        + [vm(*tile)] * 4
        + [vm(2 * LON, NL, *tile)] * 2
        + [vm(*rows)] * 4
        + [vm(*rows)] * 2
        + [vm(*tile)] * 2
        + [
            pltpu.SemaphoreType.DMA((7,)),
            pltpu.SemaphoreType.DMA((22,)),
            pltpu.SemaphoreType.DMA((22,)),
            pltpu.SemaphoreType.DMA((2, LON - 1)),
            pltpu.SemaphoreType.DMA((2, LON - 1)),
        ],
        compiler_params=pltpu.CompilerParams(
            collective_id=0, has_side_effects=True, vmem_limit_bytes=VMEM
        ),
        name="ocean",
    )(*(pltpu.with_memory_space_constraint(v, pltpu.HBM) for v in args))


def solution(mesh):
    block = P("lev", "lat", "lon")
    steps = P(None, "lev", "lat", "lon")
    return jax.shard_map(
        local,
        mesh=mesh,
        in_specs=(block, block, block, steps, steps, block, P()),
        out_specs=block,
        check_vma=False,
    )
```

```python
import jax
import jax.numpy as jnp
from jax import lax
from jax.experimental import pallas as pl
from jax.experimental.pallas import tpu as pltpu
from jax.sharding import PartitionSpec as P


LAT, LON, LEV = 16, 8, 2
NL, ROWS, COLS = 4, 64, 256
RT = ROWS // 8
VMEM = 60 * 1024 * 1024
MESH = pl.DeviceIdType.MESH
f32 = jnp.float32
X, M, G, H, A = range(5)


def kernel(
    tracer, diff, amp, noise_w, noise_z, land, partner, out,
    rx, rd, ra, rl, rw, rz, pc,
    xe, me, ge, he, ae, ke, x1, k2, we, ww, wy, wz, mp, mr, so,
    bx, bm, ve, vw, vn, vs, vz, kr, x1r, k2r, x2r, bg, bh, ba,
    na, sa, nb, sb, em, wm, dne, dnw, dse, dsw, fa, fb,
    tn1, ts1, tn2, ts2, ep, wp, dn, ds,
    isem, ssem, rsem, fsem_s, fsem_r,
):
    lat, lon, lev = lax.axis_index("lat"), lax.axis_index("lon"), lax.axis_index("lev")
    east, west = lax.rem(lon + 1, LON), lax.rem(lon + LON - 1, LON)
    other = 1 - lev
    north_in, south_in = lat < LAT - 1, lat > 0
    at_fold = lat == LAT - 1
    own, theirs = NL * lev + 1, NL * other + 1

    bar = pltpu.get_barrier_semaphore()

    def greet(**where):
        pl.semaphore_signal(bar, inc=1, device_id=where, device_id_type=MESH)

    @pl.when(north_in)
    def _():
        greet(lat=lat + 1)
        greet(lat=lat + 1, lon=east)
        greet(lat=lat + 1, lon=west)

    @pl.when(south_in)
    def _():
        greet(lat=lat - 1)
        greet(lat=lat - 1, lon=east)
        greet(lat=lat - 1, lon=west)

    greet(lon=east)
    greet(lon=west)

    @pl.when(at_fold)
    def _():
        for k in (2, 4, 6):
            greet(lon=lax.rem(lon + k, LON))

    greet(lev=other)

    loads = [
        pltpu.make_async_copy(s, d, isem.at[k])
        for k, (s, d) in enumerate(
            ((tracer, rx), (diff, rd), (land, rl), (amp, ra), (noise_z, rz), (noise_w, rw), (partner, pc))
        )
    ]
    for c in loads:
        c.start()

    lane = lax.broadcasted_iota(jnp.int32, (8, 128), 1)
    sub = lax.broadcasted_iota(jnp.int32, (8, 128), 0)
    lo_half, lo_sub = lane < 64, sub < 4
    group_e = (lane * 171) >> 11
    group_w = (((lane + 8) * 171) >> 11) - 1
    k12 = lane - 12 * group_e
    halo_e, halo_w = k12 >= 8, (k12 >= 4) & (k12 < 8)
    ring_e = (group_e == 0) | (group_e == RT + 1)
    ring_w = (group_w == 0) | (group_w == RT + 1)
    zero = jnp.zeros((8, 128), f32)
    where = jnp.where

    def lroll(v, s):
        s = s % 128
        return v if s == 0 else pltpu.roll(v, s, 1)

    def sroll(v, s):
        return pltpu.roll(v, s, 0)

    def closed(v):
        return where(v > 0, v, -1.0)

    def both(v):
        return where(lo_half, v[0], v[1])

    top, bottom = pl.ds(ROWS - 8, 8), pl.ds(0, 8)

    def rows_at(r):
        return pl.ds(pl.multiple_of(8 * r, 8), 8)

    for p in (0, 9):
        for r in range(RT):
            sl = pl.ds(8 * r, 8)
            for lt in range(2):
                me[p, lt, sl, :] = zero - 1.0
                for ref in (xe, ke, x1, k2):
                    ref[p, lt, sl, :] = zero
            bm[p, sl, :] = zero - 1.0
            for ref in (bx, kr, x1r, k2r):
                ref[p, sl, :] = zero

    @pl.when(lat == 0)
    def _():
        for i in range(NL):
            for lt in range(3):
                sa[NL * lev + i, lt] = zero
                sb[NL * lev + i, lt] = zero

    for c in loads[:3]:
        c.wait()

    def prep_first(i, _):
        p = own + i
        for r in range(RT):
            sl = pl.ds(8 * r, 8)
            for lt in range(2):
                cs = pl.ds(128 * lt, 128)
                m = 0.5 * rd[i, sl, cs] * rl[i, sl, cs].astype(f32)
                xe[p, lt, sl, :] = rx[i, sl, cs]
                mp[i, lt, sl, :] = m
                me[p, lt, sl, :] = closed(m)
        return 0

    lax.fori_loop(0, NL, prep_first, 0)

    def first_rows(x, m):
        return where(lo_sub, x, sroll(m, 4))

    def first_rows2(g, h, a):
        return where(lo_sub, g, where(sub == 7, sroll(a, 7), sroll(h, 4)))

    def last_rows(x, m):
        return where(lo_sub, sroll(m, 4), x)

    def last_rows2(g, h, a):
        return where(lo_sub, where(sub == 0, sroll(a, 1), sroll(h, 4)), g)

    def mirror_rows(v):
        for b in (1, 2, 4):
            v = where((sub & b) != 0, sroll(v, b), sroll(v, 8 - b))
        return v

    def mirror_lanes(v):
        return jnp.take_along_axis(v, 127 - lane, axis=1, mode="promise_in_bounds")

    for i in range(NL):
        for lt in range(2):
            tn1[i, lt] = first_rows(xe[own + i, lt, bottom, :], mp[i, lt, bottom, :])
            ts1[i, lt] = last_rows(xe[own + i, lt, top, :], mp[i, lt, top, :])

    @pl.when(at_fold)
    def _():
        for i in range(NL):
            for lt in range(2):
                x, m = mirror_rows(xe[own + i, lt, top, :]), mirror_rows(mp[i, lt, top, :])
                fa[2 * lon + lt, i] = mirror_lanes(first_rows(x, m))

    @pl.when(lat == 0)
    def _():
        pl.semaphore_wait(bar, 6)

    @pl.when(south_in)
    def _():
        pl.semaphore_wait(bar, 9)

    def send(k, src, dst, **where):
        return pltpu.make_async_remote_copy(
            src_ref=src, dst_ref=dst, send_sem=ssem.at[k], recv_sem=rsem.at[k],
            device_id=where, device_id_type=MESH,
        )

    mine = pl.ds(NL * lev, NL)
    two = pl.ds(0, 2)
    up, down = jnp.minimum(lat + 1, LAT - 1), jnp.maximum(lat - 1, 0)
    to_south = [
        send(0, tn1, na.at[mine, two], lat=down),
        send(1, tn2, nb.at[mine, two], lat=down),
        send(2, dn, dne, lat=down, lon=west),
        send(3, dn, dnw, lat=down, lon=east),
    ]
    to_north = [
        send(4, ts1, sa.at[mine, two], lat=up),
        send(5, ts2, sb.at[mine, two], lat=up),
        send(6, ds, dse, lat=up, lon=west),
        send(7, ds, dsw, lat=up, lon=east),
    ]
    to_side = [
        send(8, ep, em.at[mine], lon=west),
        send(9, wp, wm.at[mine], lon=east),
    ]

    def beside(i):
        return i + 1 - 2 * lax.rem(i, 2)

    def fold_copy(ref, half, n, owner, target):
        slot = ref.at[pl.ds(2 * owner, 2)]
        return pltpu.make_async_remote_copy(
            src_ref=slot, dst_ref=slot, send_sem=fsem_s.at[half, n], recv_sem=fsem_r.at[half, n],
            device_id={"lon": target}, device_id_type=MESH,
        )

    def fold_out(ref, half, n):
        k = n if n < 4 else n - 3
        target = beside(lon) if n == 0 else lax.rem(lon + 2 * k, LON)
        return fold_copy(ref, half, n, lon if n < 4 else beside(lon), target)

    def fold_in(ref, half, n):
        k = n if n < 4 else n - 3
        sender = beside(lon) if n == 0 else lax.rem(lon + LON - 2 * k, LON)
        fold_copy(ref, half, n, sender if n < 4 else beside(sender), sender).wait_recv()

    to_fold = [[fold_out(ref, half, n) for n in range(7)] for half, ref in enumerate((fa, fb))]

    def planes(ref, start, count):
        return ref.at[pl.ds(start, count)]

    def share(k, ref, start, count):
        part = planes(ref, start, count)
        return send(k, part, part, lev=other)

    @pl.when(south_in)
    def _():
        to_south[0].start()

    @pl.when(north_in)
    def _():
        to_north[0].start()

    @pl.when(at_fold)
    def _():
        for c in to_fold[0][:4]:
            c.start()

    to_core = [share(10, xe, own, NL), send(11, mp, mr, lev=other)]
    for c in to_core:
        c.start()

    for c in loads[3:]:
        c.wait()

    def prep_second(i, _):
        p = own + i
        for r in range(RT):
            sl = pl.ds(8 * r, 8)
            for lt in range(2):
                cs = pl.ds(128 * lt, 128)
                x = rx[i, sl, cs]
                amp_ = ra[i, sl, cs]
                ge[p, lt, sl, :] = x + amp_ * rz[0, i, sl, cs]
                he[p, lt, sl, :] = x + amp_ * rw[0, i, sl, cs]
                ae[p, lt, sl, :] = amp_ * rz[1, i, sl, cs]
        return 0

    lax.fori_loop(0, NL, prep_second, 0)
    late = [share(12, ge, 2 + 3 * lev, 3), share(13, he, 3 + 2 * lev, 2), share(14, ae, 4 + lev, 1)]
    for c in late:
        c.start()
    to_core += late

    for i in range(NL):
        p = own + i
        for lt in range(2):
            tn2[i, lt] = first_rows2(ge[p, lt, bottom, :], he[p, lt, bottom, :], ae[p, lt, bottom, :])
            ts2[i, lt] = last_rows2(ge[p, lt, top, :], he[p, lt, top, :], ae[p, lt, top, :])

    @pl.when(at_fold)
    def _():
        for i in range(NL):
            p = own + i
            for lt in range(2):
                g, h, a = (mirror_rows(ref[p, lt, top, :]) for ref in (ge, he, ae))
                fb[2 * lon + lt, i] = mirror_lanes(first_rows2(g, h, a))

    @pl.when(south_in)
    def _():
        to_south[1].start()

    @pl.when(north_in)
    def _():
        to_north[1].start()

    @pl.when(at_fold)
    def _():
        for c in to_fold[1][:4]:
            c.start()

    for halves, dst in (((tn1, tn2), dn), ((ts1, ts2), ds)):
        d = zero
        for i in range(NL):
            for n, half in enumerate(halves):
                k = 2 * i + n
                d = where((lane >> 3) == k, lroll(both(half[i]), 8 * k + 4), d)
        dst[...] = d

    @pl.when(south_in)
    def _():
        to_south[2].start()
        to_south[3].start()

    @pl.when(north_in)
    def _():
        to_north[2].start()
        to_north[3].start()

    def pack_strips(i, _):
        p = own + i
        strips = []
        for f, ref, q in ((X, xe, p), (M, mp, i), (G, ge, p), (H, he, p), (A, ae, p)):
            s_e, s_w = zero, zero
            for r in range(RT):
                sl = pl.ds(8 * r, 8)
                v = lroll(where(lo_half, ref[q, 0, sl, :], ref[q, 1, sl, :]), 12 * (r + 1) + 8)
                s_e = where(group_e == r + 1, v, s_e)
                s_w = where(group_w == r + 1, v, s_w)
            so[p - 1, f, 0] = s_e
            so[p - 1, f, 1] = s_w
            strips.append(s_e)
        x, m, g, h, a = strips
        ep[i, 0] = where(halo_e, x, where(halo_w, lroll(m, 124), lroll(g, 120)))
        ep[i, 1] = where(halo_e, h, lroll(a, 124))
        wp[i, 0] = where(halo_w, x, where(halo_e, lroll(m, 4), lroll(g, 124)))
        wp[i, 1] = where(halo_w, h, lroll(a, 4))
        return 0

    lax.fori_loop(0, NL, pack_strips, 0)
    for c in to_side:
        c.start()

    to_core.append(share(15, so, NL * lev, NL))
    to_core[-1].start()

    def pair(ref, p, r):
        sl = pl.ds(8 * r, 8)
        return [ref[p, lt, sl, :] for lt in range(2)]

    def shifted(ref, p, r, d):
        if 0 <= 8 * r + d <= ROWS - 8:
            return [ref[p, lt, pl.ds(8 * r + d, 8), :] for lt in range(2)]
        return [sroll(t, -d % 8) for t in pair(ref, p, r)]

    def east_of(v):
        r0, r1 = lroll(v[0], 127), lroll(v[1], 127)
        return [where(lane == 127, r1, r0), r1]

    def west_of(v):
        r0, r1 = lroll(v[0], 1), lroll(v[1], 1)
        return [r0, where(lane == 0, r0, r1)]

    def relu(v):
        return jnp.maximum(v, 0.0)

    def weights(p, face):
        for r in range(RT):
            sl = pl.ds(8 * r, 8)
            here, n = pair(me, p, r), shifted(me, p, r, 1)
            e = east_of(here)
            w = [relu(here[k] + e[k]) for k in range(2)]
            v = west_of(w)
            hi, lo = pair(me, face, r), pair(me, face - 1, r)
            for k in range(2):
                we[p, k, sl, :] = w[k]
                ww[p, k, sl, :] = v[k]
                wy[p, k, sl, :] = relu(here[k] + n[k])
                wz[face, k, sl, :] = relu(0.5 * (hi[k] + lo[k]))

    def inner(u, p, count, finish):
        for r in range(RT):
            stack = [pair(u, p + j, r) for j in range(-1, count + 1)]
            fz = [
                [w * (hi - lo) for w, lo, hi in zip(pair(wz, p + j, r), stack[j], stack[j + 1])]
                for j in range(count + 1)
            ]
            for j in range(count):
                here, q = stack[j + 1], p + j
                n, s = shifted(u, q, r, 1), shifted(u, q, r, -1)
                wn, ws = pair(wy, q, r), shifted(wy, q, r, -1)
                e, w, v, wv = east_of(here), pair(we, q, r), west_of(here), pair(ww, q, r)
                for k in range(2):
                    total = (
                        (w[k] * (e[k] - here[k]) - wv[k] * (here[k] - v[k]))
                        + (wn[k] * (n[k] - here[k]) - ws[k] * (here[k] - s[k]))
                        + (fz[j + 1][k] - fz[j][k])
                    )
                    finish(q, pl.ds(8 * r, 8), k, total)

    def finish1(p, sl, k, total):
        ke[p, k, sl, :] = ge[p, k, sl, :] + 0.5 * total

    def finish2(p, sl, k, total):
        x1[p, k, sl, :] = he[p, k, sl, :] + total

    def finish3(p, sl, k, total):
        k2[p, k, sl, :] = (x1[p, k, sl, :] + ae[p, k, sl, :]) + 0.5 * total

    def finish4(p, sl, k, total):
        j, cs = p - own, pl.ds(128 * k, 128)
        out[j, sl, cs] = (x1[p, k, sl, :] + ra[j, sl, cs] * rw[1, j, sl, cs]) + total

    far, near = 1 + 5 * lev, 4 - 2 * lev
    next_own, next_faces = 2 + 3 * other, 5 - 3 * lev

    def own_weights(j, _):
        weights(own + j, far + j)
        return 0

    def other_weights(j, _):
        weights(theirs + j, next_faces + j)
        return 0

    lax.fori_loop(0, NL, own_weights, 0)
    inner(xe, far, 3, finish1)

    def copy_own(i, _):
        p = own + i
        for ref, to in ((xe, bx), (me, bm)):
            for lt in range(2):
                to[p, pl.ds(24 * lt, 8), :] = ref[p, lt, top, :]
                to[p, pl.ds(24 * lt + 16, 8), :] = ref[p, lt, bottom, :]
        return 0

    lax.fori_loop(0, NL, copy_own, 0)

    @pl.when(at_fold)
    def _():
        for half, ref in enumerate((fa, fb)):
            fold_in(ref, half, 0)
            for c in to_fold[half][4:]:
                c.start()

    share(10, xe, theirs, NL).wait_recv()
    to_core[1].wait_recv()

    def close(i, _):
        p = theirs + i
        for r in range(RT):
            sl = pl.ds(8 * r, 8)
            for lt in range(2):
                me[p, lt, sl, :] = closed(mr[i, lt, sl, :])
        for ref, to in ((xe, bx), (me, bm)):
            for lt in range(2):
                to[p, pl.ds(24 * lt, 8), :] = ref[p, lt, top, :]
                to[p, pl.ds(24 * lt + 16, 8), :] = ref[p, lt, bottom, :]
        return 0

    lax.fori_loop(0, NL, close, 0)
    lax.fori_loop(0, NL, other_weights, 0)
    share(12, ge, next_own, 3).wait_recv()
    inner(xe, near, 4, finish1)
    share(13, he, 3 + 2 * other, 2).wait_recv()

    def inner2(j, _):
        inner(ke, 1 + 2 * lev + 3 * j, 3, finish2)
        return 0

    lax.fori_loop(0, 2, inner2, 0)
    share(14, ae, 4 + other, 1).wait_recv()
    inner(x1, 1 + 3 * lev, 5, finish3)
    inner(k2, own, 4, finish4)
    share(15, so, NL * other, NL).wait_recv()

    relays = [
        share(16, em, NL * lev, NL),
        share(17, wm, NL * lev, NL),
        share(18, na, NL * lev, NL),
        share(19, sa, NL * lev, NL),
        share(20, nb, 1 + 3 * lev, 3),
        share(21, sb, 1 + 3 * lev, 3),
    ]
    to_side[0].wait_recv()
    relays[0].start()
    to_side[1].wait_recv()
    relays[1].start()

    def corners(w_ref, e_ref, at, one, half2):
        d = where((lane & 4) == 0, w_ref[...], e_ref[...])
        for i in range(NL):
            one[NL * lev + i, 2] = lroll(d, at - 16 * i)
            half2[NL * lev + i, 2] = lroll(d, at - 16 * i - 8)

    @pl.when(south_in)
    def _():
        for k in (0, 2, 3):
            to_north[k].wait_recv()
        corners(dsw, dse, 4, sa, sb)

    relays[3].start()

    c0 = (pc[0] - COLS * lon) & (LON * COLS - 1)
    t0, shift = c0 >> 7, c0 & 127

    def unfold(src, dst):
        for i in range(NL):
            t = [src[(t0 + k) & (2 * LON - 1), i] for k in (-3, -2, -1, 0, 1)]
            v = [
                pltpu.roll(where(lane >= 127 - shift, t[k + 1], t[k]), (shift + 1) & 127, 1)
                for k in range(4)
            ]
            dst[NL * lev + i, 0] = v[2]
            dst[NL * lev + i, 1] = v[1]
            dst[NL * lev + i, 2] = lroll(where(lo_half, v[0], v[3]), 116)

    def fold_arrived(ref, half):
        for n in range(1, 7):
            fold_in(ref, half, n)

    @pl.when(north_in)
    def _():
        for k in (0, 2, 3):
            to_south[k].wait_recv()
        corners(dnw, dne, 112, na, nb)

    @pl.when(at_fold)
    def _():
        fold_arrived(fa, 0)
        unfold(fa, na)

    relays[2].start()

    @pl.when(south_in)
    def _():
        to_north[1].wait_recv()

    relays[5].start()

    @pl.when(north_in)
    def _():
        to_south[1].wait_recv()
        relays[4].start()

    def ends(n, s):
        r = where(lo_half, lroll(both(s), 8), lroll(both(n), 116))
        c = where(lo_half, s[2], n[2])
        return where(halo_e, c, r), where(halo_w, c, r)

    def strip(l, f, v_e, v_w, from_e, from_w):
        return (
            where(ring_e, v_e, where(halo_e, from_e, so[l, f, 0])),
            where(ring_w, v_w, where(halo_w, from_w, so[l, f, 1])),
        )

    def put(ref, p, tiles, which):
        for k, t in zip(which, tiles):
            ref[p, pl.ds(8 * k, 8), :] = t

    fresh = (1, 4, 6, 7)

    def place_first(l):
        p = l + 1
        n, s = [na[l, k] for k in range(3)], [sa[l, k] for k in range(3)]
        e1, w1 = em[l, 0], wm[l, 0]
        v = ends(n, s)
        x = [where(lo_sub, n[lt], s[lt]) for lt in range(2)]
        m = [sroll(where(lo_sub, s[lt], n[lt]), 4) for lt in range(2)]
        x += strip(l, X, v[0], v[1], e1, w1)
        m += strip(l, M, sroll(v[0], 4), sroll(v[1], 4), lroll(e1, 4), lroll(w1, 124))
        put(bx, p, x, fresh)
        put(bm, p, [closed(t) for t in m], fresh)

    def place_second(l):
        p = l + 1
        n, s = [nb[l, k] for k in range(3)], [sb[l, k] for k in range(3)]
        e1, w1, e2, w2 = em[l, 0], wm[l, 0], em[l, 1], wm[l, 1]
        v = ends(n, s)
        g = [where(lo_sub, n[lt], s[lt]) for lt in range(2)]
        h = [sroll(where(lo_sub, s[lt], n[lt]), 4) for lt in range(2)]
        a = [where(lo_sub, sroll(t, 5), sroll(t, 3)) for t in h]
        g += strip(l, G, v[0], v[1], lroll(e1, 8), lroll(w1, 4))
        hs = [sroll(t, 4) for t in v]
        h += strip(l, H, hs[0], hs[1], e2, w2)
        a_s = [where(lo_half, sroll(t, 3), sroll(t, 5)) for t in hs]
        a += strip(l, A, a_s[0], a_s[1], lroll(e2, 4), lroll(w2, 124))
        for k in range(4):
            bg[p, k], bh[p, k], ba[p, k] = g[k], h[k], a[k]

    def tiles(ref, p):
        return [ref[p, pl.ds(8 * k, 8), :] for k in range(8)]

    def rim_of(full, part, p):
        return [
            full[p, 0, top, :], part[p, 0], full[p, 0, bottom, :],
            full[p, 1, top, :], part[p, 1], full[p, 1, bottom, :],
            part[p, 2], part[p, 3],
        ]

    def rim_east(v):
        r = [lroll(t, 127) for t in v]
        return [where(lane == 127, r[k + 3], r[k]) for k in range(3)] + r[3:]

    def rim_west(v):
        r = [lroll(t, 1) for t in v]
        return r[:3] + [where(lane == 0, r[k], r[k + 3]) for k in range(3)] + r[6:]

    def strip_north(t):
        r = sroll(t, 7)
        return where(sub == 7, lroll(r, 116), r)

    def strip_south(t):
        r = sroll(t, 1)
        return where(sub == 0, lroll(r, 12), r)

    def rim_north(ref, p, v):
        inside = [sroll(v[k], 7) if k % 3 == 2 else ref[p, pl.ds(8 * k + 1, 8), :] for k in range(6)]
        return inside + [strip_north(t) for t in v[6:]]

    def rim_south(ref, p, v):
        inside = [sroll(v[k], 1) if k % 3 == 0 else ref[p, pl.ds(8 * k - 1, 8), :] for k in range(6)]
        return inside + [strip_south(t) for t in v[6:]]

    every = range(8)

    def rim_weights(p):
        m = tiles(bm, p)
        e, n = rim_east(m), rim_north(bm, p, m)
        w = [relu(m[k] + e[k]) for k in every]
        y = [relu(m[k] + n[k]) for k in every]
        put(ve, p, w, every)
        put(vw, p, rim_west(w), every)
        put(vn, p, y, every)
        put(vs, p, rim_south(vn, p, y), every)

    def rim_faces(p):
        lo, hi = tiles(bm, p - 1), tiles(bm, p)
        put(vz, p, [relu(0.5 * (hi[k] + lo[k])) for k in every], every)

    def rim(u, base, count, finish):
        stack = [tiles(u, base + j) for j in range(-1, count + 1)]

        def face(j):
            w = tiles(vz, base + j)
            return [w[k] * (stack[j + 1][k] - stack[j][k]) for k in every]

        fz = face(0)
        for j in range(count):
            p, here = base + j, stack[j + 1]
            fz_up = face(j + 1)
            e, w, n, s = rim_east(here), rim_west(here), rim_north(u, p, here), rim_south(u, p, here)
            we_, ww_, wn_, ws_ = (tiles(ref, p) for ref in (ve, vw, vn, vs))
            finish(
                p,
                [
                    (we_[k] * (e[k] - here[k]) - ww_[k] * (here[k] - w[k]))
                    + (wn_[k] * (n[k] - here[k]) - ws_[k] * (here[k] - s[k]))
                    + (fz_up[k] - fz[k])
                    for k in every
                ],
            )
            fz = fz_up

    def rim1(p, total):
        put(kr, p, [0.5 * t for t in total], every)

    def rim2(p, total):
        h = rim_of(he, bh, p)
        put(x1r, p, [h[k] + total[k] for k in every], every)

    def rim3(p, total):
        a, x = rim_of(ae, ba, p), tiles(x1r, p)
        put(k2r, p, [(x[k] + a[k]) + 0.5 * total[k] for k in every], every)

    def rim4(p, total):
        x = tiles(x1r, p)
        put(x2r, p, [x[k] + total[k] for k in every], every)

    def add_noise(p):
        g, k_ = rim_of(ge, bg, p), tiles(kr, p)
        put(kr, p, [g[k] + k_[k] for k in every], every)

    for i in range(NL):
        place_first(NL * lev + i)
    for i in range(NL):
        rim_weights(own + i)
    for i in range(NL):
        rim_faces(far + i)
    rim(bx, far, 3, rim1)

    for k, ref in ((16, em), (17, wm), (18, na), (19, sa)):
        share(k, ref, NL * other, NL).wait_recv()
    for i in range(NL):
        place_first(NL * other + i)
    for i in range(3):
        rim_weights(next_own + i)
    for i in range(NL):
        rim_faces(next_faces + i)
    rim(bx, near, 4, rim1)

    @pl.when(at_fold)
    def _():
        fold_arrived(fb, 1)
        unfold(fb, nb)
        relays[4].start()

    for i in range(NL):
        place_second(NL * lev + i)
    for i in range(NL):
        add_noise(own + i)
    rim(kr, far, 3, rim2)
    share(20, nb, 1 + 3 * other, 3).wait_recv()
    share(21, sb, 1 + 3 * other, 3).wait_recv()
    for i in range(NL - 1):
        place_second(1 + 3 * other + i)
    for i in range(NL - 1):
        add_noise(next_own + i)
    rim(kr, 4 - lev, 3, rim2)
    rim(x1r, 1 + 3 * lev, 5, rim3)
    rim(k2r, own, 4, rim4)

    def merge(i, _):
        p = own + i
        t = tiles(x2r, p)
        edge = where(halo_w, t[6], t[7])
        for r in range(RT):
            sl = pl.ds(8 * r, 8)
            cols = lroll(edge, 128 - (12 * (r + 1) + 8))
            for lt in range(2):
                cs = pl.ds(128 * lt, 128)
                noise = ra[i, sl, cs] * rw[1, i, sl, cs]
                at = (lane < 4) if lt == 0 else (lane >= 124)
                v = where(at, cols + noise, out[i, sl, cs])
                if r == 0:
                    v = where(lo_sub & ~at, t[3 * lt + 2] + noise, v)
                if r == RT - 1:
                    v = where(~lo_sub & ~at, t[3 * lt] + noise, v)
                out[i, sl, cs] = v
        return 0

    lax.fori_loop(0, NL, merge, 0)

    for c in to_side + to_core + relays:
        c.wait_send()

    @pl.when(south_in)
    def _():
        for c in to_south:
            c.wait_send()

    @pl.when(north_in)
    def _():
        for c in to_north:
            c.wait_send()

    @pl.when(at_fold)
    def _():
        for half in to_fold:
            for c in half:
                c.wait_send()


def local(*args):
    def vm(*shape, dtype=f32):
        return pltpu.VMEM(shape, dtype)

    cells = (NL, ROWS, COLS)
    tile = (8, 128)
    planes = (10, 2, ROWS, 128)
    rim = (2 * NL, 3) + tile
    sides = (2 * NL, 2) + tile
    rows = (NL, 2) + tile
    return pl.pallas_call(
        kernel,
        out_shape=pltpu.VMEM(cells, f32),
        in_specs=[pl.BlockSpec(memory_space=pltpu.HBM)] * 7,
        out_specs=pl.BlockSpec(memory_space=pltpu.VMEM),
        scratch_shapes=[
            vm(*cells), vm(*cells), vm(*cells), vm(*cells, dtype=jnp.int32), vm(2, *cells), vm(2, *cells),
            pltpu.SMEM((LON * COLS,), jnp.int32),
        ]
        + [vm(*planes)] * 12
        + [vm(NL, 2, ROWS, 128)] * 2
        + [vm(2 * NL, 5, 2, *tile)]
        + [vm(10, 64, 128)] * 11
        + [vm(10, 4, *tile)] * 3
        + [vm(*rim)] * 4
        + [vm(*sides)] * 2
        + [vm(*tile)] * 4
        + [vm(2 * LON, NL, *tile)] * 2
        + [vm(*rows)] * 4
        + [vm(*rows)] * 2
        + [vm(*tile)] * 2
        + [
            pltpu.SemaphoreType.DMA((7,)),
            pltpu.SemaphoreType.DMA((22,)),
            pltpu.SemaphoreType.DMA((22,)),
            pltpu.SemaphoreType.DMA((2, LON - 1)),
            pltpu.SemaphoreType.DMA((2, LON - 1)),
        ],
        compiler_params=pltpu.CompilerParams(
            collective_id=0, has_side_effects=True, vmem_limit_bytes=VMEM
        ),
        name="ocean",
    )(*(pltpu.with_memory_space_constraint(v, pltpu.HBM) for v in args))


def solution(mesh):
    block = P("lev", "lat", "lon")
    steps = P(None, "lev", "lat", "lon")
    return jax.shard_map(
        local,
        mesh=mesh,
        in_specs=(block, block, block, steps, steps, block, P()),
        out_specs=block,
        check_vma=False,
    )
```

```python
import jax
import jax.numpy as jnp
from jax import lax
from jax.experimental import pallas as pl
from jax.experimental.pallas import tpu as pltpu
from jax.sharding import PartitionSpec as P


LAT, LON, LEV = 16, 8, 2
NL, ROWS, COLS = 4, 64, 256
RT = ROWS // 8
VMEM = 60 * 1024 * 1024
MESH = pl.DeviceIdType.MESH
f32 = jnp.float32
X, M, G, H, A = range(5)


def kernel(
    tracer, diff, amp, noise_w, noise_z, land, partner, out,
    rx, rd, ra, rl, rw, rz, pc,
    xe, me, ge, he, ae, ke, x1, k2, we, ww, wy, wz, mp, mr, qe, so,
    bx, bm, vn, vs, kr, x1r, k2r, x2r, bg, bh, ba, ve, vw, vz,
    na, sa, nb, sb, em, wm, dne, dnw, dse, dsw, fa, fb,
    tn1, ts1, tn2, ts2, ep, wp, dn, ds,
    isem, ssem, rsem, fsem_s, fsem_r,
):
    lat, lon, lev = lax.axis_index("lat"), lax.axis_index("lon"), lax.axis_index("lev")
    east, west = lax.rem(lon + 1, LON), lax.rem(lon + LON - 1, LON)
    other = 1 - lev
    north_in, south_in = lat < LAT - 1, lat > 0
    at_fold = lat == LAT - 1
    own, theirs = NL * lev + 1, NL * other + 1

    bar = pltpu.get_barrier_semaphore()

    def greet(**where):
        pl.semaphore_signal(bar, inc=1, device_id=where, device_id_type=MESH)

    @pl.when(north_in)
    def _():
        greet(lat=lat + 1)
        greet(lat=lat + 1, lon=east)
        greet(lat=lat + 1, lon=west)

    @pl.when(south_in)
    def _():
        greet(lat=lat - 1)
        greet(lat=lat - 1, lon=east)
        greet(lat=lat - 1, lon=west)

    greet(lon=east)
    greet(lon=west)

    @pl.when(at_fold)
    def _():
        for k in (2, 4, 6):
            greet(lon=lax.rem(lon + k, LON))

    greet(lev=other)

    loads = [
        pltpu.make_async_copy(s, d, isem.at[k])
        for k, (s, d) in enumerate(
            ((tracer, rx), (diff, rd), (land, rl), (amp, ra), (noise_z, rz), (noise_w, rw), (partner, pc))
        )
    ]
    for c in loads:
        c.start()

    lane = lax.broadcasted_iota(jnp.int32, (8, 128), 1)
    sub = lax.broadcasted_iota(jnp.int32, (8, 128), 0)
    lo_half, lo_sub = lane < 64, sub < 4
    group_e = (lane * 171) >> 11
    group_w = (((lane + 8) * 171) >> 11) - 1
    k12 = lane - 12 * group_e
    halo_e, halo_w = k12 >= 8, (k12 >= 4) & (k12 < 8)
    ring_e = (group_e == 0) | (group_e == RT + 1)
    ring_w = (group_w == 0) | (group_w == RT + 1)
    zero = jnp.zeros((8, 128), f32)
    where = jnp.where

    def lroll(v, s):
        s = s % 128
        return v if s == 0 else pltpu.roll(v, s, 1)

    def sroll(v, s):
        return pltpu.roll(v, s, 0)

    def closed(v):
        return where(v > 0, v, -1.0)

    def both(v):
        return where(lo_half, v[0], v[1])

    top, bottom = pl.ds(ROWS - 8, 8), pl.ds(0, 8)

    def rows_at(r):
        return pl.ds(pl.multiple_of(8 * r, 8), 8)

    for p in (0, 9):
        for r in range(RT):
            sl = pl.ds(8 * r, 8)
            for lt in range(2):
                me[p, lt, sl, :] = zero - 1.0
                for ref in (xe, ke, x1, k2):
                    ref[p, lt, sl, :] = zero
            bm[p, sl, :] = zero - 1.0
            for ref in (bx, kr, x1r, k2r):
                ref[p, sl, :] = zero

    @pl.when(lat == 0)
    def _():
        for i in range(NL):
            for lt in range(3):
                sa[NL * lev + i, lt] = zero
                sb[NL * lev + i, lt] = zero

    for c in loads[:3]:
        c.wait()

    def prep_first(i, _):
        p = own + i
        for r in range(RT):
            sl = pl.ds(8 * r, 8)
            for lt in range(2):
                cs = pl.ds(128 * lt, 128)
                m = 0.5 * rd[i, sl, cs] * rl[i, sl, cs].astype(f32)
                xe[p, lt, sl, :] = rx[i, sl, cs]
                mp[i, lt, sl, :] = m
                me[p, lt, sl, :] = closed(m)
        return 0

    lax.fori_loop(0, NL, prep_first, 0)

    def first_rows(x, m):
        return where(lo_sub, x, sroll(m, 4))

    def first_rows2(g, h, a):
        return where(lo_sub, g, where(sub == 7, sroll(a, 7), sroll(h, 4)))

    def last_rows(x, m):
        return where(lo_sub, sroll(m, 4), x)

    def last_rows2(g, h, a):
        return where(lo_sub, where(sub == 0, sroll(a, 1), sroll(h, 4)), g)

    def mirror_rows(v):
        for b in (1, 2, 4):
            v = where((sub & b) != 0, sroll(v, b), sroll(v, 8 - b))
        return v

    def mirror_lanes(v):
        return jnp.take_along_axis(v, 127 - lane, axis=1, mode="promise_in_bounds")

    for i in range(NL):
        for lt in range(2):
            tn1[i, lt] = first_rows(xe[own + i, lt, bottom, :], mp[i, lt, bottom, :])
            ts1[i, lt] = last_rows(xe[own + i, lt, top, :], mp[i, lt, top, :])

    @pl.when(at_fold)
    def _():
        for i in range(NL):
            for lt in range(2):
                x, m = mirror_rows(xe[own + i, lt, top, :]), mirror_rows(mp[i, lt, top, :])
                fa[2 * lon + lt, i] = mirror_lanes(first_rows(x, m))

    def pack_strip(i, f, ref, q):
        s_e, s_w = zero, zero
        for r in range(RT):
            sl = pl.ds(8 * r, 8)
            v = lroll(where(lo_half, ref[q, 0, sl, :], ref[q, 1, sl, :]), 12 * (r + 1) + 8)
            s_e = where(group_e == r + 1, v, s_e)
            s_w = where(group_w == r + 1, v, s_w)
        so[own + i - 1, f, 0] = s_e
        so[own + i - 1, f, 1] = s_w

    def strips_first(i, _):
        pack_strip(i, X, xe, own + i)
        pack_strip(i, M, mp, i)
        return 0

    lax.fori_loop(0, NL, strips_first, 0)

    for c in loads[3:]:
        c.wait()

    def prep_second(i, _):
        p = own + i
        for r in range(RT):
            sl = pl.ds(8 * r, 8)
            for lt in range(2):
                cs = pl.ds(128 * lt, 128)
                x = rx[i, sl, cs]
                amp_ = ra[i, sl, cs]
                ge[p, lt, sl, :] = x + amp_ * rz[0, i, sl, cs]
                he[p, lt, sl, :] = x + amp_ * rw[0, i, sl, cs]
                ae[p, lt, sl, :] = amp_ * rz[1, i, sl, cs]
                qe[i, lt, sl, :] = amp_ * rw[1, i, sl, cs]
        return 0

    lax.fori_loop(0, NL, prep_second, 0)
    for i in range(NL):
        p = own + i
        for lt in range(2):
            tn2[i, lt] = first_rows2(ge[p, lt, bottom, :], he[p, lt, bottom, :], ae[p, lt, bottom, :])
            ts2[i, lt] = last_rows2(ge[p, lt, top, :], he[p, lt, top, :], ae[p, lt, top, :])

    @pl.when(at_fold)
    def _():
        for i in range(NL):
            p = own + i
            for lt in range(2):
                g, h, a = (mirror_rows(ref[p, lt, top, :]) for ref in (ge, he, ae))
                fb[2 * lon + lt, i] = mirror_lanes(first_rows2(g, h, a))

    for halves, dst in (((tn1, tn2), dn), ((ts1, ts2), ds)):
        d = zero
        for i in range(NL):
            for n, half in enumerate(halves):
                k = 2 * i + n
                d = where((lane >> 3) == k, lroll(both(half[i]), 8 * k + 4), d)
        dst[...] = d

    def strips_second(i, _):
        for f, ref in ((G, ge), (H, he), (A, ae)):
            pack_strip(i, f, ref, own + i)
        x, m, g, h, a = (so[own + i - 1, f, 0] for f in range(5))
        ep[i, 0] = where(halo_e, x, where(halo_w, lroll(m, 124), lroll(g, 120)))
        ep[i, 1] = where(halo_e, h, lroll(a, 124))
        wp[i, 0] = where(halo_w, x, where(halo_e, lroll(m, 4), lroll(g, 124)))
        wp[i, 1] = where(halo_w, h, lroll(a, 4))
        return 0

    early = lax.rem(lat, LAT // 2) < LAT // 4

    @pl.when(early)
    def _():
        lax.fori_loop(0, NL, strips_second, 0)

    @pl.when(lat == 0)
    def _():
        pl.semaphore_wait(bar, 6)

    @pl.when(south_in)
    def _():
        pl.semaphore_wait(bar, 9)

    def send(k, src, dst, **where):
        return pltpu.make_async_remote_copy(
            src_ref=src, dst_ref=dst, send_sem=ssem.at[k], recv_sem=rsem.at[k],
            device_id=where, device_id_type=MESH,
        )

    mine = pl.ds(NL * lev, NL)
    two = pl.ds(0, 2)
    up, down = jnp.minimum(lat + 1, LAT - 1), jnp.maximum(lat - 1, 0)
    to_south = [
        send(0, tn1, na.at[mine, two], lat=down),
        send(1, tn2, nb.at[mine, two], lat=down),
        send(2, dn, dne, lat=down, lon=west),
        send(3, dn, dnw, lat=down, lon=east),
    ]
    to_north = [
        send(4, ts1, sa.at[mine, two], lat=up),
        send(5, ts2, sb.at[mine, two], lat=up),
        send(6, ds, dse, lat=up, lon=west),
        send(7, ds, dsw, lat=up, lon=east),
    ]
    to_side = [
        send(8, ep, em.at[mine], lon=west),
        send(9, wp, wm.at[mine], lon=east),
    ]

    def beside(i):
        return i + 1 - 2 * lax.rem(i, 2)

    def fold_copy(ref, half, n, owner, target):
        slot = ref.at[pl.ds(2 * owner, 2)]
        return pltpu.make_async_remote_copy(
            src_ref=slot, dst_ref=slot, send_sem=fsem_s.at[half, n], recv_sem=fsem_r.at[half, n],
            device_id={"lon": target}, device_id_type=MESH,
        )

    def fold_out(ref, half, n):
        k = n if n < 4 else n - 3
        target = beside(lon) if n == 0 else lax.rem(lon + 2 * k, LON)
        return fold_copy(ref, half, n, lon if n < 4 else beside(lon), target)

    def fold_in(ref, half, n):
        k = n if n < 4 else n - 3
        sender = beside(lon) if n == 0 else lax.rem(lon + LON - 2 * k, LON)
        fold_copy(ref, half, n, sender if n < 4 else beside(sender), sender).wait_recv()

    to_fold = [[fold_out(ref, half, n) for n in range(7)] for half, ref in enumerate((fa, fb))]

    def planes(ref, start, count):
        return ref.at[pl.ds(start, count)]

    def share(k, ref, start, count):
        part = planes(ref, start, count)
        return send(k, part, part, lev=other)

    @pl.when(at_fold)
    def _():
        for half in to_fold:
            for c in half[:4]:
                c.start()

    @pl.when(south_in)
    def _():
        for k in (2, 3, 0, 1):
            to_south[k].start()

    @pl.when(north_in)
    def _():
        for k in (2, 3, 0, 1):
            to_north[k].start()

    @pl.when(early)
    def _():
        for c in to_side:
            c.start()

    to_core = [
        share(10, xe, own, NL),
        send(11, mp, mr, lev=other),
        share(12, ge, 2 + 3 * lev, 3),
        share(13, he, 3 + 2 * lev, 2),
        share(14, ae, 4 + lev, 1),
        share(15, so, NL * lev, NL),
    ]
    for c in to_core[:5]:
        c.start()

    @pl.when(jnp.logical_not(early))
    def _():
        lax.fori_loop(0, NL, strips_second, 0)
        for c in to_side:
            c.start()

    to_core[5].start()

    def pair(ref, p, r):
        sl = pl.ds(8 * r, 8)
        return [ref[p, lt, sl, :] for lt in range(2)]

    def shifted(ref, p, r, d):
        if 0 <= 8 * r + d <= ROWS - 8:
            return [ref[p, lt, pl.ds(8 * r + d, 8), :] for lt in range(2)]
        return [sroll(t, -d % 8) for t in pair(ref, p, r)]

    def east_of(v):
        r0, r1 = lroll(v[0], 127), lroll(v[1], 127)
        return [where(lane == 127, r1, r0), r1]

    def west_of(v):
        r0, r1 = lroll(v[0], 1), lroll(v[1], 1)
        return [r0, where(lane == 0, r0, r1)]

    def relu(v):
        return jnp.maximum(v, 0.0)

    def weights(p, face):
        for r in range(RT):
            sl = pl.ds(8 * r, 8)
            here, n = pair(me, p, r), shifted(me, p, r, 1)
            e = east_of(here)
            w = [relu(here[k] + e[k]) for k in range(2)]
            v = west_of(w)
            hi, lo = pair(me, face, r), pair(me, face - 1, r)
            for k in range(2):
                we[p, k, sl, :] = w[k]
                ww[p, k, sl, :] = v[k]
                wy[p, k, sl, :] = relu(here[k] + n[k])
                wz[face, k, sl, :] = relu(0.5 * (hi[k] + lo[k]))

    def inner(u, p, count, finish):
        for r in range(RT):
            stack = [pair(u, p + j, r) for j in range(-1, count + 1)]
            fz = [
                [w * (hi - lo) for w, lo, hi in zip(pair(wz, p + j, r), stack[j], stack[j + 1])]
                for j in range(count + 1)
            ]
            for j in range(count):
                here, q = stack[j + 1], p + j
                n, s = shifted(u, q, r, 1), shifted(u, q, r, -1)
                wn, ws = pair(wy, q, r), shifted(wy, q, r, -1)
                e, w, v, wv = east_of(here), pair(we, q, r), west_of(here), pair(ww, q, r)
                for k in range(2):
                    total = (
                        (w[k] * (e[k] - here[k]) - wv[k] * (here[k] - v[k]))
                        + (wn[k] * (n[k] - here[k]) - ws[k] * (here[k] - s[k]))
                        + (fz[j + 1][k] - fz[j][k])
                    )
                    finish(q, pl.ds(8 * r, 8), k, total)

    def finish1(p, sl, k, total):
        ke[p, k, sl, :] = ge[p, k, sl, :] + 0.5 * total

    def finish2(p, sl, k, total):
        x1[p, k, sl, :] = he[p, k, sl, :] + total

    def finish3(p, sl, k, total):
        k2[p, k, sl, :] = (x1[p, k, sl, :] + ae[p, k, sl, :]) + 0.5 * total

    def finish4(p, sl, k, total):
        j = p - own
        out[j, sl, pl.ds(128 * k, 128)] = (x1[p, k, sl, :] + qe[j, k, sl, :]) + total

    far, near = 1 + 5 * lev, 4 - 2 * lev
    next_own, next_faces = 2 + 3 * other, 5 - 3 * lev

    def own_weights(j, _):
        weights(own + j, far + j)
        return 0

    def other_weights(j, _):
        weights(theirs + j, next_faces + j)
        return 0

    lax.fori_loop(0, NL, own_weights, 0)
    inner(xe, far, 3, finish1)

    def copy_own(i, _):
        p = own + i
        for ref, to in ((xe, bx), (me, bm)):
            for lt in range(2):
                to[p, pl.ds(24 * lt, 8), :] = ref[p, lt, top, :]
                to[p, pl.ds(24 * lt + 16, 8), :] = ref[p, lt, bottom, :]
        return 0

    lax.fori_loop(0, NL, copy_own, 0)

    @pl.when(at_fold)
    def _():
        for half, ref in enumerate((fa, fb)):
            fold_in(ref, half, 0)
            for c in to_fold[half][4:]:
                c.start()

    share(10, xe, theirs, NL).wait_recv()
    to_core[1].wait_recv()

    def close(i, _):
        p = theirs + i
        for r in range(RT):
            sl = pl.ds(8 * r, 8)
            for lt in range(2):
                me[p, lt, sl, :] = closed(mr[i, lt, sl, :])
        for ref, to in ((xe, bx), (me, bm)):
            for lt in range(2):
                to[p, pl.ds(24 * lt, 8), :] = ref[p, lt, top, :]
                to[p, pl.ds(24 * lt + 16, 8), :] = ref[p, lt, bottom, :]
        return 0

    lax.fori_loop(0, NL, close, 0)
    lax.fori_loop(0, NL, other_weights, 0)
    share(12, ge, next_own, 3).wait_recv()
    inner(xe, near, 4, finish1)
    share(13, he, 3 + 2 * other, 2).wait_recv()

    def inner2(j, _):
        inner(ke, 1 + 2 * lev + 3 * j, 3, finish2)
        return 0

    lax.fori_loop(0, 2, inner2, 0)
    share(14, ae, 4 + other, 1).wait_recv()
    inner(x1, 1 + 3 * lev, 5, finish3)
    inner(k2, own, 4, finish4)
    share(15, so, NL * other, NL).wait_recv()

    for c in to_side + to_core:
        c.wait_send()

    @pl.when(south_in)
    def _():
        for c in to_south:
            c.wait_send()

    @pl.when(north_in)
    def _():
        for c in to_north:
            c.wait_send()

    @pl.when(at_fold)
    def _():
        for half in to_fold:
            for c in half:
                c.wait_send()

    relays = [
        share(16, em, NL * lev, NL),
        share(17, wm, NL * lev, NL),
        share(18, na, NL * lev, NL),
        share(19, sa, NL * lev, NL),
        share(20, nb, 1 + 3 * lev, 3),
        share(21, sb, 1 + 3 * lev, 3),
    ]
    to_side[0].wait_recv()
    relays[0].start()
    to_side[1].wait_recv()
    relays[1].start()

    def corners(w_ref, e_ref, at, one, half2):
        d = where((lane & 4) == 0, w_ref[...], e_ref[...])
        for i in range(NL):
            one[NL * lev + i, 2] = lroll(d, at - 16 * i)
            half2[NL * lev + i, 2] = lroll(d, at - 16 * i - 8)

    @pl.when(south_in)
    def _():
        for k in (0, 2, 3):
            to_north[k].wait_recv()
        corners(dsw, dse, 4, sa, sb)

    relays[3].start()

    c0 = (pc[0] - COLS * lon) & (LON * COLS - 1)
    t0, shift = c0 >> 7, c0 & 127

    def unfold(src, dst):
        for i in range(NL):
            t = [src[(t0 + k) & (2 * LON - 1), i] for k in (-3, -2, -1, 0, 1)]
            v = [
                pltpu.roll(where(lane >= 127 - shift, t[k + 1], t[k]), (shift + 1) & 127, 1)
                for k in range(4)
            ]
            dst[NL * lev + i, 0] = v[2]
            dst[NL * lev + i, 1] = v[1]
            dst[NL * lev + i, 2] = lroll(where(lo_half, v[0], v[3]), 116)

    def fold_arrived(ref, half):
        for n in range(1, 7):
            fold_in(ref, half, n)

    @pl.when(north_in)
    def _():
        for k in (0, 2, 3):
            to_south[k].wait_recv()
        corners(dnw, dne, 112, na, nb)

    @pl.when(at_fold)
    def _():
        fold_arrived(fa, 0)
        unfold(fa, na)

    relays[2].start()

    @pl.when(south_in)
    def _():
        to_north[1].wait_recv()

    relays[5].start()

    @pl.when(north_in)
    def _():
        to_south[1].wait_recv()
        relays[4].start()

    def ends(n, s):
        r = where(lo_half, lroll(both(s), 8), lroll(both(n), 116))
        c = where(lo_half, s[2], n[2])
        return where(halo_e, c, r), where(halo_w, c, r)

    def strip(l, f, v_e, v_w, from_e, from_w):
        return (
            where(ring_e, v_e, where(halo_e, from_e, so[l, f, 0])),
            where(ring_w, v_w, where(halo_w, from_w, so[l, f, 1])),
        )

    def put(ref, p, tiles, which):
        for k, t in zip(which, tiles):
            ref[p, pl.ds(8 * k, 8), :] = t

    fresh = (1, 4, 6, 7)

    def place_first(l):
        p = l + 1
        n, s = [na[l, k] for k in range(3)], [sa[l, k] for k in range(3)]
        e1, w1 = em[l, 0], wm[l, 0]
        v = ends(n, s)
        x = [where(lo_sub, n[lt], s[lt]) for lt in range(2)]
        m = [sroll(where(lo_sub, s[lt], n[lt]), 4) for lt in range(2)]
        x += strip(l, X, v[0], v[1], e1, w1)
        m += strip(l, M, sroll(v[0], 4), sroll(v[1], 4), lroll(e1, 4), lroll(w1, 124))
        put(bx, p, x, fresh)
        put(bm, p, [closed(t) for t in m], fresh)

    def place_second(l):
        p = l + 1
        n, s = [nb[l, k] for k in range(3)], [sb[l, k] for k in range(3)]
        e1, w1, e2, w2 = em[l, 0], wm[l, 0], em[l, 1], wm[l, 1]
        v = ends(n, s)
        g = [where(lo_sub, n[lt], s[lt]) for lt in range(2)]
        h = [sroll(where(lo_sub, s[lt], n[lt]), 4) for lt in range(2)]
        a = [where(lo_sub, sroll(t, 5), sroll(t, 3)) for t in h]
        g += strip(l, G, v[0], v[1], lroll(e1, 8), lroll(w1, 4))
        hs = [sroll(t, 4) for t in v]
        h += strip(l, H, hs[0], hs[1], e2, w2)
        a_s = [where(lo_half, sroll(t, 3), sroll(t, 5)) for t in hs]
        a += strip(l, A, a_s[0], a_s[1], lroll(e2, 4), lroll(w2, 124))
        for k in range(4):
            bg[p, k], bh[p, k], ba[p, k] = g[k], h[k], a[k]

    def tiles(ref, p):
        return [ref[p, pl.ds(8 * k, 8), :] for k in range(8)]

    def rim_of(full, part, p):
        return [
            full[p, 0, top, :], part[p, 0], full[p, 0, bottom, :],
            full[p, 1, top, :], part[p, 1], full[p, 1, bottom, :],
            part[p, 2], part[p, 3],
        ]

    def rim_east(v):
        r = [lroll(t, 127) for t in v]
        return [where(lane == 127, r[k + 3], r[k]) for k in range(3)] + r[3:]

    def rim_west(v):
        r = [lroll(t, 1) for t in v]
        return r[:3] + [where(lane == 0, r[k], r[k + 3]) for k in range(3)] + r[6:]

    def strip_north(t):
        r = sroll(t, 7)
        return where(sub == 7, lroll(r, 116), r)

    def strip_south(t):
        r = sroll(t, 1)
        return where(sub == 0, lroll(r, 12), r)

    def rim_north(ref, p, v):
        inside = [sroll(v[k], 7) if k % 3 == 2 else ref[p, pl.ds(8 * k + 1, 8), :] for k in range(6)]
        return inside + [strip_north(t) for t in v[6:]]

    def rim_south(ref, p, v):
        inside = [sroll(v[k], 1) if k % 3 == 0 else ref[p, pl.ds(8 * k - 1, 8), :] for k in range(6)]
        return inside + [strip_south(t) for t in v[6:]]

    every = range(8)

    def rim_weights(p):
        m = tiles(bm, p)
        e, n = rim_east(m), rim_north(bm, p, m)
        w = [relu(m[k] + e[k]) for k in every]
        v = rim_west(w)
        for q, k in enumerate(fresh):
            ve[p, q], vw[p, q] = w[k], v[k]
        y = [relu(m[k] + n[k]) for k in every]
        put(vn, p, y, every)
        put(vs, p, rim_south(vn, p, y), every)

    def rim_faces(p):
        for q, k in enumerate(fresh):
            sl = pl.ds(8 * k, 8)
            vz[p, q] = relu(0.5 * (bm[p, sl, :] + bm[p - 1, sl, :]))

    def rim(u, base, count, finish):
        stack = [tiles(u, base + j) for j in range(-1, count + 1)]

        def face(j):
            w = rim_of(wz, vz, base + j)
            return [w[k] * (stack[j + 1][k] - stack[j][k]) for k in every]

        fz = face(0)
        for j in range(count):
            p, here = base + j, stack[j + 1]
            fz_up = face(j + 1)
            e, w, n, s = rim_east(here), rim_west(here), rim_north(u, p, here), rim_south(u, p, here)
            we_, ww_ = rim_of(we, ve, p), rim_of(ww, vw, p)
            wn_, ws_ = tiles(vn, p), tiles(vs, p)
            finish(
                p,
                [
                    (we_[k] * (e[k] - here[k]) - ww_[k] * (here[k] - w[k]))
                    + (wn_[k] * (n[k] - here[k]) - ws_[k] * (here[k] - s[k]))
                    + (fz_up[k] - fz[k])
                    for k in every
                ],
            )
            fz = fz_up

    def rim1(p, total):
        put(kr, p, [0.5 * t for t in total], every)

    def rim2(p, total):
        h = rim_of(he, bh, p)
        put(x1r, p, [h[k] + total[k] for k in every], every)

    def rim3(p, total):
        a, x = rim_of(ae, ba, p), tiles(x1r, p)
        put(k2r, p, [(x[k] + a[k]) + 0.5 * total[k] for k in every], every)

    def rim4(p, total):
        x = tiles(x1r, p)
        put(x2r, p, [x[k] + total[k] for k in every], every)

    def add_noise(p):
        g, k_ = rim_of(ge, bg, p), tiles(kr, p)
        put(kr, p, [g[k] + k_[k] for k in every], every)

    for i in range(NL):
        place_first(NL * lev + i)
    for i in range(NL):
        rim_weights(own + i)
    for i in range(NL):
        rim_faces(far + i)
    rim(bx, far, 3, rim1)

    @pl.when(at_fold)
    def _():
        fold_arrived(fb, 1)
        unfold(fb, nb)
        relays[4].start()

    for i in range(NL):
        place_second(NL * lev + i)
    for i in range(3):
        add_noise(far + i)
    rim(kr, 1 + 6 * lev, 2, rim2)
    rim(x1r, 1 + 7 * lev, 1, rim3)

    for k, ref in ((16, em), (17, wm), (18, na), (19, sa)):
        share(k, ref, NL * other, NL).wait_recv()
    for i in range(NL):
        place_first(NL * other + i)
    for i in range(3):
        rim_weights(next_own + i)
    for i in range(NL):
        rim_faces(next_faces + i)
    rim(bx, near, 4, rim1)
    share(20, nb, 1 + 3 * other, 3).wait_recv()
    share(21, sb, 1 + 3 * other, 3).wait_recv()
    for i in range(NL - 1):
        place_second(1 + 3 * other + i)
    for i in range(NL):
        add_noise(near + i)
    rim(kr, 3, 4, rim2)
    rim(x1r, 2 + 2 * lev, 4, rim3)
    rim(k2r, own, 4, rim4)

    for i in range(NL):
        t = tiles(x2r, own + i)
        edge = where(halo_w, t[6], t[7])
        for lt in range(2):
            cs = pl.ds(128 * lt, 128)
            pltpu.store(out.at[i, bottom, cs], t[3 * lt + 2] + qe[i, lt, bottom, :], mask=lo_sub)
            pltpu.store(out.at[i, top, cs], t[3 * lt] + qe[i, lt, top, :], mask=sub >= 4)
        for r in range(RT):
            sl = pl.ds(8 * r, 8)
            cols = lroll(edge, 128 - (12 * (r + 1) + 8))
            pltpu.store(out.at[i, sl, pl.ds(0, 128)], cols + qe[i, 0, sl, :], mask=lane < 4)
            pltpu.store(out.at[i, sl, pl.ds(128, 128)], cols + qe[i, 1, sl, :], mask=lane >= 124)

    for c in relays:
        c.wait_send()


def local(*args):
    def vm(*shape, dtype=f32):
        return pltpu.VMEM(shape, dtype)

    cells = (NL, ROWS, COLS)
    tile = (8, 128)
    planes = (10, 2, ROWS, 128)
    rim = (2 * NL, 3) + tile
    sides = (2 * NL, 2) + tile
    rows = (NL, 2) + tile
    return pl.pallas_call(
        kernel,
        out_shape=pltpu.VMEM(cells, f32),
        in_specs=[pl.BlockSpec(memory_space=pltpu.HBM)] * 7,
        out_specs=pl.BlockSpec(memory_space=pltpu.VMEM),
        scratch_shapes=[
            vm(*cells), vm(*cells), vm(*cells), vm(*cells, dtype=jnp.int32), vm(2, *cells), vm(2, *cells),
            pltpu.SMEM((LON * COLS,), jnp.int32),
        ]
        + [vm(*planes)] * 12
        + [vm(NL, 2, ROWS, 128)] * 3
        + [vm(2 * NL, 5, 2, *tile)]
        + [vm(10, 64, 128)] * 8
        + [vm(10, 4, *tile)] * 6
        + [vm(*rim)] * 4
        + [vm(*sides)] * 2
        + [vm(*tile)] * 4
        + [vm(2 * LON, NL, *tile)] * 2
        + [vm(*rows)] * 4
        + [vm(*rows)] * 2
        + [vm(*tile)] * 2
        + [
            pltpu.SemaphoreType.DMA((7,)),
            pltpu.SemaphoreType.DMA((22,)),
            pltpu.SemaphoreType.DMA((22,)),
            pltpu.SemaphoreType.DMA((2, LON - 1)),
            pltpu.SemaphoreType.DMA((2, LON - 1)),
        ],
        compiler_params=pltpu.CompilerParams(
            collective_id=0, has_side_effects=True, vmem_limit_bytes=VMEM
        ),
        name="ocean",
    )(*(pltpu.with_memory_space_constraint(v, pltpu.HBM) for v in args))


def solution(mesh):
    block = P("lev", "lat", "lon")
    steps = P(None, "lev", "lat", "lon")
    return jax.shard_map(
        local,
        mesh=mesh,
        in_specs=(block, block, block, steps, steps, block, P()),
        out_specs=block,
        check_vma=False,
    )
```

```python
import jax
import jax.numpy as jnp
from jax import lax
from jax.experimental import pallas as pl
from jax.experimental.pallas import tpu as pltpu
from jax.sharding import PartitionSpec as P


LAT, LON, LEV = 16, 8, 2
NL, ROWS, COLS = 4, 64, 256
RT = ROWS // 8
VMEM = 60 * 1024 * 1024
MESH = pl.DeviceIdType.MESH
f32 = jnp.float32
X, M, G, H, A = range(5)


def kernel(
    tracer, diff, amp, noise_w, noise_z, land, partner, out,
    rx, rd, ra, rl, rw, rz, pc,
    xe, me, ge, he, ae, ke, x1, k2, we, ww, wy, wz, mp, mr, qe, so,
    bx, bm, vn, kr, x1r, k2r, x2r, bg, bh, ba, ve, vw, vz,
    na, sa, nb, sb, em, wm, dne, dnw, dse, dsw, fa, fb, ga, gb,
    tn1, ts1, tn2, ts2, ep, wp, dn, ds,
    isem, ssem, rsem, fsem_s, fsem_r, told,
):
    lat, lon, lev = lax.axis_index("lat"), lax.axis_index("lon"), lax.axis_index("lev")
    east, west = lax.rem(lon + 1, LON), lax.rem(lon + LON - 1, LON)
    other = 1 - lev
    north_in, south_in = lat < LAT - 1, lat > 0
    at_fold = lat == LAT - 1
    own, theirs = NL * lev + 1, NL * other + 1

    def beside(i):
        return i + 1 - 2 * lax.rem(i, 2)

    bar = pltpu.get_barrier_semaphore()

    def greet(**where):
        pl.semaphore_signal(bar, inc=1, device_id=where, device_id_type=MESH)

    late_row = lax.rem(lat, LAT // 2) // (LAT // 4)
    fold_row, below_fold = (lat + 1) // LAT, (lat + 2) // LAT

    @pl.when(north_in)
    def _():
        for k in (lon, east, west):
            greet(lat=lat + 1, lon=k, lev=1 - below_fold * other)

    greet(lev=other)
    for k in (east, west):
        greet(lon=k, lev=late_row - fold_row * other)

    @pl.when(at_fold)
    def _():
        greet(lon=beside(lon), lev=other)
        for k in (2, 4, 6):
            greet(lon=lax.rem(lon + k, LON))
            greet(lon=lax.rem(lon + k, LON), lev=other)

    @pl.when(south_in)
    def _():
        for k in (lon, east, west):
            greet(lat=lat - 1, lon=k, lev=0)

    loads = [
        pltpu.make_async_copy(s, d, isem.at[k])
        for k, (s, d) in enumerate(
            ((tracer, rx), (diff, rd), (land, rl), (amp, ra), (noise_z, rz), (noise_w, rw), (partner, pc))
        )
    ]
    for c in loads:
        c.start()

    lane = lax.broadcasted_iota(jnp.int32, (8, 128), 1)
    sub = lax.broadcasted_iota(jnp.int32, (8, 128), 0)
    lo_half, lo_sub = lane < 64, sub < 4
    group_e = (lane * 171) >> 11
    group_w = (((lane + 8) * 171) >> 11) - 1
    k12 = lane - 12 * group_e
    halo_e, halo_w = k12 >= 8, (k12 >= 4) & (k12 < 8)
    ring_e = (group_e == 0) | (group_e == RT + 1)
    ring_w = (group_w == 0) | (group_w == RT + 1)
    zero = jnp.zeros((8, 128), f32)
    where = jnp.where

    def lroll(v, s):
        s = s % 128
        return v if s == 0 else pltpu.roll(v, s, 1)

    def sroll(v, s):
        return pltpu.roll(v, s, 0)

    def closed(v):
        return where(v > 0, v, -1.0)

    def both(v):
        return where(lo_half, v[0], v[1])

    top, bottom = pl.ds(ROWS - 8, 8), pl.ds(0, 8)

    def rows_at(r):
        return pl.ds(pl.multiple_of(8 * r, 8), 8)

    for p in (0, 9):
        for r in range(RT + 4):
            sl = pl.ds(8 * r, 8)
            bm[p, sl, :] = zero - 1.0
            for ref in (bx, kr, x1r, k2r):
                ref[p, sl, :] = zero
        for r in range(RT):
            sl = pl.ds(8 * r, 8)
            for lt in range(2):
                me[p, lt, sl, :] = zero - 1.0
                for ref in (xe, ke, x1, k2):
                    ref[p, lt, sl, :] = zero

    @pl.when(lat == 0)
    def _():
        for i in range(NL):
            for lt in range(3):
                sa[NL * lev + i, lt] = zero
                sb[NL * lev + i, lt] = zero

    for c in loads[:3]:
        c.wait()

    def prep_first(i, _):
        p = own + i
        for r in range(RT):
            sl = pl.ds(8 * r, 8)
            for lt in range(2):
                cs = pl.ds(128 * lt, 128)
                m = 0.5 * rd[i, sl, cs] * rl[i, sl, cs].astype(f32)
                xe[p, lt, sl, :] = rx[i, sl, cs]
                mp[i, lt, sl, :] = m
                me[p, lt, sl, :] = closed(m)
        return 0

    lax.fori_loop(0, NL, prep_first, 0)

    def first_rows(x, m):
        return where(lo_sub, x, sroll(m, 4))

    def first_rows2(g, h, a):
        return where(lo_sub, g, where(sub == 7, sroll(a, 7), sroll(h, 4)))

    def last_rows(x, m):
        return where(lo_sub, sroll(m, 4), x)

    def last_rows2(g, h, a):
        return where(lo_sub, where(sub == 0, sroll(a, 1), sroll(h, 4)), g)

    def mirror_rows(v):
        for b in (1, 2, 4):
            v = where((sub & b) != 0, sroll(v, b), sroll(v, 8 - b))
        return v

    def mirror_lanes(v):
        return jnp.take_along_axis(v, 127 - lane, axis=1, mode="promise_in_bounds")

    for i in range(NL):
        for lt in range(2):
            tn1[i, lt] = first_rows(xe[own + i, lt, bottom, :], mp[i, lt, bottom, :])
            ts1[i, lt] = last_rows(xe[own + i, lt, top, :], mp[i, lt, top, :])

    @pl.when(at_fold)
    def _():
        for i in range(NL):
            for lt in range(2):
                x, m = mirror_rows(xe[own + i, lt, top, :]), mirror_rows(mp[i, lt, top, :])
                fa[2 * lon + lt, i] = mirror_lanes(first_rows(x, m))

    def pack_strip(i, f, ref, q):
        s_e, s_w = zero, zero
        for r in range(RT):
            sl = pl.ds(8 * r, 8)
            v = lroll(where(lo_half, ref[q, 0, sl, :], ref[q, 1, sl, :]), 12 * (r + 1) + 8)
            s_e = where(group_e == r + 1, v, s_e)
            s_w = where(group_w == r + 1, v, s_w)
        so[own + i - 1, f, 0] = s_e
        so[own + i - 1, f, 1] = s_w

    def strips_first(i, _):
        pack_strip(i, X, xe, own + i)
        pack_strip(i, M, mp, i)
        return 0

    lax.fori_loop(0, NL, strips_first, 0)

    for c in loads[3:]:
        c.wait()

    def prep_second(i, _):
        p = own + i
        for r in range(RT):
            sl = pl.ds(8 * r, 8)
            for lt in range(2):
                cs = pl.ds(128 * lt, 128)
                x = rx[i, sl, cs]
                amp_ = ra[i, sl, cs]
                ge[p, lt, sl, :] = x + amp_ * rz[0, i, sl, cs]
                he[p, lt, sl, :] = x + amp_ * rw[0, i, sl, cs]
                ae[p, lt, sl, :] = amp_ * rz[1, i, sl, cs]
                qe[i, lt, sl, :] = amp_ * rw[1, i, sl, cs]
        return 0

    lax.fori_loop(0, NL, prep_second, 0)
    for i in range(NL):
        p = own + i
        for lt in range(2):
            tn2[i, lt] = first_rows2(ge[p, lt, bottom, :], he[p, lt, bottom, :], ae[p, lt, bottom, :])
            ts2[i, lt] = last_rows2(ge[p, lt, top, :], he[p, lt, top, :], ae[p, lt, top, :])

    @pl.when(at_fold)
    def _():
        for i in range(NL):
            p = own + i
            for lt in range(2):
                g, h, a = (mirror_rows(ref[p, lt, top, :]) for ref in (ge, he, ae))
                fb[2 * lon + lt, i] = mirror_lanes(first_rows2(g, h, a))

    for halves, dst in (((tn1, tn2), dn), ((ts1, ts2), ds)):
        d = zero
        for i in range(NL):
            for n, half in enumerate(halves):
                k = 2 * i + n
                d = where((lane >> 3) == k, lroll(both(half[i]), 8 * k + 4), d)
        dst[...] = d

    def strips_second(i, _):
        for f, ref in ((G, ge), (H, he), (A, ae)):
            pack_strip(i, f, ref, own + i)
        x, m, g, h, a = (so[own + i - 1, f, 0] for f in range(5))
        ep[i, 0] = where(halo_e, x, where(halo_w, lroll(m, 124), lroll(g, 120)))
        ep[i, 1] = where(halo_e, h, lroll(a, 124))
        wp[i, 0] = where(halo_w, x, where(halo_e, lroll(m, 4), lroll(g, 124)))
        wp[i, 1] = where(halo_w, h, lroll(a, 4))
        return 0

    early = late_row == 0

    @pl.when(early)
    def _():
        lax.fori_loop(0, NL, strips_second, 0)

    def heard(when, count):
        @pl.when(when)
        def _():
            pl.semaphore_wait(bar, count)

    def tell():
        pl.semaphore_signal(told, inc=1, device_id={"lev": other}, device_id_type=MESH)

    heard(at_fold, 13)

    @pl.when((lev == 0) & north_in)
    def _():
        heard(early, 11)
        heard(jnp.logical_not(early), 7)
        tell()

    @pl.when((lev == 1) & north_in)
    def _():
        pl.semaphore_wait(told, 1)

    def send(k, src, dst, **where):
        return pltpu.make_async_remote_copy(
            src_ref=src, dst_ref=dst, send_sem=ssem.at[k], recv_sem=rsem.at[k],
            device_id=where, device_id_type=MESH,
        )

    mine = pl.ds(NL * lev, NL)
    two = pl.ds(0, 2)
    up, down = jnp.minimum(lat + 1, LAT - 1), jnp.maximum(lat - 1, 0)
    to_south = [
        send(0, tn1, na.at[mine, two], lat=down),
        send(1, tn2, nb.at[mine, two], lat=down),
        send(2, dn, dne, lat=down, lon=west),
        send(3, dn, dnw, lat=down, lon=east),
    ]
    to_north = [
        send(4, ts1, sa.at[mine, two], lat=up),
        send(5, ts2, sb.at[mine, two], lat=up),
        send(6, ds, dse, lat=up, lon=west),
        send(7, ds, dsw, lat=up, lon=east),
    ]
    to_side = [
        send(8, ep, em.at[mine], lon=west),
        send(9, wp, wm.at[mine], lon=east),
    ]

    def fold_copy(half, n, src, dst, **where):
        return pltpu.make_async_remote_copy(
            src_ref=src, dst_ref=dst, send_sem=fsem_s.at[half, n], recv_sem=fsem_r.at[half, n],
            device_id=where, device_id_type=MESH,
        )

    def block(half, owner):
        return (fa, fb)[half].at[pl.ds(2 * owner, 2)]

    def fold_out(half, n):
        passed = (ga, gb)[half]
        if n == 0:
            return fold_copy(half, n, block(half, lon), passed, lon=beside(lon), lev=other)
        if n < 4:
            return fold_copy(half, n, block(half, lon), block(half, lon), lon=lax.rem(lon + 2 * n, LON))
        to = block(half, beside(lon))
        if n < 7:
            return fold_copy(half, n, passed, to, lon=lax.rem(lon + 2 * n - 6, LON), lev=other)
        return fold_copy(half, n, passed, to, lev=other)

    def fold_in(half, n):
        if n == 0:
            part = (ga, gb)[half]
        elif n < 4:
            part = block(half, lax.rem(lon + LON - 2 * n, LON))
        else:
            part = block(half, beside(lax.rem(lon + LON + 6 - 2 * n, LON)) if n < 7 else beside(lon))
        fold_copy(half, n, part, part, lev=other).wait_recv()

    to_fold = [[fold_out(half, n) for n in range(8)] for half in range(2)]

    def planes(ref, start, count):
        return ref.at[pl.ds(start, count)]

    def share(k, ref, start, count):
        part = planes(ref, start, count)
        return send(k, part, part, lev=other)

    @pl.when(at_fold)
    def _():
        for half in to_fold:
            half[0].start()
        for half in to_fold:
            for c in half[1:4]:
                c.start()

    @pl.when(north_in)
    def _():
        for k in (2, 3, 0, 1):
            to_north[k].start()

    @pl.when(early)
    def _():
        for c in to_side:
            c.start()

    to_core = [
        share(10, xe, own, NL),
        send(11, mp, mr, lev=other),
        share(12, ge, 2 + 3 * lev, 3),
        share(13, he, 3 + 2 * lev, 2),
        share(14, ae, 4 + lev, 1),
        share(15, so, NL * lev, NL),
    ]
    for c in to_core[:5]:
        c.start()

    @pl.when(jnp.logical_not(early))
    def _():
        lax.fori_loop(0, NL, strips_second, 0)

    to_core[5].start()

    def to_others():
        @pl.when((lev == 0) & north_in)
        def _():
            pl.semaphore_wait(told, 1)

        @pl.when((lev == 1) & north_in)
        def _():
            heard(jnp.logical_not(early), 11)
            heard(early & south_in, 7)
            heard(lat == 0, 1)
            tell()

        @pl.when(south_in)
        def _():
            for k in (2, 3, 0, 1):
                to_south[k].start()

    after = lax.rem(lat, LAT // 2) == 0
    pl.when(jnp.logical_not(after))(to_others)

    @pl.when(jnp.logical_not(early))
    def _():
        for c in to_side:
            c.start()

    def pair(ref, p, r):
        sl = pl.ds(8 * r, 8)
        return [ref[p, lt, sl, :] for lt in range(2)]

    def shifted(ref, p, r, d):
        if 0 <= 8 * r + d <= ROWS - 8:
            return [ref[p, lt, pl.ds(8 * r + d, 8), :] for lt in range(2)]
        return [sroll(t, -d % 8) for t in pair(ref, p, r)]

    def east_of(v):
        r0, r1 = lroll(v[0], 127), lroll(v[1], 127)
        return [where(lane == 127, r1, r0), r1]

    def west_of(v):
        r0, r1 = lroll(v[0], 1), lroll(v[1], 1)
        return [r0, where(lane == 0, r0, r1)]

    def relu(v):
        return jnp.maximum(v, 0.0)

    def weights(p, face):
        for r in range(RT):
            sl = pl.ds(8 * r, 8)
            here, n = pair(me, p, r), shifted(me, p, r, 1)
            e = east_of(here)
            w = [relu(here[k] + e[k]) for k in range(2)]
            v = west_of(w)
            hi, lo = pair(me, face, r), pair(me, face - 1, r)
            for k in range(2):
                we[p, k, sl, :] = w[k]
                ww[p, k, sl, :] = v[k]
                wy[p, k, sl, :] = relu(here[k] + n[k])
                wz[face, k, sl, :] = relu(0.5 * (hi[k] + lo[k]))

    def inner(u, p, count, finish):
        for r in range(RT):
            stack = [pair(u, p + j, r) for j in range(-1, count + 1)]
            fz = [
                [w * (hi - lo) for w, lo, hi in zip(pair(wz, p + j, r), stack[j], stack[j + 1])]
                for j in range(count + 1)
            ]
            for j in range(count):
                here, q = stack[j + 1], p + j
                n, s = shifted(u, q, r, 1), shifted(u, q, r, -1)
                wn, ws = pair(wy, q, r), shifted(wy, q, r, -1)
                e, w, v, wv = east_of(here), pair(we, q, r), west_of(here), pair(ww, q, r)
                for k in range(2):
                    total = (
                        (w[k] * (e[k] - here[k]) - wv[k] * (here[k] - v[k]))
                        + (wn[k] * (n[k] - here[k]) - ws[k] * (here[k] - s[k]))
                        + (fz[j + 1][k] - fz[j][k])
                    )
                    finish(q, pl.ds(8 * r, 8), k, total)

    def finish1(p, sl, k, total):
        ke[p, k, sl, :] = ge[p, k, sl, :] + 0.5 * total

    def finish2(p, sl, k, total):
        x1[p, k, sl, :] = he[p, k, sl, :] + total

    def finish3(p, sl, k, total):
        k2[p, k, sl, :] = (x1[p, k, sl, :] + ae[p, k, sl, :]) + 0.5 * total

    def finish4(p, sl, k, total):
        j = p - own
        out[j, sl, pl.ds(128 * k, 128)] = (x1[p, k, sl, :] + qe[j, k, sl, :]) + total

    far, near = 1 + 5 * lev, 4 - 2 * lev
    next_own, next_faces = 2 + 3 * other, 5 - 3 * lev

    def own_weights(j, _):
        weights(own + j, far + j)
        return 0

    def other_weights(j, _):
        weights(theirs + j, next_faces + j)
        return 0

    lax.fori_loop(0, NL, own_weights, 0)
    inner(xe, far, 3, finish1)

    def copy_own(i, _):
        p = own + i
        for ref, to in ((xe, bx), (me, bm)):
            for lt in range(2):
                to[p, pl.ds(24 + 24 * lt, 8), :] = ref[p, lt, top, :]
                to[p, pl.ds(40 + 24 * lt, 8), :] = ref[p, lt, bottom, :]
        return 0

    lax.fori_loop(0, NL, copy_own, 0)

    @pl.when(at_fold)
    def _():
        for half in range(2):
            fold_in(half, 0)
            for c in to_fold[half][4:]:
                c.start()

    share(10, xe, theirs, NL).wait_recv()
    to_core[1].wait_recv()

    def close(i, _):
        p = theirs + i
        for r in range(RT):
            sl = pl.ds(8 * r, 8)
            for lt in range(2):
                me[p, lt, sl, :] = closed(mr[i, lt, sl, :])
        for ref, to in ((xe, bx), (me, bm)):
            for lt in range(2):
                to[p, pl.ds(24 + 24 * lt, 8), :] = ref[p, lt, top, :]
                to[p, pl.ds(40 + 24 * lt, 8), :] = ref[p, lt, bottom, :]
        return 0

    lax.fori_loop(0, NL, close, 0)
    lax.fori_loop(0, NL, other_weights, 0)
    share(12, ge, next_own, 3).wait_recv()
    inner(xe, near, 4, finish1)
    share(13, he, 3 + 2 * other, 2).wait_recv()

    def inner2(j, _):
        inner(ke, 1 + 2 * lev + 3 * j, 3, finish2)
        return 0

    lax.fori_loop(0, 2, inner2, 0)
    share(14, ae, 4 + other, 1).wait_recv()
    inner(x1, 1 + 3 * lev, 5, finish3)
    inner(k2, own, 4, finish4)
    share(15, so, NL * other, NL).wait_recv()

    pl.when(after)(to_others)

    for c in to_side + to_core:
        c.wait_send()

    @pl.when(south_in)
    def _():
        for c in to_south:
            c.wait_send()

    @pl.when(north_in)
    def _():
        for c in to_north:
            c.wait_send()

    @pl.when(at_fold)
    def _():
        for half in to_fold:
            for c in half:
                c.wait_send()

    relays = [
        share(16, em, NL * lev, NL),
        share(17, wm, NL * lev, NL),
        share(18, na, NL * lev, NL),
        share(19, sa, NL * lev, NL),
        share(20, nb, 1 + 3 * lev, 3),
        share(21, sb, 1 + 3 * lev, 3),
    ]
    to_side[0].wait_recv()
    relays[0].start()
    to_side[1].wait_recv()
    relays[1].start()

    def corners(w_ref, e_ref, at, one, half2):
        d = where((lane & 4) == 0, w_ref[...], e_ref[...])
        for i in range(NL):
            one[NL * lev + i, 2] = lroll(d, at - 16 * i)
            half2[NL * lev + i, 2] = lroll(d, at - 16 * i - 8)

    @pl.when(south_in)
    def _():
        for k in (0, 2, 3):
            to_north[k].wait_recv()
        corners(dsw, dse, 4, sa, sb)

    relays[3].start()

    c0 = (pc[0] - COLS * lon) & (LON * COLS - 1)
    t0, shift = c0 >> 7, c0 & 127

    def unfold(src, dst):
        for i in range(NL):
            t = [src[(t0 + k) & (2 * LON - 1), i] for k in (-3, -2, -1, 0, 1)]
            v = [
                pltpu.roll(where(lane >= 127 - shift, t[k + 1], t[k]), (shift + 1) & 127, 1)
                for k in range(4)
            ]
            dst[NL * lev + i, 0] = v[2]
            dst[NL * lev + i, 1] = v[1]
            dst[NL * lev + i, 2] = lroll(where(lo_half, v[0], v[3]), 116)

    def fold_arrived(half):
        for n in range(1, 8):
            fold_in(half, n)

    @pl.when(north_in)
    def _():
        for k in (0, 2, 3):
            to_south[k].wait_recv()
        corners(dnw, dne, 112, na, nb)

    @pl.when(at_fold)
    def _():
        fold_arrived(0)
        unfold(fa, na)

    relays[2].start()

    @pl.when(south_in)
    def _():
        to_north[1].wait_recv()

    relays[5].start()

    @pl.when(north_in)
    def _():
        to_south[1].wait_recv()
        relays[4].start()

    def ends(n, s):
        r = where(lo_half, lroll(both(s), 8), lroll(both(n), 116))
        c = where(lo_half, s[2], n[2])
        return where(halo_e, c, r), where(halo_w, c, r)

    def strip(l, f, v_e, v_w, from_e, from_w):
        return (
            where(ring_e, v_e, where(halo_e, from_e, so[l, f, 0])),
            where(ring_w, v_w, where(halo_w, from_w, so[l, f, 1])),
        )

    def slot(k, shift=0):
        return pl.ds((24, 32, 40, 48, 56, 64, 8, 80)[k] + shift, 8)

    def put(ref, p, tiles, which, turned=True):
        for k, t in zip(which, tiles):
            ref[p, slot(k), :] = t
            if turned and k >= 6:
                ref[p, slot(k, -8), :] = lroll(t, 12)
                ref[p, slot(k, 8), :] = lroll(t, 116)

    fresh = (1, 4, 6, 7)

    def place_first(l):
        p = l + 1
        n, s = [na[l, k] for k in range(3)], [sa[l, k] for k in range(3)]
        e1, w1 = em[l, 0], wm[l, 0]
        v = ends(n, s)
        x = [where(lo_sub, n[lt], s[lt]) for lt in range(2)]
        m = [sroll(where(lo_sub, s[lt], n[lt]), 4) for lt in range(2)]
        x += strip(l, X, v[0], v[1], e1, w1)
        m += strip(l, M, sroll(v[0], 4), sroll(v[1], 4), lroll(e1, 4), lroll(w1, 124))
        put(bx, p, x, fresh)
        put(bm, p, [closed(t) for t in m], fresh)

    def place_second(l):
        p = l + 1
        n, s = [nb[l, k] for k in range(3)], [sb[l, k] for k in range(3)]
        e1, w1, e2, w2 = em[l, 0], wm[l, 0], em[l, 1], wm[l, 1]
        v = ends(n, s)
        g = [where(lo_sub, n[lt], s[lt]) for lt in range(2)]
        h = [sroll(where(lo_sub, s[lt], n[lt]), 4) for lt in range(2)]
        a = [where(lo_sub, sroll(t, 5), sroll(t, 3)) for t in h]
        g += strip(l, G, v[0], v[1], lroll(e1, 8), lroll(w1, 4))
        hs = [sroll(t, 4) for t in v]
        h += strip(l, H, hs[0], hs[1], e2, w2)
        a_s = [where(lo_half, sroll(t, 3), sroll(t, 5)) for t in hs]
        a += strip(l, A, a_s[0], a_s[1], lroll(e2, 4), lroll(w2, 124))
        for k in range(4):
            bg[p, k], bh[p, k], ba[p, k] = g[k], h[k], a[k]

    def tiles(ref, p):
        return [ref[p, slot(k), :] for k in range(8)]

    def off(ref, p, d):
        return [ref[p, slot(k, d), :] for k in range(8)]

    def rim_of(full, part, p):
        return [
            full[p, 0, top, :], part[p, 0], full[p, 0, bottom, :],
            full[p, 1, top, :], part[p, 1], full[p, 1, bottom, :],
            part[p, 2], part[p, 3],
        ]

    def rim_east(v):
        r = [lroll(t, 127) for t in v]
        return [where(lane == 127, r[k + 3], r[k]) for k in range(3)] + r[3:]

    def rim_west(v):
        r = [lroll(t, 1) for t in v]
        return r[:3] + [where(lane == 0, r[k], r[k + 3]) for k in range(3)] + r[6:]

    every = range(8)

    def rim_weights(p):
        m, n = tiles(bm, p), off(bm, p, 1)
        put(vn, p, [relu(m[k] + n[k]) for k in every], every)
        b0, b1, t_e, t_w = (m[k] for k in fresh)
        w = east_of([b0, b1]) + [lroll(t_e, 127), lroll(t_w, 127)]
        w = [relu(m[k] + t) for k, t in zip(fresh, w)]
        v = west_of(w[:2]) + [lroll(t, 1) for t in w[2:]]
        for q in range(4):
            ve[p, q], vw[p, q] = w[q], v[q]

    def rim_faces(p):
        for q, k in enumerate(fresh):
            vz[p, q] = relu(0.5 * (bm[p, slot(k), :] + bm[p - 1, slot(k), :]))

    def rim(u, base, count, finish):
        stack = [tiles(u, base + j) for j in range(-1, count + 1)]

        def face(j):
            w = rim_of(wz, vz, base + j)
            return [w[k] * (stack[j + 1][k] - stack[j][k]) for k in every]

        fz = face(0)
        for j in range(count):
            p, here = base + j, stack[j + 1]
            fz_up = face(j + 1)
            e, w, n, s = rim_east(here), rim_west(here), off(u, p, 1), off(u, p, -1)
            we_, ww_ = rim_of(we, ve, p), rim_of(ww, vw, p)
            wn_, ws_ = tiles(vn, p), off(vn, p, -1)
            finish(
                p,
                [
                    (we_[k] * (e[k] - here[k]) - ww_[k] * (here[k] - w[k]))
                    + (wn_[k] * (n[k] - here[k]) - ws_[k] * (here[k] - s[k]))
                    + (fz_up[k] - fz[k])
                    for k in every
                ],
            )
            fz = fz_up

    def rim1(p, total):
        put(kr, p, [0.5 * t for t in total], every, False)

    def rim2(p, total):
        h = rim_of(he, bh, p)
        put(x1r, p, [h[k] + total[k] for k in every], every)

    def rim3(p, total):
        a, x = rim_of(ae, ba, p), tiles(x1r, p)
        put(k2r, p, [(x[k] + a[k]) + 0.5 * total[k] for k in every], every)

    def rim4(p, total):
        x = tiles(x1r, p)
        put(x2r, p, [x[k] + total[k] for k in every], every, False)

    def add_noise(p):
        g, k_ = rim_of(ge, bg, p), tiles(kr, p)
        put(kr, p, [g[k] + k_[k] for k in every], every)

    for i in range(NL):
        place_first(NL * lev + i)
    for i in range(NL):
        rim_weights(own + i)
    for i in range(NL):
        rim_faces(far + i)
    rim(bx, far, 3, rim1)

    @pl.when(at_fold)
    def _():
        fold_arrived(1)
        unfold(fb, nb)
        relays[4].start()

    for i in range(NL):
        place_second(NL * lev + i)
    for i in range(3):
        add_noise(far + i)
    rim(kr, 1 + 6 * lev, 2, rim2)
    rim(x1r, 1 + 7 * lev, 1, rim3)

    for k, ref in ((16, em), (17, wm), (18, na), (19, sa)):
        share(k, ref, NL * other, NL).wait_recv()
    for i in range(NL):
        place_first(NL * other + i)
    for i in range(3):
        rim_weights(next_own + i)
    for i in range(NL):
        rim_faces(next_faces + i)
    rim(bx, near, 4, rim1)
    share(20, nb, 1 + 3 * other, 3).wait_recv()
    share(21, sb, 1 + 3 * other, 3).wait_recv()
    for i in range(NL - 1):
        place_second(1 + 3 * other + i)
    for i in range(NL):
        add_noise(near + i)
    rim(kr, 3, 4, rim2)
    rim(x1r, 2 + 2 * lev, 4, rim3)
    rim(k2r, own, 4, rim4)

    for i in range(NL):
        t = tiles(x2r, own + i)
        edge = where(halo_w, t[6], t[7])
        for lt in range(2):
            cs = pl.ds(128 * lt, 128)
            pltpu.store(out.at[i, bottom, cs], t[3 * lt + 2] + qe[i, lt, bottom, :], mask=lo_sub)
            pltpu.store(out.at[i, top, cs], t[3 * lt] + qe[i, lt, top, :], mask=sub >= 4)
        for r in range(RT):
            sl = pl.ds(8 * r, 8)
            cols = lroll(edge, 128 - (12 * (r + 1) + 8))
            pltpu.store(out.at[i, sl, pl.ds(0, 128)], cols + qe[i, 0, sl, :], mask=lane < 4)
            pltpu.store(out.at[i, sl, pl.ds(128, 128)], cols + qe[i, 1, sl, :], mask=lane >= 124)

    for c in relays:
        c.wait_send()


def local(*args):
    def vm(*shape, dtype=f32):
        return pltpu.VMEM(shape, dtype)

    cells = (NL, ROWS, COLS)
    tile = (8, 128)
    planes = (10, 2, ROWS, 128)
    rim = (2 * NL, 3) + tile
    sides = (2 * NL, 2) + tile
    rows = (NL, 2) + tile
    return pl.pallas_call(
        kernel,
        out_shape=pltpu.VMEM(cells, f32),
        in_specs=[pl.BlockSpec(memory_space=pltpu.HBM)] * 7,
        out_specs=pl.BlockSpec(memory_space=pltpu.VMEM),
        scratch_shapes=[
            vm(*cells), vm(*cells), vm(*cells), vm(*cells, dtype=jnp.int32), vm(2, *cells), vm(2, *cells),
            pltpu.SMEM((LON * COLS,), jnp.int32),
        ]
        + [vm(*planes)] * 12
        + [vm(NL, 2, ROWS, 128)] * 3
        + [vm(2 * NL, 5, 2, *tile)]
        + [vm(10, 96, 128)] * 7
        + [vm(10, 4, *tile)] * 6
        + [vm(*rim)] * 4
        + [vm(*sides)] * 2
        + [vm(*tile)] * 4
        + [vm(2 * LON, NL, *tile)] * 2
        + [vm(2, NL, *tile)] * 2
        + [vm(*rows)] * 4
        + [vm(*rows)] * 2
        + [vm(*tile)] * 2
        + [
            pltpu.SemaphoreType.DMA((7,)),
            pltpu.SemaphoreType.DMA((22,)),
            pltpu.SemaphoreType.DMA((22,)),
            pltpu.SemaphoreType.DMA((2, 8)),
            pltpu.SemaphoreType.DMA((2, 8)),
            pltpu.SemaphoreType.REGULAR,
        ],
        compiler_params=pltpu.CompilerParams(
            collective_id=0, has_side_effects=True, vmem_limit_bytes=VMEM
        ),
        name="ocean",
    )(*(pltpu.with_memory_space_constraint(v, pltpu.HBM) for v in args))


def solution(mesh):
    block = P("lev", "lat", "lon")
    steps = P(None, "lev", "lat", "lon")
    return jax.shard_map(
        local,
        mesh=mesh,
        in_specs=(block, block, block, steps, steps, block, P()),
        out_specs=block,
        check_vma=False,
    )
```

```python
import jax
import jax.numpy as jnp
from jax import lax
from jax.experimental import pallas as pl
from jax.experimental.pallas import tpu as pltpu
from jax.sharding import PartitionSpec as P


LAT, LON, LEV = 16, 8, 2
NL, ROWS, COLS = 4, 64, 256
RT = ROWS // 8
VMEM = 60 * 1024 * 1024
MESH = pl.DeviceIdType.MESH
f32 = jnp.float32
X, M, G, H, A = range(5)


def kernel(
    tracer, diff, amp, noise_w, noise_z, land, partner, out,
    rx, rd, ra, rl, rw, rz, pc,
    xe, me, ge, he, ae, ke, x1, k2, we, ww, wy, wz, mp, mr, qe, so,
    bx, bm, vn, kr, x1r, k2r, x2r, bg, bh, ba, ve, vw, vz,
    na, sa, nb, sb, em, wm, dne, dnw, dse, dsw, fa, fb, ga, gb,
    tn1, ts1, tn2, ts2, ep, wp, dn, ds,
    isem, ssem, rsem, fsem_s, fsem_r, told,
):
    lat, lon, lev = lax.axis_index("lat"), lax.axis_index("lon"), lax.axis_index("lev")
    east, west = lax.rem(lon + 1, LON), lax.rem(lon + LON - 1, LON)
    other = 1 - lev
    north_in, south_in = lat < LAT - 1, lat > 0
    at_fold = lat == LAT - 1
    own, theirs = NL * lev + 1, NL * other + 1

    def beside(i):
        return i + 1 - 2 * lax.rem(i, 2)

    bar = pltpu.get_barrier_semaphore()

    def greet(**where):
        pl.semaphore_signal(bar, inc=1, device_id=where, device_id_type=MESH)

    late_row = lax.rem(lat, LAT // 2) // (LAT // 4)
    fold_row, below_fold = (lat + 1) // LAT, (lat + 2) // LAT

    @pl.when(north_in)
    def _():
        for k in (lon, east, west):
            greet(lat=lat + 1, lon=k, lev=1 - below_fold * other)

    greet(lev=other)
    for k in (east, west):
        greet(lon=k, lev=late_row - fold_row * other)

    @pl.when(at_fold)
    def _():
        greet(lon=beside(lon), lev=other)
        for k in (2, 4, 6):
            greet(lon=lax.rem(lon + k, LON))
            greet(lon=lax.rem(lon + k, LON), lev=other)

    @pl.when(south_in)
    def _():
        for k in (lon, east, west):
            greet(lat=lat - 1, lon=k, lev=0)

    loads = [
        pltpu.make_async_copy(s, d, isem.at[k])
        for k, (s, d) in enumerate(
            ((tracer, rx), (diff, rd), (land, rl), (amp, ra), (noise_z, rz), (noise_w, rw), (partner, pc))
        )
    ]
    for c in loads:
        c.start()

    lane = lax.broadcasted_iota(jnp.int32, (8, 128), 1)
    sub = lax.broadcasted_iota(jnp.int32, (8, 128), 0)
    lo_half, lo_sub = lane < 64, sub < 4
    group_e = (lane * 171) >> 11
    group_w = (((lane + 8) * 171) >> 11) - 1
    k12 = lane - 12 * group_e
    halo_e, halo_w = k12 >= 8, (k12 >= 4) & (k12 < 8)
    ring_e = (group_e == 0) | (group_e == RT + 1)
    ring_w = (group_w == 0) | (group_w == RT + 1)
    zero = jnp.zeros((8, 128), f32)
    where = jnp.where

    def lroll(v, s):
        s = s % 128
        return v if s == 0 else pltpu.roll(v, s, 1)

    def sroll(v, s):
        return pltpu.roll(v, s, 0)

    def closed(v):
        return where(v > 0, v, -1.0)

    def both(v):
        return where(lo_half, v[0], v[1])

    top, bottom = pl.ds(ROWS - 8, 8), pl.ds(0, 8)

    def rows_at(r):
        return pl.ds(pl.multiple_of(8 * r, 8), 8)

    for p in (0, 9):
        for r in range(RT + 4):
            sl = pl.ds(8 * r, 8)
            bm[p, sl, :] = zero - 1.0
            for ref in (bx, kr, x1r, k2r):
                ref[p, sl, :] = zero
        for r in range(RT):
            sl = pl.ds(8 * r, 8)
            for lt in range(2):
                me[p, lt, sl, :] = zero - 1.0
                for ref in (xe, ke, x1, k2):
                    ref[p, lt, sl, :] = zero

    @pl.when(lat == 0)
    def _():
        for i in range(NL):
            for lt in range(3):
                sa[NL * lev + i, lt] = zero
                sb[NL * lev + i, lt] = zero

    last, last2 = 7 - 7 * lev, 6 - 5 * lev
    for lt in range(3):
        na[last, lt] = zero
        sa[last, lt] = zero
        nb[last2, lt] = zero
        sb[last2, lt] = zero
    for k in range(2):
        em[last, k] = zero
        wm[last, k] = zero

    for c in loads[:3]:
        c.wait()

    def prep_first(i, _):
        p = own + i
        for r in range(RT):
            sl = pl.ds(8 * r, 8)
            for lt in range(2):
                cs = pl.ds(128 * lt, 128)
                m = 0.5 * rd[i, sl, cs] * rl[i, sl, cs].astype(f32)
                xe[p, lt, sl, :] = rx[i, sl, cs]
                mp[i, lt, sl, :] = m
                me[p, lt, sl, :] = closed(m)
        return 0

    lax.fori_loop(0, NL, prep_first, 0)

    def first_rows(x, m):
        return where(lo_sub, x, sroll(m, 4))

    def first_rows2(g, h, a):
        return where(lo_sub, g, where(sub == 7, sroll(a, 7), sroll(h, 4)))

    def last_rows(x, m):
        return where(lo_sub, sroll(m, 4), x)

    def last_rows2(g, h, a):
        return where(lo_sub, where(sub == 0, sroll(a, 1), sroll(h, 4)), g)

    def mirror_rows(v):
        for b in (1, 2, 4):
            v = where((sub & b) != 0, sroll(v, b), sroll(v, 8 - b))
        return v

    def mirror_lanes(v):
        return jnp.take_along_axis(v, 127 - lane, axis=1, mode="promise_in_bounds")

    for i in range(NL):
        for lt in range(2):
            tn1[i, lt] = first_rows(xe[own + i, lt, bottom, :], mp[i, lt, bottom, :])
            ts1[i, lt] = last_rows(xe[own + i, lt, top, :], mp[i, lt, top, :])

    @pl.when(at_fold)
    def _():
        for i in range(NL):
            for lt in range(2):
                x, m = mirror_rows(xe[own + i, lt, top, :]), mirror_rows(mp[i, lt, top, :])
                fa[2 * lon + lt, i] = mirror_lanes(first_rows(x, m))

    def pack_strip(i, f, ref, q):
        s_e, s_w = zero, zero
        for r in range(RT):
            sl = pl.ds(8 * r, 8)
            v = lroll(where(lo_half, ref[q, 0, sl, :], ref[q, 1, sl, :]), 12 * (r + 1) + 8)
            s_e = where(group_e == r + 1, v, s_e)
            s_w = where(group_w == r + 1, v, s_w)
        so[own + i - 1, f, 0] = s_e
        so[own + i - 1, f, 1] = s_w

    def strips_first(i, _):
        pack_strip(i, X, xe, own + i)
        pack_strip(i, M, mp, i)
        return 0

    lax.fori_loop(0, NL, strips_first, 0)

    for c in loads[3:]:
        c.wait()

    def prep_second(i, _):
        p = own + i
        for r in range(RT):
            sl = pl.ds(8 * r, 8)
            for lt in range(2):
                cs = pl.ds(128 * lt, 128)
                x = rx[i, sl, cs]
                amp_ = ra[i, sl, cs]
                ge[p, lt, sl, :] = x + amp_ * rz[0, i, sl, cs]
                he[p, lt, sl, :] = x + amp_ * rw[0, i, sl, cs]
                ae[p, lt, sl, :] = amp_ * rz[1, i, sl, cs]
                qe[i, lt, sl, :] = amp_ * rw[1, i, sl, cs]
        return 0

    lax.fori_loop(0, NL, prep_second, 0)
    for i in range(NL):
        p = own + i
        for lt in range(2):
            tn2[i, lt] = first_rows2(ge[p, lt, bottom, :], he[p, lt, bottom, :], ae[p, lt, bottom, :])
            ts2[i, lt] = last_rows2(ge[p, lt, top, :], he[p, lt, top, :], ae[p, lt, top, :])

    @pl.when(at_fold)
    def _():
        for i in range(NL):
            p = own + i
            for lt in range(2):
                g, h, a = (mirror_rows(ref[p, lt, top, :]) for ref in (ge, he, ae))
                fb[2 * lon + lt, i] = mirror_lanes(first_rows2(g, h, a))

    for halves, dst in (((tn1, tn2), dn), ((ts1, ts2), ds)):
        d = zero
        for i in range(NL):
            for n, half in enumerate(halves):
                k = 2 * i + n
                d = where((lane >> 3) == k, lroll(both(half[i]), 8 * k + 4), d)
        dst[...] = d

    def strips_second(i, _):
        for f, ref in ((G, ge), (H, he), (A, ae)):
            pack_strip(i, f, ref, own + i)
        x, m, g, h, a = (so[own + i - 1, f, 0] for f in range(5))
        ep[i, 0] = where(halo_e, x, where(halo_w, lroll(m, 124), lroll(g, 120)))
        ep[i, 1] = where(halo_e, h, lroll(a, 124))
        wp[i, 0] = where(halo_w, x, where(halo_e, lroll(m, 4), lroll(g, 124)))
        wp[i, 1] = where(halo_w, h, lroll(a, 4))
        return 0

    early = late_row == 0

    @pl.when(early)
    def _():
        lax.fori_loop(0, NL, strips_second, 0)

    def heard(when, count):
        @pl.when(when)
        def _():
            pl.semaphore_wait(bar, count)

    def tell():
        pl.semaphore_signal(told, inc=1, device_id={"lev": other}, device_id_type=MESH)

    heard(at_fold, 13)

    @pl.when((lev == 0) & north_in)
    def _():
        heard(early, 11)
        heard(jnp.logical_not(early), 7)
        tell()

    @pl.when((lev == 1) & north_in)
    def _():
        pl.semaphore_wait(told, 1)

    def send(k, src, dst, **where):
        return pltpu.make_async_remote_copy(
            src_ref=src, dst_ref=dst, send_sem=ssem.at[k], recv_sem=rsem.at[k],
            device_id=where, device_id_type=MESH,
        )

    mine = pl.ds(NL * lev, NL)
    two = pl.ds(0, 2)
    up, down = jnp.minimum(lat + 1, LAT - 1), jnp.maximum(lat - 1, 0)
    to_south = [
        send(0, tn1, na.at[mine, two], lat=down),
        send(1, tn2, nb.at[mine, two], lat=down),
        send(2, dn, dne, lat=down, lon=west),
        send(3, dn, dnw, lat=down, lon=east),
    ]
    to_north = [
        send(4, ts1, sa.at[mine, two], lat=up),
        send(5, ts2, sb.at[mine, two], lat=up),
        send(6, ds, dse, lat=up, lon=west),
        send(7, ds, dsw, lat=up, lon=east),
    ]
    to_side = [
        send(8, ep, em.at[mine], lon=west),
        send(9, wp, wm.at[mine], lon=east),
    ]

    def fold_copy(half, n, src, dst, **where):
        return pltpu.make_async_remote_copy(
            src_ref=src, dst_ref=dst, send_sem=fsem_s.at[half, n], recv_sem=fsem_r.at[half, n],
            device_id=where, device_id_type=MESH,
        )

    def block(half, owner):
        return (fa, fb)[half].at[pl.ds(2 * owner, 2)]

    def fold_out(half, n):
        passed = (ga, gb)[half]
        if n == 0:
            return fold_copy(half, n, block(half, lon), passed, lon=beside(lon), lev=other)
        if n < 4:
            return fold_copy(half, n, block(half, lon), block(half, lon), lon=lax.rem(lon + 2 * n, LON))
        to = block(half, beside(lon))
        if n < 7:
            return fold_copy(half, n, passed, to, lon=lax.rem(lon + 2 * n - 6, LON), lev=other)
        return fold_copy(half, n, passed, to, lev=other)

    def fold_in(half, n):
        if n == 0:
            part = (ga, gb)[half]
        elif n < 4:
            part = block(half, lax.rem(lon + LON - 2 * n, LON))
        else:
            part = block(half, beside(lax.rem(lon + LON + 6 - 2 * n, LON)) if n < 7 else beside(lon))
        fold_copy(half, n, part, part, lev=other).wait_recv()

    to_fold = [[fold_out(half, n) for n in range(8)] for half in range(2)]

    def planes(ref, start, count):
        return ref.at[pl.ds(start, count)]

    def share(k, ref, start, count):
        part = planes(ref, start, count)
        return send(k, part, part, lev=other)

    @pl.when(at_fold)
    def _():
        for half in to_fold:
            half[0].start()
        for half in to_fold:
            for c in half[1:4]:
                c.start()

    @pl.when(north_in)
    def _():
        for k in (2, 3, 0, 1):
            to_north[k].start()

    @pl.when(early)
    def _():
        for c in to_side:
            c.start()

    to_core = [
        share(10, xe, own, NL),
        send(11, mp, mr, lev=other),
        share(12, ge, 2 + 3 * lev, 3),
        share(13, he, 3 + 2 * lev, 2),
        share(14, ae, 4 + lev, 1),
        share(15, so, NL * lev, NL),
    ]
    for c in to_core[:5]:
        c.start()

    @pl.when(jnp.logical_not(early))
    def _():
        lax.fori_loop(0, NL, strips_second, 0)

    to_core[5].start()

    def to_others():
        @pl.when((lev == 0) & north_in)
        def _():
            pl.semaphore_wait(told, 1)

        @pl.when((lev == 1) & north_in)
        def _():
            heard(jnp.logical_not(early), 11)
            heard(early & south_in, 7)
            heard(lat == 0, 1)
            tell()

        @pl.when(south_in)
        def _():
            for k in (2, 3, 0, 1):
                to_south[k].start()

    after = lax.rem(lat, LAT // 2) == 0
    pl.when(jnp.logical_not(after))(to_others)

    @pl.when(jnp.logical_not(early))
    def _():
        for c in to_side:
            c.start()

    def pair(ref, p, r):
        sl = pl.ds(8 * r, 8)
        return [ref[p, lt, sl, :] for lt in range(2)]

    def shifted(ref, p, r, d):
        if 0 <= 8 * r + d <= ROWS - 8:
            return [ref[p, lt, pl.ds(8 * r + d, 8), :] for lt in range(2)]
        return [sroll(t, -d % 8) for t in pair(ref, p, r)]

    def east_of(v):
        r0, r1 = lroll(v[0], 127), lroll(v[1], 127)
        return [where(lane == 127, r1, r0), r1]

    def west_of(v):
        r0, r1 = lroll(v[0], 1), lroll(v[1], 1)
        return [r0, where(lane == 0, r0, r1)]

    def relu(v):
        return jnp.maximum(v, 0.0)

    def weights(p, face):
        for r in range(RT):
            sl = pl.ds(8 * r, 8)
            here, n = pair(me, p, r), shifted(me, p, r, 1)
            e = east_of(here)
            w = [relu(here[k] + e[k]) for k in range(2)]
            v = west_of(w)
            hi, lo = pair(me, face, r), pair(me, face - 1, r)
            for k in range(2):
                we[p, k, sl, :] = w[k]
                ww[p, k, sl, :] = v[k]
                wy[p, k, sl, :] = relu(here[k] + n[k])
                wz[face, k, sl, :] = relu(0.5 * (hi[k] + lo[k]))

    def inner(u, p, count, finish):
        for r in range(RT):
            stack = [pair(u, p + j, r) for j in range(-1, count + 1)]
            fz = [
                [w * (hi - lo) for w, lo, hi in zip(pair(wz, p + j, r), stack[j], stack[j + 1])]
                for j in range(count + 1)
            ]
            for j in range(count):
                here, q = stack[j + 1], p + j
                n, s = shifted(u, q, r, 1), shifted(u, q, r, -1)
                wn, ws = pair(wy, q, r), shifted(wy, q, r, -1)
                e, w, v, wv = east_of(here), pair(we, q, r), west_of(here), pair(ww, q, r)
                for k in range(2):
                    total = (
                        (w[k] * (e[k] - here[k]) - wv[k] * (here[k] - v[k]))
                        + (wn[k] * (n[k] - here[k]) - ws[k] * (here[k] - s[k]))
                        + (fz[j + 1][k] - fz[j][k])
                    )
                    finish(q, pl.ds(8 * r, 8), k, total)

    def finish1(p, sl, k, total):
        ke[p, k, sl, :] = ge[p, k, sl, :] + 0.5 * total

    def finish2(p, sl, k, total):
        x1[p, k, sl, :] = he[p, k, sl, :] + total

    def finish3(p, sl, k, total):
        k2[p, k, sl, :] = (x1[p, k, sl, :] + ae[p, k, sl, :]) + 0.5 * total

    def finish4(p, sl, k, total):
        j = p - own
        out[j, sl, pl.ds(128 * k, 128)] = (x1[p, k, sl, :] + qe[j, k, sl, :]) + total

    far, near = 1 + 5 * lev, 4 - 2 * lev
    next_own, next_faces = 2 + 3 * other, 5 - 3 * lev

    def own_weights(j, _):
        weights(own + j, far + j)
        return 0

    def other_weights(j, _):
        weights(theirs + j, next_faces + j)
        return 0

    lax.fori_loop(0, NL, own_weights, 0)
    inner(xe, far, 3, finish1)

    def copy_own(i, _):
        p = own + i
        for ref, to in ((xe, bx), (me, bm)):
            for lt in range(2):
                to[p, pl.ds(24 + 24 * lt, 8), :] = ref[p, lt, top, :]
                to[p, pl.ds(40 + 24 * lt, 8), :] = ref[p, lt, bottom, :]
        return 0

    lax.fori_loop(0, NL, copy_own, 0)

    @pl.when(at_fold)
    def _():
        for half in range(2):
            fold_in(half, 0)
            for c in to_fold[half][4:]:
                c.start()

    share(10, xe, theirs, NL).wait_recv()
    to_core[1].wait_recv()

    def close(i, _):
        p = theirs + i
        for r in range(RT):
            sl = pl.ds(8 * r, 8)
            for lt in range(2):
                me[p, lt, sl, :] = closed(mr[i, lt, sl, :])
        for ref, to in ((xe, bx), (me, bm)):
            for lt in range(2):
                to[p, pl.ds(24 + 24 * lt, 8), :] = ref[p, lt, top, :]
                to[p, pl.ds(40 + 24 * lt, 8), :] = ref[p, lt, bottom, :]
        return 0

    lax.fori_loop(0, NL, close, 0)
    lax.fori_loop(0, NL, other_weights, 0)
    share(12, ge, next_own, 3).wait_recv()
    inner(xe, near, 4, finish1)
    share(13, he, 3 + 2 * other, 2).wait_recv()

    def inner2(j, _):
        inner(ke, 1 + 2 * lev + 3 * j, 3, finish2)
        return 0

    lax.fori_loop(0, 2, inner2, 0)
    share(14, ae, 4 + other, 1).wait_recv()
    inner(x1, 1 + 3 * lev, 5, finish3)
    inner(k2, own, 4, finish4)
    share(15, so, NL * other, NL).wait_recv()

    pl.when(after)(to_others)

    for c in to_side + to_core:
        c.wait_send()

    @pl.when(south_in)
    def _():
        for c in to_south:
            c.wait_send()

    @pl.when(north_in)
    def _():
        for c in to_north:
            c.wait_send()

    @pl.when(at_fold)
    def _():
        for half in to_fold:
            for c in half:
                c.wait_send()

    def next_levels(k, ref, l, count):
        piece = ref.at[pl.ds(NL * l + (1 - l) * (NL - count), count)]
        return send(k, piece, piece, lev=other)

    halos = ((16, em, 3), (17, wm, 3), (18, na, 3), (19, sa, 3), (20, nb, 2), (21, sb, 2))
    relays = [next_levels(k, ref, lev, count) for k, ref, count in halos]
    to_side[0].wait_recv()
    relays[0].start()
    to_side[1].wait_recv()
    relays[1].start()

    def corners(w_ref, e_ref, at, one, half2):
        d = where((lane & 4) == 0, w_ref[...], e_ref[...])
        for i in range(NL):
            one[NL * lev + i, 2] = lroll(d, at - 16 * i)
            half2[NL * lev + i, 2] = lroll(d, at - 16 * i - 8)

    c0 = (pc[0] - COLS * lon) & (LON * COLS - 1)
    t0, shift = c0 >> 7, c0 & 127

    def unfold(src, dst):
        for i in range(NL):
            t = [src[(t0 + k) & (2 * LON - 1), i] for k in (-3, -2, -1, 0, 1)]
            v = [
                pltpu.roll(where(lane >= 127 - shift, t[k + 1], t[k]), (shift + 1) & 127, 1)
                for k in range(4)
            ]
            dst[NL * lev + i, 0] = v[2]
            dst[NL * lev + i, 1] = v[1]
            dst[NL * lev + i, 2] = lroll(where(lo_half, v[0], v[3]), 116)

    def fold_arrived(half):
        for n in range(1, 8):
            fold_in(half, n)

    @pl.when(north_in)
    def _():
        for k in (0, 2, 3, 1):
            to_south[k].wait_recv()
        corners(dnw, dne, 112, na, nb)
        relays[2].start()
        relays[4].start()

    @pl.when(south_in)
    def _():
        for k in (0, 2, 3, 1):
            to_north[k].wait_recv()
        corners(dsw, dse, 4, sa, sb)

    relays[3].start()
    relays[5].start()

    @pl.when(at_fold)
    def _():
        fold_arrived(0)
        unfold(fa, na)
        relays[2].start()

    def ends(n, s):
        r = where(lo_half, lroll(both(s), 8), lroll(both(n), 116))
        c = where(lo_half, s[2], n[2])
        return where(halo_e, c, r), where(halo_w, c, r)

    def strip(l, f, v_e, v_w, from_e, from_w):
        return (
            where(ring_e, v_e, where(halo_e, from_e, so[l, f, 0])),
            where(ring_w, v_w, where(halo_w, from_w, so[l, f, 1])),
        )

    def slot(k, shift=0):
        return pl.ds((24, 32, 40, 48, 56, 64, 8, 80)[k] + shift, 8)

    def put(ref, p, tiles, which, turned=True):
        for k, t in zip(which, tiles):
            ref[p, slot(k), :] = t
            if turned and k >= 6:
                ref[p, slot(k, -8), :] = lroll(t, 12)
                ref[p, slot(k, 8), :] = lroll(t, 116)

    fresh = (1, 4, 6, 7)

    def place_first(l):
        p = l + 1
        n, s = [na[l, k] for k in range(3)], [sa[l, k] for k in range(3)]
        e1, w1 = em[l, 0], wm[l, 0]
        v = ends(n, s)
        x = [where(lo_sub, n[lt], s[lt]) for lt in range(2)]
        m = [sroll(where(lo_sub, s[lt], n[lt]), 4) for lt in range(2)]
        x += strip(l, X, v[0], v[1], e1, w1)
        m += strip(l, M, sroll(v[0], 4), sroll(v[1], 4), lroll(e1, 4), lroll(w1, 124))
        put(bx, p, x, fresh)
        put(bm, p, [closed(t) for t in m], fresh)

    def place_second(l):
        p = l + 1
        n, s = [nb[l, k] for k in range(3)], [sb[l, k] for k in range(3)]
        e1, w1, e2, w2 = em[l, 0], wm[l, 0], em[l, 1], wm[l, 1]
        v = ends(n, s)
        g = [where(lo_sub, n[lt], s[lt]) for lt in range(2)]
        h = [sroll(where(lo_sub, s[lt], n[lt]), 4) for lt in range(2)]
        a = [where(lo_sub, sroll(t, 5), sroll(t, 3)) for t in h]
        g += strip(l, G, v[0], v[1], lroll(e1, 8), lroll(w1, 4))
        hs = [sroll(t, 4) for t in v]
        h += strip(l, H, hs[0], hs[1], e2, w2)
        a_s = [where(lo_half, sroll(t, 3), sroll(t, 5)) for t in hs]
        a += strip(l, A, a_s[0], a_s[1], lroll(e2, 4), lroll(w2, 124))
        for k in range(4):
            bg[p, k], bh[p, k], ba[p, k] = g[k], h[k], a[k]

    def tiles(ref, p):
        return [ref[p, slot(k), :] for k in range(8)]

    def off(ref, p, d):
        return [ref[p, slot(k, d), :] for k in range(8)]

    def rim_of(full, part, p):
        return [
            full[p, 0, top, :], part[p, 0], full[p, 0, bottom, :],
            full[p, 1, top, :], part[p, 1], full[p, 1, bottom, :],
            part[p, 2], part[p, 3],
        ]

    def rim_east(v):
        r = [lroll(t, 127) for t in v]
        return [where(lane == 127, r[k + 3], r[k]) for k in range(3)] + r[3:]

    def rim_west(v):
        r = [lroll(t, 1) for t in v]
        return r[:3] + [where(lane == 0, r[k], r[k + 3]) for k in range(3)] + r[6:]

    every = range(8)

    def rim_weights(p):
        m, n = tiles(bm, p), off(bm, p, 1)
        put(vn, p, [relu(m[k] + n[k]) for k in every], every)
        b0, b1, t_e, t_w = (m[k] for k in fresh)
        w = east_of([b0, b1]) + [lroll(t_e, 127), lroll(t_w, 127)]
        w = [relu(m[k] + t) for k, t in zip(fresh, w)]
        v = west_of(w[:2]) + [lroll(t, 1) for t in w[2:]]
        for q in range(4):
            ve[p, q], vw[p, q] = w[q], v[q]

    def rim_faces(p):
        for q, k in enumerate(fresh):
            vz[p, q] = relu(0.5 * (bm[p, slot(k), :] + bm[p - 1, slot(k), :]))

    def mixed(full, part, p, k):
        if k in fresh:
            return part[p, fresh.index(k)]
        return full[p, k // 3, top if k % 3 == 0 else bottom, :]

    def rim(u, base, count, finish):
        for group in ((0, 3), (1, 4), (2, 5), (6,), (7,)):
            pairs = len(group) == 2
            stack = [[u[base + j, slot(k), :] for k in group] for j in range(-1, count + 1)]
            faces = [
                [mixed(wz, vz, base + j, k) * (hi - lo) for k, lo, hi in zip(group, stack[j], stack[j + 1])]
                for j in range(count + 1)
            ]
            for j in range(count):
                p, here = base + j, stack[j + 1]
                e = east_of(here) if pairs else [lroll(here[0], 127)]
                w = west_of(here) if pairs else [lroll(here[0], 1)]
                for q, k in enumerate(group):
                    c = here[q]
                    total = (
                        (mixed(we, ve, p, k) * (e[q] - c) - mixed(ww, vw, p, k) * (c - w[q]))
                        + (vn[p, slot(k), :] * (u[p, slot(k, 1), :] - c) - vn[p, slot(k, -1), :] * (c - u[p, slot(k, -1), :]))
                        + (faces[j + 1][q] - faces[j][q])
                    )
                    finish(p, k, total)

    def rim1(p, k, total):
        put(kr, p, [0.5 * total], (k,), False)

    def rim2(p, k, total):
        put(x1r, p, [mixed(he, bh, p, k) + total], (k,))

    def rim3(p, k, total):
        put(k2r, p, [(x1r[p, slot(k), :] + mixed(ae, ba, p, k)) + 0.5 * total], (k,))

    def rim4(p, k, total):
        if k not in (1, 4):
            put(x2r, p, [x1r[p, slot(k), :] + total], (k,), False)

    def add_noise(p):
        put(kr, p, [mixed(ge, bg, p, k) + kr[p, slot(k), :] for k in every], every)

    for i in range(NL):
        place_first(NL * lev + i)
    for i in range(NL):
        rim_weights(own + i)
    for i in range(NL):
        rim_faces(far + i)
    rim(bx, far, 3, rim1)

    @pl.when(at_fold)
    def _():
        fold_arrived(1)
        unfold(fb, nb)
        relays[4].start()

    for i in range(NL):
        place_second(NL * lev + i)
    for i in range(3):
        add_noise(far + i)
    rim(kr, 1 + 6 * lev, 2, rim2)
    rim(x1r, 1 + 7 * lev, 1, rim3)

    for k, ref, count in halos[:4]:
        next_levels(k, ref, other, count).wait_recv()
    for i in range(NL):
        place_first(NL * other + i)
    for i in range(3):
        rim_weights(next_own + i)
    for i in range(NL):
        rim_faces(next_faces + i)
    rim(bx, near, 4, rim1)
    for k, ref, count in halos[4:]:
        next_levels(k, ref, other, count).wait_recv()
    for i in range(NL - 1):
        place_second(1 + 3 * other + i)
    for i in range(NL):
        add_noise(near + i)
    rim(kr, 3, 4, rim2)
    rim(x1r, 2 + 2 * lev, 4, rim3)
    rim(k2r, own, 4, rim4)

    for i in range(NL):
        t = {k: x2r[own + i, slot(k), :] for k in (0, 2, 3, 5, 6, 7)}
        edge = where(halo_w, t[6], t[7])
        for lt in range(2):
            cs = pl.ds(128 * lt, 128)
            pltpu.store(out.at[i, bottom, cs], t[3 * lt + 2] + qe[i, lt, bottom, :], mask=lo_sub)
            pltpu.store(out.at[i, top, cs], t[3 * lt] + qe[i, lt, top, :], mask=sub >= 4)
        for r in range(RT):
            sl = pl.ds(8 * r, 8)
            cols = lroll(edge, 128 - (12 * (r + 1) + 8))
            pltpu.store(out.at[i, sl, pl.ds(0, 128)], cols + qe[i, 0, sl, :], mask=lane < 4)
            pltpu.store(out.at[i, sl, pl.ds(128, 128)], cols + qe[i, 1, sl, :], mask=lane >= 124)

    for c in relays:
        c.wait_send()


def local(*args):
    def vm(*shape, dtype=f32):
        return pltpu.VMEM(shape, dtype)

    cells = (NL, ROWS, COLS)
    tile = (8, 128)
    planes = (10, 2, ROWS, 128)
    rim = (2 * NL, 3) + tile
    sides = (2 * NL, 2) + tile
    rows = (NL, 2) + tile
    return pl.pallas_call(
        kernel,
        out_shape=pltpu.VMEM(cells, f32),
        in_specs=[pl.BlockSpec(memory_space=pltpu.HBM)] * 7,
        out_specs=pl.BlockSpec(memory_space=pltpu.VMEM),
        scratch_shapes=[
            vm(*cells), vm(*cells), vm(*cells), vm(*cells, dtype=jnp.int32), vm(2, *cells), vm(2, *cells),
            pltpu.SMEM((LON * COLS,), jnp.int32),
        ]
        + [vm(*planes)] * 12
        + [vm(NL, 2, ROWS, 128)] * 3
        + [vm(2 * NL, 5, 2, *tile)]
        + [vm(10, 96, 128)] * 7
        + [vm(10, 4, *tile)] * 6
        + [vm(*rim)] * 4
        + [vm(*sides)] * 2
        + [vm(*tile)] * 4
        + [vm(2 * LON, NL, *tile)] * 2
        + [vm(2, NL, *tile)] * 2
        + [vm(*rows)] * 4
        + [vm(*rows)] * 2
        + [vm(*tile)] * 2
        + [
            pltpu.SemaphoreType.DMA((7,)),
            pltpu.SemaphoreType.DMA((22,)),
            pltpu.SemaphoreType.DMA((22,)),
            pltpu.SemaphoreType.DMA((2, 8)),
            pltpu.SemaphoreType.DMA((2, 8)),
            pltpu.SemaphoreType.REGULAR,
        ],
        compiler_params=pltpu.CompilerParams(
            collective_id=0, has_side_effects=True, vmem_limit_bytes=VMEM
        ),
        name="ocean",
    )(*(pltpu.with_memory_space_constraint(v, pltpu.HBM) for v in args))


def solution(mesh):
    block = P("lev", "lat", "lon")
    steps = P(None, "lev", "lat", "lon")
    return jax.shard_map(
        local,
        mesh=mesh,
        in_specs=(block, block, block, steps, steps, block, P()),
        out_specs=block,
        check_vma=False,
    )
```

```python
import jax
import jax.numpy as jnp
from jax import lax
from jax.experimental import pallas as pl
from jax.experimental.pallas import tpu as pltpu
from jax.sharding import PartitionSpec as P


LAT, LON, LEV = 16, 8, 2
NL, ROWS, COLS = 4, 64, 256
RT = ROWS // 8
VMEM = 60 * 1024 * 1024
MESH = pl.DeviceIdType.MESH
f32 = jnp.float32
X, M, G, H, A = range(5)


def kernel(
    tracer, diff, amp, noise_w, noise_z, land, partner, out,
    rx, rd, ra, rl, rw, rz, pc,
    xe, me, ge, he, ae, ke, x1, k2, we, ww, wy, wz, mp, mr, qe, so,
    bx, bm, vn, kr, x1r, k2r, x2r, bg, bh, ba, ve, vw, vz,
    na, sa, nb, sb, em, wm, dne, dnw, dse, dsw, fa, fb, ga, gb,
    tn1, ts1, tn2, ts2, ep, wp, dn, ds,
    isem, ssem, rsem, fsem_s, fsem_r, told,
):
    lat, lon, lev = lax.axis_index("lat"), lax.axis_index("lon"), lax.axis_index("lev")
    east, west = lax.rem(lon + 1, LON), lax.rem(lon + LON - 1, LON)
    other = 1 - lev
    north_in, south_in = lat < LAT - 1, lat > 0
    at_fold = lat == LAT - 1
    own, theirs = NL * lev + 1, NL * other + 1

    def beside(i):
        return i + 1 - 2 * lax.rem(i, 2)

    bar = pltpu.get_barrier_semaphore()

    def greet(**where):
        pl.semaphore_signal(bar, inc=1, device_id=where, device_id_type=MESH)

    late_row = lax.rem(lat, LAT // 2) // (LAT // 4)
    fold_row, below_fold = (lat + 1) // LAT, (lat + 2) // LAT

    @pl.when(north_in)
    def _():
        for k in (lon, east, west):
            greet(lat=lat + 1, lon=k, lev=1 - below_fold * other)

    greet(lev=other)
    for k in (east, west):
        greet(lon=k, lev=late_row - fold_row * other)

    @pl.when(at_fold)
    def _():
        greet(lon=beside(lon), lev=other)
        for k in (2, 4, 6):
            greet(lon=lax.rem(lon + k, LON))
            greet(lon=lax.rem(lon + k, LON), lev=other)

    @pl.when(south_in)
    def _():
        for k in (lon, east, west):
            greet(lat=lat - 1, lon=k, lev=0)

    loads = [
        pltpu.make_async_copy(s, d, isem.at[k])
        for k, (s, d) in enumerate(
            ((tracer, rx), (diff, rd), (land, rl), (amp, ra), (noise_z, rz), (noise_w, rw), (partner, pc))
        )
    ]
    for c in loads:
        c.start()

    lane = lax.broadcasted_iota(jnp.int32, (8, 128), 1)
    sub = lax.broadcasted_iota(jnp.int32, (8, 128), 0)
    lo_half, lo_sub = lane < 64, sub < 4
    group_e = (lane * 171) >> 11
    group_w = (((lane + 8) * 171) >> 11) - 1
    k12 = lane - 12 * group_e
    halo_e, halo_w = k12 >= 8, (k12 >= 4) & (k12 < 8)
    ring_e = (group_e == 0) | (group_e == RT + 1)
    ring_w = (group_w == 0) | (group_w == RT + 1)
    zero = jnp.zeros((8, 128), f32)
    where = jnp.where

    def lroll(v, s):
        s = s % 128
        return v if s == 0 else pltpu.roll(v, s, 1)

    def sroll(v, s):
        return pltpu.roll(v, s, 0)

    def closed(v):
        return where(v > 0, v, -1.0)

    def both(v):
        return where(lo_half, v[0], v[1])

    top, bottom = pl.ds(ROWS - 8, 8), pl.ds(0, 8)

    def rows_at(r):
        return pl.ds(pl.multiple_of(8 * r, 8), 8)

    for p in (0, 9):
        for r in range(RT + 4):
            sl = pl.ds(8 * r, 8)
            bm[p, sl, :] = zero - 1.0
            for ref in (bx, kr, x1r, k2r):
                ref[p, sl, :] = zero
        for r in range(RT):
            sl = pl.ds(8 * r, 8)
            for lt in range(2):
                me[p, lt, sl, :] = zero - 1.0
                for ref in (xe, ke, x1, k2):
                    ref[p, lt, sl, :] = zero

    @pl.when(lat == 0)
    def _():
        for i in range(NL):
            for lt in range(3):
                sa[NL * lev + i, lt] = zero
                sb[NL * lev + i, lt] = zero

    last, last2 = 7 - 7 * lev, 6 - 5 * lev
    for lt in range(3):
        na[last, lt] = zero
        sa[last, lt] = zero
        nb[last2, lt] = zero
        sb[last2, lt] = zero
    for k in range(2):
        em[last, k] = zero
        wm[last, k] = zero

    for c in loads[:3]:
        c.wait()

    def prep_first(i, _):
        p = own + i
        for r in range(RT):
            sl = pl.ds(8 * r, 8)
            for lt in range(2):
                cs = pl.ds(128 * lt, 128)
                m = 0.5 * rd[i, sl, cs] * rl[i, sl, cs].astype(f32)
                xe[p, lt, sl, :] = rx[i, sl, cs]
                mp[i, lt, sl, :] = m
                me[p, lt, sl, :] = closed(m)
        return 0

    lax.fori_loop(0, NL, prep_first, 0)

    def first_rows(x, m):
        return where(lo_sub, x, sroll(m, 4))

    def first_rows2(g, h, a):
        return where(lo_sub, g, where(sub == 7, sroll(a, 7), sroll(h, 4)))

    def last_rows(x, m):
        return where(lo_sub, sroll(m, 4), x)

    def last_rows2(g, h, a):
        return where(lo_sub, where(sub == 0, sroll(a, 1), sroll(h, 4)), g)

    def mirror_rows(v):
        for b in (1, 2, 4):
            v = where((sub & b) != 0, sroll(v, b), sroll(v, 8 - b))
        return v

    def mirror_lanes(v):
        return jnp.take_along_axis(v, 127 - lane, axis=1, mode="promise_in_bounds")

    for i in range(NL):
        for lt in range(2):
            tn1[i, lt] = first_rows(xe[own + i, lt, bottom, :], mp[i, lt, bottom, :])
            ts1[i, lt] = last_rows(xe[own + i, lt, top, :], mp[i, lt, top, :])

    @pl.when(at_fold)
    def _():
        for i in range(NL):
            for lt in range(2):
                x, m = mirror_rows(xe[own + i, lt, top, :]), mirror_rows(mp[i, lt, top, :])
                fa[2 * lon + lt, i] = mirror_lanes(first_rows(x, m))

    def pack_strip(i, f, ref, q):
        s_e, s_w = zero, zero
        for r in range(RT):
            sl = pl.ds(8 * r, 8)
            v = lroll(where(lo_half, ref[q, 0, sl, :], ref[q, 1, sl, :]), 12 * (r + 1) + 8)
            s_e = where(group_e == r + 1, v, s_e)
            s_w = where(group_w == r + 1, v, s_w)
        so[own + i - 1, f, 0] = s_e
        so[own + i - 1, f, 1] = s_w

    def strips_first(i, _):
        pack_strip(i, X, xe, own + i)
        pack_strip(i, M, mp, i)
        return 0

    lax.fori_loop(0, NL, strips_first, 0)

    for c in loads[3:]:
        c.wait()

    def prep_second(i, _):
        p = own + i
        for r in range(RT):
            sl = pl.ds(8 * r, 8)
            for lt in range(2):
                cs = pl.ds(128 * lt, 128)
                x = rx[i, sl, cs]
                amp_ = ra[i, sl, cs]
                ge[p, lt, sl, :] = x + amp_ * rz[0, i, sl, cs]
                he[p, lt, sl, :] = x + amp_ * rw[0, i, sl, cs]
                ae[p, lt, sl, :] = amp_ * rz[1, i, sl, cs]
                qe[i, lt, sl, :] = amp_ * rw[1, i, sl, cs]
        return 0

    lax.fori_loop(0, NL, prep_second, 0)
    for i in range(NL):
        p = own + i
        for lt in range(2):
            tn2[i, lt] = first_rows2(ge[p, lt, bottom, :], he[p, lt, bottom, :], ae[p, lt, bottom, :])
            ts2[i, lt] = last_rows2(ge[p, lt, top, :], he[p, lt, top, :], ae[p, lt, top, :])

    @pl.when(at_fold)
    def _():
        for i in range(NL):
            p = own + i
            for lt in range(2):
                g, h, a = (mirror_rows(ref[p, lt, top, :]) for ref in (ge, he, ae))
                fb[2 * lon + lt, i] = mirror_lanes(first_rows2(g, h, a))

    for halves, dst in (((tn1, tn2), dn), ((ts1, ts2), ds)):
        d = zero
        for i in range(NL):
            for n, half in enumerate(halves):
                k = 2 * i + n
                d = where((lane >> 3) == k, lroll(both(half[i]), 8 * k + 4), d)
        dst[...] = d

    def strips_second(i, _):
        for f, ref in ((G, ge), (H, he), (A, ae)):
            pack_strip(i, f, ref, own + i)
        x, m, g, h, a = (so[own + i - 1, f, 0] for f in range(5))
        ep[i, 0] = where(halo_e, x, where(halo_w, lroll(m, 124), lroll(g, 120)))
        ep[i, 1] = where(halo_e, h, lroll(a, 124))
        wp[i, 0] = where(halo_w, x, where(halo_e, lroll(m, 4), lroll(g, 124)))
        wp[i, 1] = where(halo_w, h, lroll(a, 4))
        return 0

    early = late_row == 0

    @pl.when(early)
    def _():
        lax.fori_loop(0, NL, strips_second, 0)

    def heard(when, count):
        @pl.when(when)
        def _():
            pl.semaphore_wait(bar, count)

    def tell():
        pl.semaphore_signal(told, inc=1, device_id={"lev": other}, device_id_type=MESH)

    heard(at_fold, 13)

    @pl.when((lev == 0) & north_in)
    def _():
        heard(early, 11)
        heard(jnp.logical_not(early), 7)
        tell()

    @pl.when((lev == 1) & north_in)
    def _():
        pl.semaphore_wait(told, 1)

    def send(k, src, dst, **where):
        return pltpu.make_async_remote_copy(
            src_ref=src, dst_ref=dst, send_sem=ssem.at[k], recv_sem=rsem.at[k],
            device_id=where, device_id_type=MESH,
        )

    mine = pl.ds(NL * lev, NL)
    two = pl.ds(0, 2)
    up, down = jnp.minimum(lat + 1, LAT - 1), jnp.maximum(lat - 1, 0)
    to_south = [
        send(0, tn1, na.at[mine, two], lat=down),
        send(1, tn2, nb.at[mine, two], lat=down),
        send(2, dn, dne, lat=down, lon=west),
        send(3, dn, dnw, lat=down, lon=east),
    ]
    to_north = [
        send(4, ts1, sa.at[mine, two], lat=up),
        send(5, ts2, sb.at[mine, two], lat=up),
        send(6, ds, dse, lat=up, lon=west),
        send(7, ds, dsw, lat=up, lon=east),
    ]
    to_side = [
        send(8, ep, em.at[mine], lon=west),
        send(9, wp, wm.at[mine], lon=east),
    ]

    def fold_copy(half, n, src, dst, **where):
        return pltpu.make_async_remote_copy(
            src_ref=src, dst_ref=dst, send_sem=fsem_s.at[half, n], recv_sem=fsem_r.at[half, n],
            device_id=where, device_id_type=MESH,
        )

    def block(half, owner):
        return (fa, fb)[half].at[pl.ds(2 * owner, 2)]

    def fold_out(half, n):
        passed = (ga, gb)[half]
        if n == 0:
            return fold_copy(half, n, block(half, lon), passed, lon=beside(lon), lev=other)
        if n < 4:
            return fold_copy(half, n, block(half, lon), block(half, lon), lon=lax.rem(lon + 2 * n, LON))
        to = block(half, beside(lon))
        if n < 7:
            return fold_copy(half, n, passed, to, lon=lax.rem(lon + 2 * n - 6, LON), lev=other)
        return fold_copy(half, n, passed, to, lev=other)

    def fold_in(half, n):
        if n == 0:
            part = (ga, gb)[half]
        elif n < 4:
            part = block(half, lax.rem(lon + LON - 2 * n, LON))
        else:
            part = block(half, beside(lax.rem(lon + LON + 6 - 2 * n, LON)) if n < 7 else beside(lon))
        fold_copy(half, n, part, part, lev=other).wait_recv()

    to_fold = [[fold_out(half, n) for n in range(8)] for half in range(2)]

    def planes(ref, start, count):
        return ref.at[pl.ds(start, count)]

    def share(k, ref, start, count):
        part = planes(ref, start, count)
        return send(k, part, part, lev=other)

    @pl.when(at_fold)
    def _():
        for half in to_fold:
            half[0].start()
        for half in to_fold:
            for n in (2, 1, 3):
                half[n].start()

    @pl.when(north_in)
    def _():
        for k in (2, 3, 0, 1):
            to_north[k].start()

    @pl.when(early)
    def _():
        for c in to_side:
            c.start()

    to_core = [
        share(10, xe, own, NL),
        send(11, mp, mr, lev=other),
        share(12, ge, 2 + 3 * lev, 3),
        share(13, he, 3 + 2 * lev, 2),
        share(14, ae, 4 + lev, 1),
        share(15, so, NL * lev, NL),
    ]
    for c in to_core[:5]:
        c.start()

    @pl.when(jnp.logical_not(early))
    def _():
        lax.fori_loop(0, NL, strips_second, 0)

    to_core[5].start()

    def to_others():
        @pl.when((lev == 0) & north_in)
        def _():
            pl.semaphore_wait(told, 1)

        @pl.when((lev == 1) & north_in)
        def _():
            heard(jnp.logical_not(early), 11)
            heard(early & south_in, 7)
            heard(lat == 0, 1)
            tell()

        @pl.when(south_in)
        def _():
            for k in (2, 3, 0, 1):
                to_south[k].start()

    after = lax.rem(lat, LAT // 2) == 0
    pl.when(jnp.logical_not(after))(to_others)

    @pl.when(jnp.logical_not(early))
    def _():
        for c in to_side:
            c.start()

    def pair(ref, p, r):
        sl = pl.ds(8 * r, 8)
        return [ref[p, lt, sl, :] for lt in range(2)]

    def shifted(ref, p, r, d):
        if 0 <= 8 * r + d <= ROWS - 8:
            return [ref[p, lt, pl.ds(8 * r + d, 8), :] for lt in range(2)]
        return [sroll(t, -d % 8) for t in pair(ref, p, r)]

    def east_of(v):
        r0, r1 = lroll(v[0], 127), lroll(v[1], 127)
        return [where(lane == 127, r1, r0), r1]

    def west_of(v):
        r0, r1 = lroll(v[0], 1), lroll(v[1], 1)
        return [r0, where(lane == 0, r0, r1)]

    def relu(v):
        return jnp.maximum(v, 0.0)

    def weights(p, face):
        for r in range(RT):
            sl = pl.ds(8 * r, 8)
            here, n = pair(me, p, r), shifted(me, p, r, 1)
            e = east_of(here)
            w = [relu(here[k] + e[k]) for k in range(2)]
            v = west_of(w)
            hi, lo = pair(me, face, r), pair(me, face - 1, r)
            for k in range(2):
                we[p, k, sl, :] = w[k]
                ww[p, k, sl, :] = v[k]
                wy[p, k, sl, :] = relu(here[k] + n[k])
                wz[face, k, sl, :] = relu(0.5 * (hi[k] + lo[k]))

    def inner(u, p, count, finish):
        for r in range(RT):
            stack = [pair(u, p + j, r) for j in range(-1, count + 1)]
            fz = [
                [w * (hi - lo) for w, lo, hi in zip(pair(wz, p + j, r), stack[j], stack[j + 1])]
                for j in range(count + 1)
            ]
            for j in range(count):
                here, q = stack[j + 1], p + j
                n, s = shifted(u, q, r, 1), shifted(u, q, r, -1)
                wn, ws = pair(wy, q, r), shifted(wy, q, r, -1)
                e, w, v, wv = east_of(here), pair(we, q, r), west_of(here), pair(ww, q, r)
                for k in range(2):
                    total = (
                        (w[k] * (e[k] - here[k]) - wv[k] * (here[k] - v[k]))
                        + (wn[k] * (n[k] - here[k]) - ws[k] * (here[k] - s[k]))
                        + (fz[j + 1][k] - fz[j][k])
                    )
                    finish(q, pl.ds(8 * r, 8), k, total)

    def finish1(p, sl, k, total):
        ke[p, k, sl, :] = ge[p, k, sl, :] + 0.5 * total

    def finish2(p, sl, k, total):
        x1[p, k, sl, :] = he[p, k, sl, :] + total

    def finish3(p, sl, k, total):
        k2[p, k, sl, :] = (x1[p, k, sl, :] + ae[p, k, sl, :]) + 0.5 * total

    def finish4(p, sl, k, total):
        j = p - own
        out[j, sl, pl.ds(128 * k, 128)] = (x1[p, k, sl, :] + qe[j, k, sl, :]) + total

    far, near = 1 + 5 * lev, 4 - 2 * lev
    next_own, next_faces = 2 + 3 * other, 5 - 3 * lev

    def own_weights(j, _):
        weights(own + j, far + j)
        return 0

    def other_weights(j, _):
        weights(theirs + j, next_faces + j)
        return 0

    lax.fori_loop(0, NL, own_weights, 0)
    inner(xe, far, 3, finish1)

    def copy_own(i, _):
        p = own + i
        for ref, to in ((xe, bx), (me, bm)):
            for lt in range(2):
                to[p, pl.ds(24 + 24 * lt, 8), :] = ref[p, lt, top, :]
                to[p, pl.ds(40 + 24 * lt, 8), :] = ref[p, lt, bottom, :]
        return 0

    lax.fori_loop(0, NL, copy_own, 0)

    @pl.when(at_fold)
    def _():
        for half in range(2):
            fold_in(half, 0)
            for n in (5, 4, 6, 7):
                to_fold[half][n].start()

    share(10, xe, theirs, NL).wait_recv()
    to_core[1].wait_recv()

    def close(i, _):
        p = theirs + i
        for r in range(RT):
            sl = pl.ds(8 * r, 8)
            for lt in range(2):
                me[p, lt, sl, :] = closed(mr[i, lt, sl, :])
        for ref, to in ((xe, bx), (me, bm)):
            for lt in range(2):
                to[p, pl.ds(24 + 24 * lt, 8), :] = ref[p, lt, top, :]
                to[p, pl.ds(40 + 24 * lt, 8), :] = ref[p, lt, bottom, :]
        return 0

    lax.fori_loop(0, NL, close, 0)
    lax.fori_loop(0, NL, other_weights, 0)
    share(12, ge, next_own, 3).wait_recv()
    inner(xe, near, 4, finish1)
    share(13, he, 3 + 2 * other, 2).wait_recv()

    def inner2(j, _):
        inner(ke, 1 + 2 * lev + 3 * j, 3, finish2)
        return 0

    lax.fori_loop(0, 2, inner2, 0)
    share(14, ae, 4 + other, 1).wait_recv()
    inner(x1, 1 + 3 * lev, 5, finish3)
    inner(k2, own, 4, finish4)
    share(15, so, NL * other, NL).wait_recv()

    pl.when(after)(to_others)

    for c in to_side + to_core:
        c.wait_send()

    @pl.when(south_in)
    def _():
        for c in to_south:
            c.wait_send()

    @pl.when(north_in)
    def _():
        for c in to_north:
            c.wait_send()

    @pl.when(at_fold)
    def _():
        for half in to_fold:
            for c in half:
                c.wait_send()

    def next_levels(k, ref, l, count):
        piece = ref.at[pl.ds(NL * l + (1 - l) * (NL - count), count)]
        return send(k, piece, piece, lev=other)

    halos = ((16, em, 3), (17, wm, 3), (18, na, 3), (19, sa, 3), (20, nb, 2), (21, sb, 2))
    relays = [next_levels(k, ref, lev, count) for k, ref, count in halos]
    to_side[0].wait_recv()
    relays[0].start()
    to_side[1].wait_recv()
    relays[1].start()

    def corners(w_ref, e_ref, at, one, half2):
        d = where((lane & 4) == 0, w_ref[...], e_ref[...])
        for i in range(NL):
            one[NL * lev + i, 2] = lroll(d, at - 16 * i)
            half2[NL * lev + i, 2] = lroll(d, at - 16 * i - 8)

    c0 = (pc[0] - COLS * lon) & (LON * COLS - 1)
    t0, shift = c0 >> 7, c0 & 127

    def unfold(src, dst):
        for i in range(NL):
            t = [src[(t0 + k) & (2 * LON - 1), i] for k in (-3, -2, -1, 0, 1)]
            v = [
                pltpu.roll(where(lane >= 127 - shift, t[k + 1], t[k]), (shift + 1) & 127, 1)
                for k in range(4)
            ]
            dst[NL * lev + i, 0] = v[2]
            dst[NL * lev + i, 1] = v[1]
            dst[NL * lev + i, 2] = lroll(where(lo_half, v[0], v[3]), 116)

    def fold_arrived(half):
        for n in range(1, 8):
            fold_in(half, n)

    @pl.when(north_in)
    def _():
        for k in (0, 2, 3, 1):
            to_south[k].wait_recv()
        corners(dnw, dne, 112, na, nb)
        relays[2].start()
        relays[4].start()

    @pl.when(south_in)
    def _():
        for k in (0, 2, 3, 1):
            to_north[k].wait_recv()
        corners(dsw, dse, 4, sa, sb)

    relays[3].start()
    relays[5].start()

    @pl.when(at_fold)
    def _():
        fold_arrived(0)
        unfold(fa, na)
        relays[2].start()

    def ends(n, s):
        r = where(lo_half, lroll(both(s), 8), lroll(both(n), 116))
        c = where(lo_half, s[2], n[2])
        return where(halo_e, c, r), where(halo_w, c, r)

    def strip(l, f, v_e, v_w, from_e, from_w):
        return (
            where(ring_e, v_e, where(halo_e, from_e, so[l, f, 0])),
            where(ring_w, v_w, where(halo_w, from_w, so[l, f, 1])),
        )

    def slot(k, shift=0):
        return pl.ds((24, 32, 40, 48, 56, 64, 8, 80)[k] + shift, 8)

    def put(ref, p, tiles, which, turned=True):
        for k, t in zip(which, tiles):
            ref[p, slot(k), :] = t
            if turned and k >= 6:
                ref[p, slot(k, -8), :] = lroll(t, 12)
                ref[p, slot(k, 8), :] = lroll(t, 116)

    fresh = (1, 4, 6, 7)

    def place_first(l):
        p = l + 1
        n, s = [na[l, k] for k in range(3)], [sa[l, k] for k in range(3)]
        e1, w1 = em[l, 0], wm[l, 0]
        v = ends(n, s)
        x = [where(lo_sub, n[lt], s[lt]) for lt in range(2)]
        m = [sroll(where(lo_sub, s[lt], n[lt]), 4) for lt in range(2)]
        x += strip(l, X, v[0], v[1], e1, w1)
        m += strip(l, M, sroll(v[0], 4), sroll(v[1], 4), lroll(e1, 4), lroll(w1, 124))
        put(bx, p, x, fresh)
        put(bm, p, [closed(t) for t in m], fresh)

    def place_second(l):
        p = l + 1
        n, s = [nb[l, k] for k in range(3)], [sb[l, k] for k in range(3)]
        e1, w1, e2, w2 = em[l, 0], wm[l, 0], em[l, 1], wm[l, 1]
        v = ends(n, s)
        g = [where(lo_sub, n[lt], s[lt]) for lt in range(2)]
        h = [sroll(where(lo_sub, s[lt], n[lt]), 4) for lt in range(2)]
        a = [where(lo_sub, sroll(t, 5), sroll(t, 3)) for t in h]
        g += strip(l, G, v[0], v[1], lroll(e1, 8), lroll(w1, 4))
        hs = [sroll(t, 4) for t in v]
        h += strip(l, H, hs[0], hs[1], e2, w2)
        a_s = [where(lo_half, sroll(t, 3), sroll(t, 5)) for t in hs]
        a += strip(l, A, a_s[0], a_s[1], lroll(e2, 4), lroll(w2, 124))
        for k in range(4):
            bg[p, k], bh[p, k], ba[p, k] = g[k], h[k], a[k]

    def tiles(ref, p):
        return [ref[p, slot(k), :] for k in range(8)]

    def off(ref, p, d):
        return [ref[p, slot(k, d), :] for k in range(8)]

    def rim_of(full, part, p):
        return [
            full[p, 0, top, :], part[p, 0], full[p, 0, bottom, :],
            full[p, 1, top, :], part[p, 1], full[p, 1, bottom, :],
            part[p, 2], part[p, 3],
        ]

    def rim_east(v):
        r = [lroll(t, 127) for t in v]
        return [where(lane == 127, r[k + 3], r[k]) for k in range(3)] + r[3:]

    def rim_west(v):
        r = [lroll(t, 1) for t in v]
        return r[:3] + [where(lane == 0, r[k], r[k + 3]) for k in range(3)] + r[6:]

    every = range(8)

    def rim_weights(p):
        m, n = tiles(bm, p), off(bm, p, 1)
        put(vn, p, [relu(m[k] + n[k]) for k in every], every)
        b0, b1, t_e, t_w = (m[k] for k in fresh)
        w = east_of([b0, b1]) + [lroll(t_e, 127), lroll(t_w, 127)]
        w = [relu(m[k] + t) for k, t in zip(fresh, w)]
        v = west_of(w[:2]) + [lroll(t, 1) for t in w[2:]]
        for q in range(4):
            ve[p, q], vw[p, q] = w[q], v[q]

    def rim_faces(p):
        for q, k in enumerate(fresh):
            vz[p, q] = relu(0.5 * (bm[p, slot(k), :] + bm[p - 1, slot(k), :]))

    def mixed(full, part, p, k):
        if k in fresh:
            return part[p, fresh.index(k)]
        return full[p, k // 3, top if k % 3 == 0 else bottom, :]

    def rim(u, base, count, finish):
        for group in ((0, 3), (1, 4), (2, 5), (6,), (7,)):
            pairs = len(group) == 2
            stack = [[u[base + j, slot(k), :] for k in group] for j in range(-1, count + 1)]
            faces = [
                [mixed(wz, vz, base + j, k) * (hi - lo) for k, lo, hi in zip(group, stack[j], stack[j + 1])]
                for j in range(count + 1)
            ]
            for j in range(count):
                p, here = base + j, stack[j + 1]
                e = east_of(here) if pairs else [lroll(here[0], 127)]
                w = west_of(here) if pairs else [lroll(here[0], 1)]
                for q, k in enumerate(group):
                    c = here[q]
                    total = (
                        (mixed(we, ve, p, k) * (e[q] - c) - mixed(ww, vw, p, k) * (c - w[q]))
                        + (vn[p, slot(k), :] * (u[p, slot(k, 1), :] - c) - vn[p, slot(k, -1), :] * (c - u[p, slot(k, -1), :]))
                        + (faces[j + 1][q] - faces[j][q])
                    )
                    finish(p, k, total)

    def rim1(p, k, total):
        put(kr, p, [0.5 * total], (k,), False)

    def rim2(p, k, total):
        put(x1r, p, [mixed(he, bh, p, k) + total], (k,))

    def rim3(p, k, total):
        put(k2r, p, [(x1r[p, slot(k), :] + mixed(ae, ba, p, k)) + 0.5 * total], (k,))

    def rim4(p, k, total):
        if k not in (1, 4):
            put(x2r, p, [x1r[p, slot(k), :] + total], (k,), False)

    def add_noise(p):
        put(kr, p, [mixed(ge, bg, p, k) + kr[p, slot(k), :] for k in every], every)

    for i in range(NL):
        place_first(NL * lev + i)
    for i in range(NL):
        rim_weights(own + i)
    for i in range(NL):
        rim_faces(far + i)
    rim(bx, far, 3, rim1)

    @pl.when(at_fold)
    def _():
        fold_arrived(1)
        unfold(fb, nb)
        relays[4].start()

    for i in range(NL):
        place_second(NL * lev + i)
    for i in range(3):
        add_noise(far + i)
    rim(kr, 1 + 6 * lev, 2, rim2)
    rim(x1r, 1 + 7 * lev, 1, rim3)

    for k, ref, count in halos[:4]:
        next_levels(k, ref, other, count).wait_recv()
    for i in range(NL):
        place_first(NL * other + i)
    for i in range(3):
        rim_weights(next_own + i)
    for i in range(NL):
        rim_faces(next_faces + i)
    rim(bx, near, 4, rim1)
    for k, ref, count in halos[4:]:
        next_levels(k, ref, other, count).wait_recv()
    for i in range(NL - 1):
        place_second(1 + 3 * other + i)
    for i in range(NL):
        add_noise(near + i)
    rim(kr, 3, 4, rim2)
    rim(x1r, 2 + 2 * lev, 4, rim3)
    rim(k2r, own, 4, rim4)

    for i in range(NL):
        t = {k: x2r[own + i, slot(k), :] for k in (0, 2, 3, 5, 6, 7)}
        edge = where(halo_w, t[6], t[7])
        for lt in range(2):
            cs = pl.ds(128 * lt, 128)
            pltpu.store(out.at[i, bottom, cs], t[3 * lt + 2] + qe[i, lt, bottom, :], mask=lo_sub)
            pltpu.store(out.at[i, top, cs], t[3 * lt] + qe[i, lt, top, :], mask=sub >= 4)
        for r in range(RT):
            sl = pl.ds(8 * r, 8)
            cols = lroll(edge, 128 - (12 * (r + 1) + 8))
            pltpu.store(out.at[i, sl, pl.ds(0, 128)], cols + qe[i, 0, sl, :], mask=lane < 4)
            pltpu.store(out.at[i, sl, pl.ds(128, 128)], cols + qe[i, 1, sl, :], mask=lane >= 124)

    for c in relays:
        c.wait_send()


def local(*args):
    def vm(*shape, dtype=f32):
        return pltpu.VMEM(shape, dtype)

    cells = (NL, ROWS, COLS)
    tile = (8, 128)
    planes = (10, 2, ROWS, 128)
    rim = (2 * NL, 3) + tile
    sides = (2 * NL, 2) + tile
    rows = (NL, 2) + tile
    return pl.pallas_call(
        kernel,
        out_shape=pltpu.VMEM(cells, f32),
        in_specs=[pl.BlockSpec(memory_space=pltpu.HBM)] * 7,
        out_specs=pl.BlockSpec(memory_space=pltpu.VMEM),
        scratch_shapes=[
            vm(*cells), vm(*cells), vm(*cells), vm(*cells, dtype=jnp.int32), vm(2, *cells), vm(2, *cells),
            pltpu.SMEM((LON * COLS,), jnp.int32),
        ]
        + [vm(*planes)] * 12
        + [vm(NL, 2, ROWS, 128)] * 3
        + [vm(2 * NL, 5, 2, *tile)]
        + [vm(10, 96, 128)] * 7
        + [vm(10, 4, *tile)] * 6
        + [vm(*rim)] * 4
        + [vm(*sides)] * 2
        + [vm(*tile)] * 4
        + [vm(2 * LON, NL, *tile)] * 2
        + [vm(2, NL, *tile)] * 2
        + [vm(*rows)] * 4
        + [vm(*rows)] * 2
        + [vm(*tile)] * 2
        + [
            pltpu.SemaphoreType.DMA((7,)),
            pltpu.SemaphoreType.DMA((22,)),
            pltpu.SemaphoreType.DMA((22,)),
            pltpu.SemaphoreType.DMA((2, 8)),
            pltpu.SemaphoreType.DMA((2, 8)),
            pltpu.SemaphoreType.REGULAR,
        ],
        compiler_params=pltpu.CompilerParams(
            collective_id=0, has_side_effects=True, vmem_limit_bytes=VMEM
        ),
        name="ocean",
    )(*(pltpu.with_memory_space_constraint(v, pltpu.HBM) for v in args))


def solution(mesh):
    block = P("lev", "lat", "lon")
    steps = P(None, "lev", "lat", "lon")
    return jax.shard_map(
        local,
        mesh=mesh,
        in_specs=(block, block, block, steps, steps, block, P()),
        out_specs=block,
        check_vma=False,
    )
```

```python
import jax
import jax.numpy as jnp
from jax import lax
from jax.experimental import pallas as pl
from jax.experimental.pallas import tpu as pltpu
from jax.sharding import PartitionSpec as P


LAT, LON, LEV = 16, 8, 2
NL, ROWS, COLS = 4, 64, 256
RT = ROWS // 8
VMEM = 60 * 1024 * 1024
MESH = pl.DeviceIdType.MESH
f32 = jnp.float32
X, M, G, H, A = range(5)


def kernel(
    tracer, diff, amp, noise_w, noise_z, land, partner, out,
    rx, rd, ra, rl, rw, rz, pc,
    xe, me, ge, he, ae, ke, x1, k2, we, ww, wy, wz, mp, mr, qe, so,
    bx, bm, vn, kr, x1r, k2r, x2r, bg, bh, ba, ve, vw, vz,
    na, sa, nb, sb, em, wm, dne, dnw, dse, dsw, fa, fb, ga, gb,
    tn1, ts1, tn2, ts2, ep, wp, dn, ds,
    isem, ssem, rsem, fsem_s, fsem_r, told,
):
    lat, lon, lev = lax.axis_index("lat"), lax.axis_index("lon"), lax.axis_index("lev")
    east, west = lax.rem(lon + 1, LON), lax.rem(lon + LON - 1, LON)
    other = 1 - lev
    north_in, south_in = lat < LAT - 1, lat > 0
    at_fold = lat == LAT - 1
    own, theirs = NL * lev + 1, NL * other + 1

    def beside(i):
        return i + 1 - 2 * lax.rem(i, 2)

    bar = pltpu.get_barrier_semaphore()

    def greet(**where):
        pl.semaphore_signal(bar, inc=1, device_id=where, device_id_type=MESH)

    late_row = lax.rem(lat, LAT // 2) // (LAT // 4)
    fold_row, below_fold = (lat + 1) // LAT, (lat + 2) // LAT

    @pl.when(north_in)
    def _():
        for k in (lon, east, west):
            greet(lat=lat + 1, lon=k, lev=1 - below_fold * other)

    greet(lev=other)
    for k in (east, west):
        greet(lon=k, lev=late_row - fold_row * other)

    @pl.when(at_fold)
    def _():
        greet(lon=beside(lon), lev=other)
        for k in (2, 4, 6):
            greet(lon=lax.rem(lon + k, LON))
            greet(lon=lax.rem(lon + k, LON), lev=other)

    @pl.when(south_in)
    def _():
        for k in (lon, east, west):
            greet(lat=lat - 1, lon=k, lev=0)

    loads = [
        pltpu.make_async_copy(s, d, isem.at[k])
        for k, (s, d) in enumerate(
            ((tracer, rx), (diff, rd), (land, rl), (amp, ra), (noise_z, rz), (noise_w, rw), (partner, pc))
        )
    ]
    for c in loads:
        c.start()

    lane = lax.broadcasted_iota(jnp.int32, (8, 128), 1)
    sub = lax.broadcasted_iota(jnp.int32, (8, 128), 0)
    lo_half, lo_sub = lane < 64, sub < 4
    group_e = (lane * 171) >> 11
    group_w = (((lane + 8) * 171) >> 11) - 1
    k12 = lane - 12 * group_e
    halo_e, halo_w = k12 >= 8, (k12 >= 4) & (k12 < 8)
    ring_e = (group_e == 0) | (group_e == RT + 1)
    ring_w = (group_w == 0) | (group_w == RT + 1)
    zero = jnp.zeros((8, 128), f32)
    where = jnp.where

    def lroll(v, s):
        s = s % 128
        return v if s == 0 else pltpu.roll(v, s, 1)

    def sroll(v, s):
        return pltpu.roll(v, s, 0)

    def closed(v):
        return where(v > 0, v, -1.0)

    def both(v):
        return where(lo_half, v[0], v[1])

    top, bottom = pl.ds(ROWS - 8, 8), pl.ds(0, 8)

    def rows_at(r):
        return pl.ds(pl.multiple_of(8 * r, 8), 8)

    for p in (0, 9):
        for r in range(RT + 4):
            sl = pl.ds(8 * r, 8)
            bm[p, sl, :] = zero - 1.0
            for ref in (bx, kr, x1r, k2r):
                ref[p, sl, :] = zero
        for r in range(RT):
            sl = pl.ds(8 * r, 8)
            for lt in range(2):
                me[p, lt, sl, :] = zero - 1.0
                for ref in (xe, ke, x1, k2):
                    ref[p, lt, sl, :] = zero

    @pl.when(lat == 0)
    def _():
        for i in range(NL):
            for lt in range(3):
                sa[NL * lev + i, lt] = zero
                sb[NL * lev + i, lt] = zero

    last, last2 = 7 - 7 * lev, 6 - 5 * lev
    for lt in range(3):
        na[last, lt] = zero
        sa[last, lt] = zero
        nb[last2, lt] = zero
        sb[last2, lt] = zero
    for k in range(2):
        em[last, k] = zero
        wm[last, k] = zero

    for c in loads[:3]:
        c.wait()

    def prep_first(i, _):
        p = own + i
        for r in range(RT):
            sl = pl.ds(8 * r, 8)
            for lt in range(2):
                cs = pl.ds(128 * lt, 128)
                m = 0.5 * rd[i, sl, cs] * rl[i, sl, cs].astype(f32)
                xe[p, lt, sl, :] = rx[i, sl, cs]
                mp[i, lt, sl, :] = m
                me[p, lt, sl, :] = closed(m)
        return 0

    lax.fori_loop(0, NL, prep_first, 0)

    def first_rows(x, m):
        return where(lo_sub, x, sroll(m, 4))

    def first_rows2(g, h, a):
        return where(lo_sub, g, where(sub == 7, sroll(a, 7), sroll(h, 4)))

    def last_rows(x, m):
        return where(lo_sub, sroll(m, 4), x)

    def last_rows2(g, h, a):
        return where(lo_sub, where(sub == 0, sroll(a, 1), sroll(h, 4)), g)

    def mirror_rows(v):
        for b in (1, 2, 4):
            v = where((sub & b) != 0, sroll(v, b), sroll(v, 8 - b))
        return v

    def mirror_lanes(v):
        return jnp.take_along_axis(v, 127 - lane, axis=1, mode="promise_in_bounds")

    for i in range(NL):
        for lt in range(2):
            tn1[i, lt] = first_rows(xe[own + i, lt, bottom, :], mp[i, lt, bottom, :])
            ts1[i, lt] = last_rows(xe[own + i, lt, top, :], mp[i, lt, top, :])

    @pl.when(at_fold)
    def _():
        for i in range(NL):
            for lt in range(2):
                x, m = mirror_rows(xe[own + i, lt, top, :]), mirror_rows(mp[i, lt, top, :])
                fa[2 * lon + lt, i] = mirror_lanes(first_rows(x, m))

    def pack_strip(i, f, ref, q):
        s_e, s_w = zero, zero
        for r in range(RT):
            sl = pl.ds(8 * r, 8)
            v = lroll(where(lo_half, ref[q, 0, sl, :], ref[q, 1, sl, :]), 12 * (r + 1) + 8)
            s_e = where(group_e == r + 1, v, s_e)
            s_w = where(group_w == r + 1, v, s_w)
        so[own + i - 1, f, 0] = s_e
        so[own + i - 1, f, 1] = s_w

    def strips_first(i, _):
        pack_strip(i, X, xe, own + i)
        pack_strip(i, M, mp, i)
        return 0

    lax.fori_loop(0, NL, strips_first, 0)

    for c in loads[3:]:
        c.wait()

    def prep_second(i, _):
        p = own + i
        for r in range(RT):
            sl = pl.ds(8 * r, 8)
            for lt in range(2):
                cs = pl.ds(128 * lt, 128)
                x = rx[i, sl, cs]
                amp_ = ra[i, sl, cs]
                ge[p, lt, sl, :] = x + amp_ * rz[0, i, sl, cs]
                he[p, lt, sl, :] = x + amp_ * rw[0, i, sl, cs]
                ae[p, lt, sl, :] = amp_ * rz[1, i, sl, cs]
                qe[i, lt, sl, :] = amp_ * rw[1, i, sl, cs]
        return 0

    lax.fori_loop(0, NL, prep_second, 0)
    for i in range(NL):
        p = own + i
        for lt in range(2):
            tn2[i, lt] = first_rows2(ge[p, lt, bottom, :], he[p, lt, bottom, :], ae[p, lt, bottom, :])
            ts2[i, lt] = last_rows2(ge[p, lt, top, :], he[p, lt, top, :], ae[p, lt, top, :])

    @pl.when(at_fold)
    def _():
        for i in range(NL):
            p = own + i
            for lt in range(2):
                g, h, a = (mirror_rows(ref[p, lt, top, :]) for ref in (ge, he, ae))
                fb[2 * lon + lt, i] = mirror_lanes(first_rows2(g, h, a))

    for halves, dst in (((tn1, tn2), dn), ((ts1, ts2), ds)):
        d = zero
        for i in range(NL):
            for n, half in enumerate(halves):
                k = 2 * i + n
                d = where((lane >> 3) == k, lroll(both(half[i]), 8 * k + 4), d)
        dst[...] = d

    def strips_second(i, _):
        for f, ref in ((G, ge), (H, he), (A, ae)):
            pack_strip(i, f, ref, own + i)
        x, m, g, h, a = (so[own + i - 1, f, 0] for f in range(5))
        ep[i, 0] = where(halo_e, x, where(halo_w, lroll(m, 124), lroll(g, 120)))
        ep[i, 1] = where(halo_e, h, lroll(a, 124))
        wp[i, 0] = where(halo_w, x, where(halo_e, lroll(m, 4), lroll(g, 124)))
        wp[i, 1] = where(halo_w, h, lroll(a, 4))
        return 0

    early = late_row == 0

    @pl.when(early)
    def _():
        lax.fori_loop(0, NL, strips_second, 0)

    def heard(when, count):
        @pl.when(when)
        def _():
            pl.semaphore_wait(bar, count)

    def tell():
        pl.semaphore_signal(told, inc=1, device_id={"lev": other}, device_id_type=MESH)

    heard(at_fold, 13)

    @pl.when((lev == 0) & north_in)
    def _():
        heard(early, 11)
        heard(jnp.logical_not(early), 7)
        tell()

    @pl.when((lev == 1) & north_in)
    def _():
        pl.semaphore_wait(told, 1)

    def send(k, src, dst, **where):
        return pltpu.make_async_remote_copy(
            src_ref=src, dst_ref=dst, send_sem=ssem.at[k], recv_sem=rsem.at[k],
            device_id=where, device_id_type=MESH,
        )

    mine = pl.ds(NL * lev, NL)
    two = pl.ds(0, 2)
    up, down = jnp.minimum(lat + 1, LAT - 1), jnp.maximum(lat - 1, 0)
    to_south = [
        send(0, tn1, na.at[mine, two], lat=down),
        send(1, tn2, nb.at[mine, two], lat=down),
        send(2, dn, dne, lat=down, lon=west),
        send(3, dn, dnw, lat=down, lon=east),
    ]
    to_north = [
        send(4, ts1, sa.at[mine, two], lat=up),
        send(5, ts2, sb.at[mine, two], lat=up),
        send(6, ds, dse, lat=up, lon=west),
        send(7, ds, dsw, lat=up, lon=east),
    ]
    to_side = [
        send(8, ep, em.at[mine], lon=west),
        send(9, wp, wm.at[mine], lon=east),
    ]

    def fold_copy(half, n, src, dst, **where):
        return pltpu.make_async_remote_copy(
            src_ref=src, dst_ref=dst, send_sem=fsem_s.at[half, n], recv_sem=fsem_r.at[half, n],
            device_id=where, device_id_type=MESH,
        )

    def block(half, owner):
        return (fa, fb)[half].at[pl.ds(2 * owner, 2)]

    def fold_out(half, n):
        passed = (ga, gb)[half]
        if n == 0:
            return fold_copy(half, n, block(half, lon), passed, lon=beside(lon), lev=other)
        if n < 4:
            return fold_copy(half, n, block(half, lon), block(half, lon), lon=lax.rem(lon + 2 * n, LON))
        to = block(half, beside(lon))
        if n < 7:
            return fold_copy(half, n, passed, to, lon=lax.rem(lon + 2 * n - 6, LON), lev=other)
        return fold_copy(half, n, passed, to, lev=other)

    def fold_in(half, n):
        if n == 0:
            part = (ga, gb)[half]
        elif n < 4:
            part = block(half, lax.rem(lon + LON - 2 * n, LON))
        else:
            part = block(half, beside(lax.rem(lon + LON + 6 - 2 * n, LON)) if n < 7 else beside(lon))
        fold_copy(half, n, part, part, lev=other).wait_recv()

    to_fold = [[fold_out(half, n) for n in range(8)] for half in range(2)]

    def planes(ref, start, count):
        return ref.at[pl.ds(start, count)]

    def share(k, ref, start, count):
        part = planes(ref, start, count)
        return send(k, part, part, lev=other)

    @pl.when(at_fold)
    def _():
        for half in to_fold:
            half[0].start()
        for half in to_fold:
            for n in (2, 1, 3):
                half[n].start()

    @pl.when(north_in)
    def _():
        for k in (2, 3, 0, 1):
            to_north[k].start()

    @pl.when(early)
    def _():
        for c in to_side:
            c.start()

    to_core = [
        share(10, xe, own, NL),
        send(11, mp, mr, lev=other),
        share(12, ge, 2 + 3 * lev, 3),
        share(13, he, 3 + 2 * lev, 2),
        share(14, ae, 4 + lev, 1),
        share(15, so, NL * lev, NL),
    ]
    for c in to_core[:5]:
        c.start()

    @pl.when(jnp.logical_not(early))
    def _():
        lax.fori_loop(0, NL, strips_second, 0)

    to_core[5].start()

    def to_others():
        @pl.when((lev == 0) & north_in)
        def _():
            pl.semaphore_wait(told, 1)

        @pl.when((lev == 1) & north_in)
        def _():
            heard(jnp.logical_not(early), 11)
            heard(early & south_in, 7)
            heard(lat == 0, 1)
            tell()

        @pl.when(south_in)
        def _():
            for k in (2, 3, 0, 1):
                to_south[k].start()

    after = lax.rem(lat, LAT // 2) == 0
    pl.when(jnp.logical_not(after))(to_others)

    @pl.when(jnp.logical_not(early))
    def _():
        for c in to_side:
            c.start()

    def pair(ref, p, r):
        sl = pl.ds(8 * r, 8)
        return [ref[p, lt, sl, :] for lt in range(2)]

    def shifted(ref, p, r, d):
        if 0 <= 8 * r + d <= ROWS - 8:
            return [ref[p, lt, pl.ds(8 * r + d, 8), :] for lt in range(2)]
        return [sroll(t, -d % 8) for t in pair(ref, p, r)]

    def east_of(v):
        r0, r1 = lroll(v[0], 127), lroll(v[1], 127)
        return [where(lane == 127, r1, r0), r1]

    def west_of(v):
        r0, r1 = lroll(v[0], 1), lroll(v[1], 1)
        return [r0, where(lane == 0, r0, r1)]

    def relu(v):
        return jnp.maximum(v, 0.0)

    def weights(p, face):
        for r in range(RT):
            sl = pl.ds(8 * r, 8)
            here, n = pair(me, p, r), shifted(me, p, r, 1)
            e = east_of(here)
            w = [relu(here[k] + e[k]) for k in range(2)]
            v = west_of(w)
            hi, lo = pair(me, face, r), pair(me, face - 1, r)
            for k in range(2):
                we[p, k, sl, :] = w[k]
                ww[p, k, sl, :] = v[k]
                wy[p, k, sl, :] = relu(here[k] + n[k])
                wz[face, k, sl, :] = relu(0.5 * (hi[k] + lo[k]))

    def inner(u, p, count, finish):
        for r in range(RT):
            stack = [pair(u, p + j, r) for j in range(-1, count + 1)]
            fz = [
                [w * (hi - lo) for w, lo, hi in zip(pair(wz, p + j, r), stack[j], stack[j + 1])]
                for j in range(count + 1)
            ]
            for j in range(count):
                here, q = stack[j + 1], p + j
                n, s = shifted(u, q, r, 1), shifted(u, q, r, -1)
                wn, ws = pair(wy, q, r), shifted(wy, q, r, -1)
                e, w, v, wv = east_of(here), pair(we, q, r), west_of(here), pair(ww, q, r)
                for k in range(2):
                    total = (
                        (w[k] * (e[k] - here[k]) - wv[k] * (here[k] - v[k]))
                        + (wn[k] * (n[k] - here[k]) - ws[k] * (here[k] - s[k]))
                        + (fz[j + 1][k] - fz[j][k])
                    )
                    finish(q, pl.ds(8 * r, 8), k, total)

    def finish1(p, sl, k, total):
        ke[p, k, sl, :] = ge[p, k, sl, :] + 0.5 * total

    def finish2(p, sl, k, total):
        x1[p, k, sl, :] = he[p, k, sl, :] + total

    def finish3(p, sl, k, total):
        k2[p, k, sl, :] = (x1[p, k, sl, :] + ae[p, k, sl, :]) + 0.5 * total

    def finish4(p, sl, k, total):
        j = p - own
        out[j, sl, pl.ds(128 * k, 128)] = (x1[p, k, sl, :] + qe[j, k, sl, :]) + total

    far, near = 1 + 5 * lev, 4 - 2 * lev
    next_own, next_faces = 2 + 3 * other, 5 - 3 * lev

    def own_weights(j, _):
        weights(own + j, far + j)
        return 0

    def other_weights(j, _):
        weights(theirs + j, next_faces + j)
        return 0

    lax.fori_loop(0, NL, own_weights, 0)
    inner(xe, far, 3, finish1)

    def copy_own(i, _):
        p = own + i
        for ref, to in ((xe, bx), (me, bm)):
            for lt in range(2):
                to[p, pl.ds(24 + 24 * lt, 8), :] = ref[p, lt, top, :]
                to[p, pl.ds(40 + 24 * lt, 8), :] = ref[p, lt, bottom, :]
        return 0

    lax.fori_loop(0, NL, copy_own, 0)

    @pl.when(at_fold)
    def _():
        for half in range(2):
            fold_in(half, 0)
            for n in (5, 4, 6, 7):
                to_fold[half][n].start()

    share(10, xe, theirs, NL).wait_recv()
    to_core[1].wait_recv()

    def close(i, _):
        p = theirs + i
        for r in range(RT):
            sl = pl.ds(8 * r, 8)
            for lt in range(2):
                me[p, lt, sl, :] = closed(mr[i, lt, sl, :])
        for ref, to in ((xe, bx), (me, bm)):
            for lt in range(2):
                to[p, pl.ds(24 + 24 * lt, 8), :] = ref[p, lt, top, :]
                to[p, pl.ds(40 + 24 * lt, 8), :] = ref[p, lt, bottom, :]
        return 0

    lax.fori_loop(0, NL, close, 0)
    lax.fori_loop(0, NL, other_weights, 0)
    share(12, ge, next_own, 3).wait_recv()
    inner(xe, near, 4, finish1)
    share(13, he, 3 + 2 * other, 2).wait_recv()

    def inner2(j, _):
        inner(ke, 1 + 2 * lev + 3 * j, 3, finish2)
        return 0

    lax.fori_loop(0, 2, inner2, 0)
    share(14, ae, 4 + other, 1).wait_recv()
    inner(x1, 1 + 3 * lev, 5, finish3)
    inner(k2, own, 4, finish4)
    share(15, so, NL * other, NL).wait_recv()

    pl.when(after)(to_others)

    for c in to_side + to_core:
        c.wait_send()

    @pl.when(south_in)
    def _():
        for c in to_south:
            c.wait_send()

    @pl.when(north_in)
    def _():
        for c in to_north:
            c.wait_send()

    @pl.when(at_fold)
    def _():
        for half in to_fold:
            for c in half:
                c.wait_send()

    def next_levels(k, ref, l, count):
        piece = ref.at[pl.ds(NL * l + (1 - l) * (NL - count), count)]
        return send(k, piece, piece, lev=other)

    halos = ((16, em, 3), (17, wm, 3), (18, na, 3), (19, sa, 3), (20, nb, 2), (21, sb, 2))
    relays = [next_levels(k, ref, lev, count) for k, ref, count in halos]
    to_side[0].wait_recv()
    relays[0].start()
    to_side[1].wait_recv()
    relays[1].start()

    def corners(w_ref, e_ref, at, one, half2):
        d = where((lane & 4) == 0, w_ref[...], e_ref[...])
        for i in range(NL):
            one[NL * lev + i, 2] = lroll(d, at - 16 * i)
            half2[NL * lev + i, 2] = lroll(d, at - 16 * i - 8)

    c0 = (pc[0] - COLS * lon) & (LON * COLS - 1)
    t0, shift = c0 >> 7, c0 & 127

    def unfold(src, dst):
        for i in range(NL):
            t = [src[(t0 + k) & (2 * LON - 1), i] for k in (-3, -2, -1, 0, 1)]
            v = [
                pltpu.roll(where(lane >= 127 - shift, t[k + 1], t[k]), (shift + 1) & 127, 1)
                for k in range(4)
            ]
            dst[NL * lev + i, 0] = v[2]
            dst[NL * lev + i, 1] = v[1]
            dst[NL * lev + i, 2] = lroll(where(lo_half, v[0], v[3]), 116)

    def fold_arrived(half):
        for n in range(1, 8):
            fold_in(half, n)

    @pl.when(north_in)
    def _():
        for k in (0, 2, 3, 1):
            to_south[k].wait_recv()
        corners(dnw, dne, 112, na, nb)
        relays[2].start()
        relays[4].start()

    @pl.when(south_in)
    def _():
        for k in (0, 2, 3, 1):
            to_north[k].wait_recv()
        corners(dsw, dse, 4, sa, sb)

    relays[3].start()
    relays[5].start()

    @pl.when(at_fold)
    def _():
        fold_arrived(0)
        unfold(fa, na)
        relays[2].start()

    def ends(n, s):
        r = where(lo_half, lroll(both(s), 8), lroll(both(n), 116))
        c = where(lo_half, s[2], n[2])
        return where(halo_e, c, r), where(halo_w, c, r)

    def strip(l, f, v_e, v_w, from_e, from_w):
        return (
            where(ring_e, v_e, where(halo_e, from_e, so[l, f, 0])),
            where(ring_w, v_w, where(halo_w, from_w, so[l, f, 1])),
        )

    def slot(k, shift=0):
        return pl.ds((24, 32, 40, 48, 56, 64, 8, 80)[k] + shift, 8)

    def put(ref, p, tiles, which, turned=True):
        for k, t in zip(which, tiles):
            ref[p, slot(k), :] = t
            if turned and k >= 6:
                ref[p, slot(k, -8), :] = lroll(t, 12)
                ref[p, slot(k, 8), :] = lroll(t, 116)

    fresh = (1, 4, 6, 7)

    def place_first(l):
        p = l + 1
        n, s = [na[l, k] for k in range(3)], [sa[l, k] for k in range(3)]
        e1, w1 = em[l, 0], wm[l, 0]
        v = ends(n, s)
        x = [where(lo_sub, n[lt], s[lt]) for lt in range(2)]
        m = [sroll(where(lo_sub, s[lt], n[lt]), 4) for lt in range(2)]
        x += strip(l, X, v[0], v[1], e1, w1)
        m += strip(l, M, sroll(v[0], 4), sroll(v[1], 4), lroll(e1, 4), lroll(w1, 124))
        put(bx, p, x, fresh)
        put(bm, p, [closed(t) for t in m], fresh)

    def place_second(l):
        p = l + 1
        n, s = [nb[l, k] for k in range(3)], [sb[l, k] for k in range(3)]
        e1, w1, e2, w2 = em[l, 0], wm[l, 0], em[l, 1], wm[l, 1]
        v = ends(n, s)
        g = [where(lo_sub, n[lt], s[lt]) for lt in range(2)]
        h = [sroll(where(lo_sub, s[lt], n[lt]), 4) for lt in range(2)]
        a = [where(lo_sub, sroll(t, 5), sroll(t, 3)) for t in h]
        g += strip(l, G, v[0], v[1], lroll(e1, 8), lroll(w1, 4))
        hs = [sroll(t, 4) for t in v]
        h += strip(l, H, hs[0], hs[1], e2, w2)
        a_s = [where(lo_half, sroll(t, 3), sroll(t, 5)) for t in hs]
        a += strip(l, A, a_s[0], a_s[1], lroll(e2, 4), lroll(w2, 124))
        for k in range(4):
            bg[p, k], bh[p, k], ba[p, k] = g[k], h[k], a[k]

    def tiles(ref, p):
        return [ref[p, slot(k), :] for k in range(8)]

    def off(ref, p, d):
        return [ref[p, slot(k, d), :] for k in range(8)]

    def rim_of(full, part, p):
        return [
            full[p, 0, top, :], part[p, 0], full[p, 0, bottom, :],
            full[p, 1, top, :], part[p, 1], full[p, 1, bottom, :],
            part[p, 2], part[p, 3],
        ]

    def rim_east(v):
        r = [lroll(t, 127) for t in v]
        return [where(lane == 127, r[k + 3], r[k]) for k in range(3)] + r[3:]

    def rim_west(v):
        r = [lroll(t, 1) for t in v]
        return r[:3] + [where(lane == 0, r[k], r[k + 3]) for k in range(3)] + r[6:]

    every = range(8)

    def rim_weights(p):
        m, n = tiles(bm, p), off(bm, p, 1)
        put(vn, p, [relu(m[k] + n[k]) for k in every], every)
        b0, b1, t_e, t_w = (m[k] for k in fresh)
        w = east_of([b0, b1]) + [lroll(t_e, 127), lroll(t_w, 127)]
        w = [relu(m[k] + t) for k, t in zip(fresh, w)]
        v = west_of(w[:2]) + [lroll(t, 1) for t in w[2:]]
        for q in range(4):
            ve[p, q], vw[p, q] = w[q], v[q]

    def rim_faces(p):
        for q, k in enumerate(fresh):
            vz[p, q] = relu(0.5 * (bm[p, slot(k), :] + bm[p - 1, slot(k), :]))

    def mixed(full, part, p, k):
        if k in fresh:
            return part[p, fresh.index(k)]
        return full[p, k // 3, top if k % 3 == 0 else bottom, :]

    def rim(u, base, count, finish):
        for group in ((0, 3), (1, 4), (2, 5), (6,), (7,)):
            pairs = len(group) == 2
            stack = [[u[base + j, slot(k), :] for k in group] for j in range(-1, count + 1)]
            faces = [
                [mixed(wz, vz, base + j, k) * (hi - lo) for k, lo, hi in zip(group, stack[j], stack[j + 1])]
                for j in range(count + 1)
            ]
            for j in range(count):
                p, here = base + j, stack[j + 1]
                e = east_of(here) if pairs else [lroll(here[0], 127)]
                w = west_of(here) if pairs else [lroll(here[0], 1)]
                for q, k in enumerate(group):
                    c = here[q]
                    total = (
                        (mixed(we, ve, p, k) * (e[q] - c) - mixed(ww, vw, p, k) * (c - w[q]))
                        + (vn[p, slot(k), :] * (u[p, slot(k, 1), :] - c) - vn[p, slot(k, -1), :] * (c - u[p, slot(k, -1), :]))
                        + (faces[j + 1][q] - faces[j][q])
                    )
                    finish(p, k, total)

    def rim1(p, k, total):
        put(kr, p, [0.5 * total], (k,), False)

    def rim2(p, k, total):
        put(x1r, p, [mixed(he, bh, p, k) + total], (k,))

    def rim3(p, k, total):
        put(k2r, p, [(x1r[p, slot(k), :] + mixed(ae, ba, p, k)) + 0.5 * total], (k,))

    def rim4(p, k, total):
        if k not in (1, 4):
            put(x2r, p, [x1r[p, slot(k), :] + total], (k,), False)

    def add_noise(p):
        put(kr, p, [mixed(ge, bg, p, k) + kr[p, slot(k), :] for k in every], every)

    for i in range(NL):
        place_first(NL * lev + i)
    @pl.when(at_fold)
    def _():
        fold_arrived(1)
        unfold(fb, nb)
        relays[4].start()

    for i in range(NL):
        rim_weights(own + i)
    for i in range(NL):
        rim_faces(far + i)
    rim(bx, far, 3, rim1)

    for i in range(NL):
        place_second(NL * lev + i)
    for i in range(3):
        add_noise(far + i)
    rim(kr, 1 + 6 * lev, 2, rim2)
    rim(x1r, 1 + 7 * lev, 1, rim3)

    for k, ref, count in halos[:4]:
        next_levels(k, ref, other, count).wait_recv()
    for i in range(NL):
        place_first(NL * other + i)
    for i in range(3):
        rim_weights(next_own + i)
    for i in range(NL):
        rim_faces(next_faces + i)
    rim(bx, near, 4, rim1)
    for k, ref, count in halos[4:]:
        next_levels(k, ref, other, count).wait_recv()
    for i in range(NL - 1):
        place_second(1 + 3 * other + i)
    for i in range(NL):
        add_noise(near + i)
    rim(kr, 3, 4, rim2)
    rim(x1r, 2 + 2 * lev, 4, rim3)
    rim(k2r, own, 4, rim4)

    for i in range(NL):
        t = {k: x2r[own + i, slot(k), :] for k in (0, 2, 3, 5, 6, 7)}
        edge = where(halo_w, t[6], t[7])
        for lt in range(2):
            cs = pl.ds(128 * lt, 128)
            pltpu.store(out.at[i, bottom, cs], t[3 * lt + 2] + qe[i, lt, bottom, :], mask=lo_sub)
            pltpu.store(out.at[i, top, cs], t[3 * lt] + qe[i, lt, top, :], mask=sub >= 4)
        for r in range(RT):
            sl = pl.ds(8 * r, 8)
            cols = lroll(edge, 128 - (12 * (r + 1) + 8))
            pltpu.store(out.at[i, sl, pl.ds(0, 128)], cols + qe[i, 0, sl, :], mask=lane < 4)
            pltpu.store(out.at[i, sl, pl.ds(128, 128)], cols + qe[i, 1, sl, :], mask=lane >= 124)

    for c in relays:
        c.wait_send()


def local(*args):
    def vm(*shape, dtype=f32):
        return pltpu.VMEM(shape, dtype)

    cells = (NL, ROWS, COLS)
    tile = (8, 128)
    planes = (10, 2, ROWS, 128)
    rim = (2 * NL, 3) + tile
    sides = (2 * NL, 2) + tile
    rows = (NL, 2) + tile
    return pl.pallas_call(
        kernel,
        out_shape=pltpu.VMEM(cells, f32),
        in_specs=[pl.BlockSpec(memory_space=pltpu.HBM)] * 7,
        out_specs=pl.BlockSpec(memory_space=pltpu.VMEM),
        scratch_shapes=[
            vm(*cells), vm(*cells), vm(*cells), vm(*cells, dtype=jnp.int32), vm(2, *cells), vm(2, *cells),
            pltpu.SMEM((LON * COLS,), jnp.int32),
        ]
        + [vm(*planes)] * 12
        + [vm(NL, 2, ROWS, 128)] * 3
        + [vm(2 * NL, 5, 2, *tile)]
        + [vm(10, 96, 128)] * 7
        + [vm(10, 4, *tile)] * 6
        + [vm(*rim)] * 4
        + [vm(*sides)] * 2
        + [vm(*tile)] * 4
        + [vm(2 * LON, NL, *tile)] * 2
        + [vm(2, NL, *tile)] * 2
        + [vm(*rows)] * 4
        + [vm(*rows)] * 2
        + [vm(*tile)] * 2
        + [
            pltpu.SemaphoreType.DMA((7,)),
            pltpu.SemaphoreType.DMA((22,)),
            pltpu.SemaphoreType.DMA((22,)),
            pltpu.SemaphoreType.DMA((2, 8)),
            pltpu.SemaphoreType.DMA((2, 8)),
            pltpu.SemaphoreType.REGULAR,
        ],
        compiler_params=pltpu.CompilerParams(
            collective_id=0, has_side_effects=True, vmem_limit_bytes=VMEM
        ),
        name="ocean",
    )(*(pltpu.with_memory_space_constraint(v, pltpu.HBM) for v in args))


def solution(mesh):
    block = P("lev", "lat", "lon")
    steps = P(None, "lev", "lat", "lon")
    return jax.shard_map(
        local,
        mesh=mesh,
        in_specs=(block, block, block, steps, steps, block, P()),
        out_specs=block,
        check_vma=False,
    )
```

```python
import jax
import jax.numpy as jnp
from jax import lax
from jax.experimental import pallas as pl
from jax.experimental.pallas import tpu as pltpu
from jax.sharding import PartitionSpec as P


LAT, LON, LEV = 16, 8, 2
NL, ROWS, COLS = 4, 64, 256
RT = ROWS // 8
VMEM = 60 * 1024 * 1024
MESH = pl.DeviceIdType.MESH
f32 = jnp.float32
X, M, G, H, A = range(5)


def kernel(
    tracer, diff, amp, noise_w, noise_z, land, partner, out,
    rx, rd, ra, rl, rw, rz, pc,
    xe, me, ge, he, ae, ke, x1, k2, we, ww, wy, wz, mp, mr, qe, so,
    bx, bm, vn, kr, x1r, k2r, x2r, bg, bh, ba, ve, vw, vz,
    na, sa, nb, sb, em, wm, dne, dnw, dse, dsw, fa, fb, ga, gb,
    tn1, ts1, tn2, ts2, ep, wp, dn, ds,
    isem, ssem, rsem, fsem_s, fsem_r, told,
):
    lat, lon, lev = lax.axis_index("lat"), lax.axis_index("lon"), lax.axis_index("lev")
    east, west = lax.rem(lon + 1, LON), lax.rem(lon + LON - 1, LON)
    other = 1 - lev
    north_in, south_in = lat < LAT - 1, lat > 0
    at_fold = lat == LAT - 1
    own, theirs = NL * lev + 1, NL * other + 1

    def beside(i):
        return i + 1 - 2 * lax.rem(i, 2)

    bar = pltpu.get_barrier_semaphore()

    def greet(**where):
        pl.semaphore_signal(bar, inc=1, device_id=where, device_id_type=MESH)

    late_row = lax.rem(lat, LAT // 2) // (LAT // 4)
    fold_row, below_fold = (lat + 1) // LAT, (lat + 2) // LAT

    @pl.when(north_in)
    def _():
        for k in (lon, east, west):
            greet(lat=lat + 1, lon=k, lev=1 - below_fold * other)

    greet(lev=other)
    for k in (east, west):
        greet(lon=k, lev=late_row - fold_row * other)

    @pl.when(at_fold)
    def _():
        greet(lon=beside(lon), lev=other)
        for k in (2, 4, 6):
            greet(lon=lax.rem(lon + k, LON))
            greet(lon=lax.rem(lon + k, LON), lev=other)

    @pl.when(south_in)
    def _():
        for k in (lon, east, west):
            greet(lat=lat - 1, lon=k, lev=0)

    loads = [
        pltpu.make_async_copy(s, d, isem.at[k])
        for k, (s, d) in enumerate(
            ((tracer, rx), (diff, rd), (land, rl), (amp, ra), (noise_z, rz), (noise_w, rw), (partner, pc))
        )
    ]
    for c in loads:
        c.start()

    lane = lax.broadcasted_iota(jnp.int32, (8, 128), 1)
    sub = lax.broadcasted_iota(jnp.int32, (8, 128), 0)
    lo_half, lo_sub = lane < 64, sub < 4
    group_e = (lane * 171) >> 11
    group_w = (((lane + 8) * 171) >> 11) - 1
    k12 = lane - 12 * group_e
    halo_e, halo_w = k12 >= 8, (k12 >= 4) & (k12 < 8)
    ring_e = (group_e == 0) | (group_e == RT + 1)
    ring_w = (group_w == 0) | (group_w == RT + 1)
    zero = jnp.zeros((8, 128), f32)
    where = jnp.where

    def lroll(v, s):
        s = s % 128
        return v if s == 0 else pltpu.roll(v, s, 1)

    def sroll(v, s):
        return pltpu.roll(v, s, 0)

    def closed(v):
        return where(v > 0, v, -1.0)

    def both(v):
        return where(lo_half, v[0], v[1])

    top, bottom = pl.ds(ROWS - 8, 8), pl.ds(0, 8)

    def rows_at(r):
        return pl.ds(pl.multiple_of(8 * r, 8), 8)

    for p in (0, 9):
        for r in range(RT + 4):
            sl = pl.ds(8 * r, 8)
            bm[p, sl, :] = zero - 1.0
            for ref in (bx, kr, x1r, k2r):
                ref[p, sl, :] = zero
        for r in range(RT):
            sl = pl.ds(8 * r, 8)
            for lt in range(2):
                me[p, lt, sl, :] = zero - 1.0
                for ref in (xe, ke, x1, k2):
                    ref[p, lt, sl, :] = zero

    @pl.when(lat == 0)
    def _():
        for i in range(NL):
            for lt in range(3):
                sa[NL * lev + i, lt] = zero
                sb[NL * lev + i, lt] = zero

    last, last2 = 7 - 7 * lev, 6 - 5 * lev
    for lt in range(3):
        na[last, lt] = zero
        sa[last, lt] = zero
        nb[last2, lt] = zero
        sb[last2, lt] = zero
    for k in range(2):
        em[last, k] = zero
        wm[last, k] = zero

    for c in loads[:3]:
        c.wait()

    def prep_first(i, _):
        p = own + i
        for r in range(RT):
            sl = pl.ds(8 * r, 8)
            for lt in range(2):
                cs = pl.ds(128 * lt, 128)
                m = 0.5 * rd[i, sl, cs] * rl[i, sl, cs].astype(f32)
                xe[p, lt, sl, :] = rx[i, sl, cs]
                mp[i, lt, sl, :] = m
                me[p, lt, sl, :] = closed(m)
        return 0

    lax.fori_loop(0, NL, prep_first, 0)

    def first_rows(x, m):
        return where(lo_sub, x, sroll(m, 4))

    def first_rows2(g, h, a):
        return where(lo_sub, g, where(sub == 7, sroll(a, 7), sroll(h, 4)))

    def last_rows(x, m):
        return where(lo_sub, sroll(m, 4), x)

    def last_rows2(g, h, a):
        return where(lo_sub, where(sub == 0, sroll(a, 1), sroll(h, 4)), g)

    def mirror_rows(v):
        for b in (1, 2, 4):
            v = where((sub & b) != 0, sroll(v, b), sroll(v, 8 - b))
        return v

    def mirror_lanes(v):
        return jnp.take_along_axis(v, 127 - lane, axis=1, mode="promise_in_bounds")

    for i in range(NL):
        for lt in range(2):
            tn1[i, lt] = first_rows(xe[own + i, lt, bottom, :], mp[i, lt, bottom, :])
            ts1[i, lt] = last_rows(xe[own + i, lt, top, :], mp[i, lt, top, :])

    @pl.when(at_fold)
    def _():
        for i in range(NL):
            for lt in range(2):
                x, m = mirror_rows(xe[own + i, lt, top, :]), mirror_rows(mp[i, lt, top, :])
                fa[2 * lon + lt, i] = mirror_lanes(first_rows(x, m))

    def pack_strip(i, f, ref, q):
        s_e, s_w = zero, zero
        for r in range(RT):
            sl = pl.ds(8 * r, 8)
            v = lroll(where(lo_half, ref[q, 0, sl, :], ref[q, 1, sl, :]), 12 * (r + 1) + 8)
            s_e = where(group_e == r + 1, v, s_e)
            s_w = where(group_w == r + 1, v, s_w)
        so[own + i - 1, f, 0] = s_e
        so[own + i - 1, f, 1] = s_w

    def strips_first(i, _):
        pack_strip(i, X, xe, own + i)
        pack_strip(i, M, mp, i)
        return 0

    lax.fori_loop(0, NL, strips_first, 0)

    for c in loads[3:]:
        c.wait()

    def prep_second(i, _):
        p = own + i
        for r in range(RT):
            sl = pl.ds(8 * r, 8)
            for lt in range(2):
                cs = pl.ds(128 * lt, 128)
                x = rx[i, sl, cs]
                amp_ = ra[i, sl, cs]
                ge[p, lt, sl, :] = x + amp_ * rz[0, i, sl, cs]
                he[p, lt, sl, :] = x + amp_ * rw[0, i, sl, cs]
                ae[p, lt, sl, :] = amp_ * rz[1, i, sl, cs]
                qe[i, lt, sl, :] = amp_ * rw[1, i, sl, cs]
        return 0

    lax.fori_loop(0, NL, prep_second, 0)
    for i in range(NL):
        p = own + i
        for lt in range(2):
            tn2[i, lt] = first_rows2(ge[p, lt, bottom, :], he[p, lt, bottom, :], ae[p, lt, bottom, :])
            ts2[i, lt] = last_rows2(ge[p, lt, top, :], he[p, lt, top, :], ae[p, lt, top, :])

    @pl.when(at_fold)
    def _():
        for i in range(NL):
            p = own + i
            for lt in range(2):
                g, h, a = (mirror_rows(ref[p, lt, top, :]) for ref in (ge, he, ae))
                fb[2 * lon + lt, i] = mirror_lanes(first_rows2(g, h, a))

    for halves, dst in (((tn1, tn2), dn), ((ts1, ts2), ds)):
        d = zero
        for i in range(NL):
            for n, half in enumerate(halves):
                k = 2 * i + n
                d = where((lane >> 3) == k, lroll(both(half[i]), 8 * k + 4), d)
        dst[...] = d

    def strips_second(i, _):
        for f, ref in ((G, ge), (H, he), (A, ae)):
            pack_strip(i, f, ref, own + i)
        x, m, g, h, a = (so[own + i - 1, f, 0] for f in range(5))
        ep[i, 0] = where(halo_e, x, where(halo_w, lroll(m, 124), lroll(g, 120)))
        ep[i, 1] = where(halo_e, h, lroll(a, 124))
        wp[i, 0] = where(halo_w, x, where(halo_e, lroll(m, 4), lroll(g, 124)))
        wp[i, 1] = where(halo_w, h, lroll(a, 4))
        return 0

    early = late_row == 0

    @pl.when(early)
    def _():
        lax.fori_loop(0, NL, strips_second, 0)

    def heard(when, count):
        @pl.when(when)
        def _():
            pl.semaphore_wait(bar, count)

    def tell():
        pl.semaphore_signal(told, inc=1, device_id={"lev": other}, device_id_type=MESH)

    heard(at_fold, 13)

    @pl.when((lev == 0) & north_in)
    def _():
        heard(early, 11)
        heard(jnp.logical_not(early), 7)
        tell()

    @pl.when((lev == 1) & north_in)
    def _():
        pl.semaphore_wait(told, 1)

    def send(k, src, dst, **where):
        return pltpu.make_async_remote_copy(
            src_ref=src, dst_ref=dst, send_sem=ssem.at[k], recv_sem=rsem.at[k],
            device_id=where, device_id_type=MESH,
        )

    mine = pl.ds(NL * lev, NL)
    two = pl.ds(0, 2)
    up, down = jnp.minimum(lat + 1, LAT - 1), jnp.maximum(lat - 1, 0)
    to_south = [
        send(0, tn1, na.at[mine, two], lat=down),
        send(1, tn2, nb.at[mine, two], lat=down),
        send(2, dn, dne, lat=down, lon=west),
        send(3, dn, dnw, lat=down, lon=east),
    ]
    to_north = [
        send(4, ts1, sa.at[mine, two], lat=up),
        send(5, ts2, sb.at[mine, two], lat=up),
        send(6, ds, dse, lat=up, lon=west),
        send(7, ds, dsw, lat=up, lon=east),
    ]
    to_side = [
        send(8, ep, em.at[mine], lon=west),
        send(9, wp, wm.at[mine], lon=east),
    ]

    def fold_copy(half, n, src, dst, **where):
        return pltpu.make_async_remote_copy(
            src_ref=src, dst_ref=dst, send_sem=fsem_s.at[half, n], recv_sem=fsem_r.at[half, n],
            device_id=where, device_id_type=MESH,
        )

    def block(half, owner):
        return (fa, fb)[half].at[pl.ds(2 * owner, 2)]

    def fold_out(half, n):
        passed = (ga, gb)[half]
        if n == 0:
            return fold_copy(half, n, block(half, lon), passed, lon=beside(lon), lev=other)
        if n < 4:
            return fold_copy(half, n, block(half, lon), block(half, lon), lon=lax.rem(lon + 2 * n, LON))
        to = block(half, beside(lon))
        if n < 7:
            return fold_copy(half, n, passed, to, lon=lax.rem(lon + 2 * n - 6, LON), lev=other)
        return fold_copy(half, n, passed, to, lev=other)

    def fold_in(half, n):
        if n == 0:
            part = (ga, gb)[half]
        elif n < 4:
            part = block(half, lax.rem(lon + LON - 2 * n, LON))
        else:
            part = block(half, beside(lax.rem(lon + LON + 6 - 2 * n, LON)) if n < 7 else beside(lon))
        fold_copy(half, n, part, part, lev=other).wait_recv()

    to_fold = [[fold_out(half, n) for n in range(8)] for half in range(2)]

    def planes(ref, start, count):
        return ref.at[pl.ds(start, count)]

    def share(k, ref, start, count):
        part = planes(ref, start, count)
        return send(k, part, part, lev=other)

    @pl.when(at_fold)
    def _():
        for half in to_fold:
            half[0].start()
        for half in to_fold:
            for n in (2, 1, 3):
                half[n].start()

    @pl.when(north_in)
    def _():
        for k in (2, 3, 0, 1):
            to_north[k].start()

    @pl.when(early)
    def _():
        for c in to_side:
            c.start()

    to_core = [
        share(10, xe, own, NL),
        send(11, mp, mr, lev=other),
        share(12, ge, 2 + 3 * lev, 3),
        share(13, he, 3 + 2 * lev, 2),
        share(14, ae, 4 + lev, 1),
        share(15, so, NL * lev, NL),
    ]
    for c in to_core[:5]:
        c.start()

    @pl.when(jnp.logical_not(early))
    def _():
        lax.fori_loop(0, NL, strips_second, 0)

    to_core[5].start()

    def to_others():
        @pl.when((lev == 0) & north_in)
        def _():
            pl.semaphore_wait(told, 1)

        @pl.when((lev == 1) & north_in)
        def _():
            heard(jnp.logical_not(early), 11)
            heard(early & south_in, 7)
            heard(lat == 0, 1)
            tell()

        @pl.when(south_in)
        def _():
            for k in (2, 3, 0, 1):
                to_south[k].start()

    after = lax.rem(lat, LAT // 2) == 0
    pl.when(jnp.logical_not(after))(to_others)

    @pl.when(jnp.logical_not(early))
    def _():
        for c in to_side:
            c.start()

    def pair(ref, p, r):
        sl = pl.ds(8 * r, 8)
        return [ref[p, lt, sl, :] for lt in range(2)]

    def shifted(ref, p, r, d):
        if 0 <= 8 * r + d <= ROWS - 8:
            return [ref[p, lt, pl.ds(8 * r + d, 8), :] for lt in range(2)]
        return [sroll(t, -d % 8) for t in pair(ref, p, r)]

    def east_of(v):
        r0, r1 = lroll(v[0], 127), lroll(v[1], 127)
        return [where(lane == 127, r1, r0), r1]

    def west_of(v):
        r0, r1 = lroll(v[0], 1), lroll(v[1], 1)
        return [r0, where(lane == 0, r0, r1)]

    def relu(v):
        return jnp.maximum(v, 0.0)

    def weights(p, face):
        for r in range(RT):
            sl = pl.ds(8 * r, 8)
            here, n = pair(me, p, r), shifted(me, p, r, 1)
            e = east_of(here)
            w = [relu(here[k] + e[k]) for k in range(2)]
            v = west_of(w)
            hi, lo = pair(me, face, r), pair(me, face - 1, r)
            for k in range(2):
                we[p, k, sl, :] = w[k]
                ww[p, k, sl, :] = v[k]
                wy[p, k, sl, :] = relu(here[k] + n[k])
                wz[face, k, sl, :] = relu(0.5 * (hi[k] + lo[k]))

    def inner(u, p, count, finish):
        for r in range(RT):
            stack = [pair(u, p + j, r) for j in range(-1, count + 1)]
            fz = [
                [w * (hi - lo) for w, lo, hi in zip(pair(wz, p + j, r), stack[j], stack[j + 1])]
                for j in range(count + 1)
            ]
            for j in range(count):
                here, q = stack[j + 1], p + j
                n, s = shifted(u, q, r, 1), shifted(u, q, r, -1)
                wn, ws = pair(wy, q, r), shifted(wy, q, r, -1)
                e, w, v, wv = east_of(here), pair(we, q, r), west_of(here), pair(ww, q, r)
                for k in range(2):
                    total = (
                        (w[k] * (e[k] - here[k]) - wv[k] * (here[k] - v[k]))
                        + (wn[k] * (n[k] - here[k]) - ws[k] * (here[k] - s[k]))
                        + (fz[j + 1][k] - fz[j][k])
                    )
                    finish(q, pl.ds(8 * r, 8), k, total)

    def finish1(p, sl, k, total):
        ke[p, k, sl, :] = ge[p, k, sl, :] + 0.5 * total

    def finish2(p, sl, k, total):
        x1[p, k, sl, :] = he[p, k, sl, :] + total

    def finish3(p, sl, k, total):
        k2[p, k, sl, :] = (x1[p, k, sl, :] + ae[p, k, sl, :]) + 0.5 * total

    def finish4(p, sl, k, total):
        j = p - own
        out[j, sl, pl.ds(128 * k, 128)] = (x1[p, k, sl, :] + qe[j, k, sl, :]) + total

    far, near = 1 + 5 * lev, 4 - 2 * lev
    next_own, next_faces = 2 + 3 * other, 5 - 3 * lev

    def own_weights(j, _):
        weights(own + j, far + j)
        return 0

    def other_weights(j, _):
        weights(theirs + j, next_faces + j)
        return 0

    lax.fori_loop(0, NL, own_weights, 0)
    inner(xe, far, 3, finish1)

    def copy_own(i, _):
        p = own + i
        for ref, to in ((xe, bx), (me, bm)):
            for lt in range(2):
                to[p, pl.ds(24 + 24 * lt, 8), :] = ref[p, lt, top, :]
                to[p, pl.ds(40 + 24 * lt, 8), :] = ref[p, lt, bottom, :]
        return 0

    lax.fori_loop(0, NL, copy_own, 0)

    @pl.when(at_fold)
    def _():
        for half in range(2):
            fold_in(half, 0)
            for n in (5, 6, 4, 7):
                to_fold[half][n].start()

    share(10, xe, theirs, NL).wait_recv()
    to_core[1].wait_recv()

    def close(i, _):
        p = theirs + i
        for r in range(RT):
            sl = pl.ds(8 * r, 8)
            for lt in range(2):
                me[p, lt, sl, :] = closed(mr[i, lt, sl, :])
        for ref, to in ((xe, bx), (me, bm)):
            for lt in range(2):
                to[p, pl.ds(24 + 24 * lt, 8), :] = ref[p, lt, top, :]
                to[p, pl.ds(40 + 24 * lt, 8), :] = ref[p, lt, bottom, :]
        return 0

    lax.fori_loop(0, NL, close, 0)
    lax.fori_loop(0, NL, other_weights, 0)
    share(12, ge, next_own, 3).wait_recv()
    inner(xe, near, 4, finish1)
    share(13, he, 3 + 2 * other, 2).wait_recv()

    def inner2(j, _):
        inner(ke, 1 + 2 * lev + 3 * j, 3, finish2)
        return 0

    lax.fori_loop(0, 2, inner2, 0)
    share(14, ae, 4 + other, 1).wait_recv()
    inner(x1, 1 + 3 * lev, 5, finish3)
    inner(k2, own, 4, finish4)
    share(15, so, NL * other, NL).wait_recv()

    pl.when(after)(to_others)

    for c in to_side + to_core:
        c.wait_send()

    @pl.when(south_in)
    def _():
        for c in to_south:
            c.wait_send()

    @pl.when(north_in)
    def _():
        for c in to_north:
            c.wait_send()

    @pl.when(at_fold)
    def _():
        for half in to_fold:
            for c in half:
                c.wait_send()

    def next_levels(k, ref, l, count):
        piece = ref.at[pl.ds(NL * l + (1 - l) * (NL - count), count)]
        return send(k, piece, piece, lev=other)

    halos = ((16, em, 3), (17, wm, 3), (18, na, 3), (19, sa, 3), (20, nb, 2), (21, sb, 2))
    relays = [next_levels(k, ref, lev, count) for k, ref, count in halos]
    to_side[0].wait_recv()
    relays[0].start()
    to_side[1].wait_recv()
    relays[1].start()

    def corners(w_ref, e_ref, at, one, half2):
        d = where((lane & 4) == 0, w_ref[...], e_ref[...])
        for i in range(NL):
            one[NL * lev + i, 2] = lroll(d, at - 16 * i)
            half2[NL * lev + i, 2] = lroll(d, at - 16 * i - 8)

    c0 = (pc[0] - COLS * lon) & (LON * COLS - 1)
    t0, shift = c0 >> 7, c0 & 127

    def unfold(src, dst):
        for i in range(NL):
            t = [src[(t0 + k) & (2 * LON - 1), i] for k in (-3, -2, -1, 0, 1)]
            v = [
                pltpu.roll(where(lane >= 127 - shift, t[k + 1], t[k]), (shift + 1) & 127, 1)
                for k in range(4)
            ]
            dst[NL * lev + i, 0] = v[2]
            dst[NL * lev + i, 1] = v[1]
            dst[NL * lev + i, 2] = lroll(where(lo_half, v[0], v[3]), 116)

    def fold_arrived(half):
        for n in range(1, 8):
            fold_in(half, n)

    @pl.when(north_in)
    def _():
        for k in (0, 2, 3, 1):
            to_south[k].wait_recv()
        corners(dnw, dne, 112, na, nb)
        relays[2].start()
        relays[4].start()

    @pl.when(south_in)
    def _():
        for k in (0, 2, 3, 1):
            to_north[k].wait_recv()
        corners(dsw, dse, 4, sa, sb)

    relays[3].start()
    relays[5].start()

    @pl.when(at_fold)
    def _():
        fold_arrived(0)
        unfold(fa, na)
        relays[2].start()

    def ends(n, s):
        r = where(lo_half, lroll(both(s), 8), lroll(both(n), 116))
        c = where(lo_half, s[2], n[2])
        return where(halo_e, c, r), where(halo_w, c, r)

    def strip(l, f, v_e, v_w, from_e, from_w):
        return (
            where(ring_e, v_e, where(halo_e, from_e, so[l, f, 0])),
            where(ring_w, v_w, where(halo_w, from_w, so[l, f, 1])),
        )

    def slot(k, shift=0):
        return pl.ds((24, 32, 40, 48, 56, 64, 8, 80)[k] + shift, 8)

    def put(ref, p, tiles, which, turned=True):
        for k, t in zip(which, tiles):
            ref[p, slot(k), :] = t
            if turned and k >= 6:
                ref[p, slot(k, -8), :] = lroll(t, 12)
                ref[p, slot(k, 8), :] = lroll(t, 116)

    fresh = (1, 4, 6, 7)

    def place_first(l):
        p = l + 1
        n, s = [na[l, k] for k in range(3)], [sa[l, k] for k in range(3)]
        e1, w1 = em[l, 0], wm[l, 0]
        v = ends(n, s)
        x = [where(lo_sub, n[lt], s[lt]) for lt in range(2)]
        m = [sroll(where(lo_sub, s[lt], n[lt]), 4) for lt in range(2)]
        x += strip(l, X, v[0], v[1], e1, w1)
        m += strip(l, M, sroll(v[0], 4), sroll(v[1], 4), lroll(e1, 4), lroll(w1, 124))
        put(bx, p, x, fresh)
        put(bm, p, [closed(t) for t in m], fresh)

    def place_second(l):
        p = l + 1
        n, s = [nb[l, k] for k in range(3)], [sb[l, k] for k in range(3)]
        e1, w1, e2, w2 = em[l, 0], wm[l, 0], em[l, 1], wm[l, 1]
        v = ends(n, s)
        g = [where(lo_sub, n[lt], s[lt]) for lt in range(2)]
        h = [sroll(where(lo_sub, s[lt], n[lt]), 4) for lt in range(2)]
        a = [where(lo_sub, sroll(t, 5), sroll(t, 3)) for t in h]
        g += strip(l, G, v[0], v[1], lroll(e1, 8), lroll(w1, 4))
        hs = [sroll(t, 4) for t in v]
        h += strip(l, H, hs[0], hs[1], e2, w2)
        a_s = [where(lo_half, sroll(t, 3), sroll(t, 5)) for t in hs]
        a += strip(l, A, a_s[0], a_s[1], lroll(e2, 4), lroll(w2, 124))
        for k in range(4):
            bg[p, k], bh[p, k], ba[p, k] = g[k], h[k], a[k]

    def tiles(ref, p):
        return [ref[p, slot(k), :] for k in range(8)]

    def off(ref, p, d):
        return [ref[p, slot(k, d), :] for k in range(8)]

    def rim_of(full, part, p):
        return [
            full[p, 0, top, :], part[p, 0], full[p, 0, bottom, :],
            full[p, 1, top, :], part[p, 1], full[p, 1, bottom, :],
            part[p, 2], part[p, 3],
        ]

    def rim_east(v):
        r = [lroll(t, 127) for t in v]
        return [where(lane == 127, r[k + 3], r[k]) for k in range(3)] + r[3:]

    def rim_west(v):
        r = [lroll(t, 1) for t in v]
        return r[:3] + [where(lane == 0, r[k], r[k + 3]) for k in range(3)] + r[6:]

    every = range(8)

    def rim_weights(p):
        m, n = tiles(bm, p), off(bm, p, 1)
        put(vn, p, [relu(m[k] + n[k]) for k in every], every)
        b0, b1, t_e, t_w = (m[k] for k in fresh)
        w = east_of([b0, b1]) + [lroll(t_e, 127), lroll(t_w, 127)]
        w = [relu(m[k] + t) for k, t in zip(fresh, w)]
        v = west_of(w[:2]) + [lroll(t, 1) for t in w[2:]]
        for q in range(4):
            ve[p, q], vw[p, q] = w[q], v[q]

    def rim_faces(p):
        for q, k in enumerate(fresh):
            vz[p, q] = relu(0.5 * (bm[p, slot(k), :] + bm[p - 1, slot(k), :]))

    def mixed(full, part, p, k):
        if k in fresh:
            return part[p, fresh.index(k)]
        return full[p, k // 3, top if k % 3 == 0 else bottom, :]

    def rim(u, base, count, finish):
        for group in ((0, 3), (1, 4), (2, 5), (6,), (7,)):
            pairs = len(group) == 2
            stack = [[u[base + j, slot(k), :] for k in group] for j in range(-1, count + 1)]
            faces = [
                [mixed(wz, vz, base + j, k) * (hi - lo) for k, lo, hi in zip(group, stack[j], stack[j + 1])]
                for j in range(count + 1)
            ]
            for j in range(count):
                p, here = base + j, stack[j + 1]
                e = east_of(here) if pairs else [lroll(here[0], 127)]
                w = west_of(here) if pairs else [lroll(here[0], 1)]
                for q, k in enumerate(group):
                    c = here[q]
                    total = (
                        (mixed(we, ve, p, k) * (e[q] - c) - mixed(ww, vw, p, k) * (c - w[q]))
                        + (vn[p, slot(k), :] * (u[p, slot(k, 1), :] - c) - vn[p, slot(k, -1), :] * (c - u[p, slot(k, -1), :]))
                        + (faces[j + 1][q] - faces[j][q])
                    )
                    finish(p, k, total)

    def rim1(p, k, total):
        put(kr, p, [0.5 * total], (k,), False)

    def rim2(p, k, total):
        put(x1r, p, [mixed(he, bh, p, k) + total], (k,))

    def rim3(p, k, total):
        put(k2r, p, [(x1r[p, slot(k), :] + mixed(ae, ba, p, k)) + 0.5 * total], (k,))

    def rim4(p, k, total):
        if k not in (1, 4):
            put(x2r, p, [x1r[p, slot(k), :] + total], (k,), False)

    def add_noise(p):
        put(kr, p, [mixed(ge, bg, p, k) + kr[p, slot(k), :] for k in every], every)

    for i in range(NL):
        place_first(NL * lev + i)
    @pl.when(at_fold)
    def _():
        fold_arrived(1)
        unfold(fb, nb)
        relays[4].start()

    for i in range(NL):
        rim_weights(own + i)
    for i in range(NL):
        rim_faces(far + i)
    rim(bx, far, 3, rim1)

    for i in range(NL):
        place_second(NL * lev + i)
    for i in range(3):
        add_noise(far + i)
    rim(kr, 1 + 6 * lev, 2, rim2)
    rim(x1r, 1 + 7 * lev, 1, rim3)

    for k, ref, count in halos[:4]:
        next_levels(k, ref, other, count).wait_recv()
    for i in range(NL):
        place_first(NL * other + i)
    for i in range(3):
        rim_weights(next_own + i)
    for i in range(NL):
        rim_faces(next_faces + i)
    rim(bx, near, 4, rim1)
    for k, ref, count in halos[4:]:
        next_levels(k, ref, other, count).wait_recv()
    for i in range(NL - 1):
        place_second(1 + 3 * other + i)
    for i in range(NL):
        add_noise(near + i)
    rim(kr, 3, 4, rim2)
    rim(x1r, 2 + 2 * lev, 4, rim3)
    rim(k2r, own, 4, rim4)

    for i in range(NL):
        t = {k: x2r[own + i, slot(k), :] for k in (0, 2, 3, 5, 6, 7)}
        edge = where(halo_w, t[6], t[7])
        for lt in range(2):
            cs = pl.ds(128 * lt, 128)
            pltpu.store(out.at[i, bottom, cs], t[3 * lt + 2] + qe[i, lt, bottom, :], mask=lo_sub)
            pltpu.store(out.at[i, top, cs], t[3 * lt] + qe[i, lt, top, :], mask=sub >= 4)
        for r in range(RT):
            sl = pl.ds(8 * r, 8)
            cols = lroll(edge, 128 - (12 * (r + 1) + 8))
            pltpu.store(out.at[i, sl, pl.ds(0, 128)], cols + qe[i, 0, sl, :], mask=lane < 4)
            pltpu.store(out.at[i, sl, pl.ds(128, 128)], cols + qe[i, 1, sl, :], mask=lane >= 124)

    for c in relays:
        c.wait_send()


def local(*args):
    def vm(*shape, dtype=f32):
        return pltpu.VMEM(shape, dtype)

    cells = (NL, ROWS, COLS)
    tile = (8, 128)
    planes = (10, 2, ROWS, 128)
    rim = (2 * NL, 3) + tile
    sides = (2 * NL, 2) + tile
    rows = (NL, 2) + tile
    return pl.pallas_call(
        kernel,
        out_shape=pltpu.VMEM(cells, f32),
        in_specs=[pl.BlockSpec(memory_space=pltpu.HBM)] * 7,
        out_specs=pl.BlockSpec(memory_space=pltpu.VMEM),
        scratch_shapes=[
            vm(*cells), vm(*cells), vm(*cells), vm(*cells, dtype=jnp.int32), vm(2, *cells), vm(2, *cells),
            pltpu.SMEM((LON * COLS,), jnp.int32),
        ]
        + [vm(*planes)] * 12
        + [vm(NL, 2, ROWS, 128)] * 3
        + [vm(2 * NL, 5, 2, *tile)]
        + [vm(10, 96, 128)] * 7
        + [vm(10, 4, *tile)] * 6
        + [vm(*rim)] * 4
        + [vm(*sides)] * 2
        + [vm(*tile)] * 4
        + [vm(2 * LON, NL, *tile)] * 2
        + [vm(2, NL, *tile)] * 2
        + [vm(*rows)] * 4
        + [vm(*rows)] * 2
        + [vm(*tile)] * 2
        + [
            pltpu.SemaphoreType.DMA((7,)),
            pltpu.SemaphoreType.DMA((22,)),
            pltpu.SemaphoreType.DMA((22,)),
            pltpu.SemaphoreType.DMA((2, 8)),
            pltpu.SemaphoreType.DMA((2, 8)),
            pltpu.SemaphoreType.REGULAR,
        ],
        compiler_params=pltpu.CompilerParams(
            collective_id=0, has_side_effects=True, vmem_limit_bytes=VMEM
        ),
        name="ocean",
    )(*(pltpu.with_memory_space_constraint(v, pltpu.HBM) for v in args))


def solution(mesh):
    block = P("lev", "lat", "lon")
    steps = P(None, "lev", "lat", "lon")
    return jax.shard_map(
        local,
        mesh=mesh,
        in_specs=(block, block, block, steps, steps, block, P()),
        out_specs=block,
        check_vma=False,
    )
```
